32 devices in a mesh: ctx: 8 (over y, x, core), tp: 4 (over z).
Axes of the slice: x: 2, y: 2, z: 4, core: 2. Of those that a mesh axis runs over, the one named last changes fastest.
Arguments:
- query_in: bfloat16 [1024, 4096], P('ctx', 'tp'), may hold values from -6 to 6
- key_in: bfloat16 [1024, 4096], P('ctx', 'tp'), may hold values from -6 to 6
- value_in: bfloat16 [1024, 4096], P('ctx', 'tp'), may hold values from -6 to 6
- long_filter: bfloat16 [1024, 4096], P('ctx', 'tp'), may hold values from -1.1 to 1.1
- short_taps: bfloat16 [3, 3, 4096], P(None, None, 'tp'), may hold values from -3.5 to 3.5
- out_grad: bfloat16 [1024, 4096], P('ctx', 'tp'), may hold values from -6 to 6
Outputs:
- output: bfloat16 [1024, 4096], P('ctx', 'tp')
- query_grad: bfloat16 [1024, 4096], P('ctx', 'tp')
- key_grad: bfloat16 [1024, 4096], P('ctx', 'tp')
- value_grad: bfloat16 [1024, 4096], P('ctx', 'tp')
- filter_grad: float32 [1024, 4096], P('ctx', 'tp')
- taps_grad: float32 [3, 3, 4096], P(None, None, 'tp')
The draws below stay inside these ranges and needn't reach their ends.
All inputs are finite; a program needn't handle non-finite values.
Results may differ from the reference program's by a relative error of at most 0.001.
Values may be sent and summed in bfloat16 or wider, within the bound.
No kernel may reach another device: no remote copies, remote signals or barrier semaphores. Data moves between devices by JAX's collectives and lax.ppermute only.
A program may use at most 64 MiB of HBM per device.

```python
import math
import jax
import jax.numpy as jnp
from jax import lax

FEATURE_COUNT = 4096
KT = 3
STEP_TOTAL = 1024


def draw_long_filter(key, part):
    key_span = jax.random.fold_in(key, 11)
    key_noise = jax.random.fold_in(key, 12)
    key_marks = jax.random.fold_in(key, 13)
    key_drops = jax.random.fold_in(key, 14)
    fading_span = jnp.exp(jax.random.uniform(key_span, (1, FEATURE_COUNT), jnp.float32, math.log(30.0), math.log(4.0 * STEP_TOTAL)))
    jagged_perturbation = jnp.clip(jax.random.normal(key_noise, (STEP_TOTAL, FEATURE_COUNT), jnp.float32), -4.0, 4.0)
    element_indices = jnp.arange(STEP_TOTAL, dtype=jnp.int32)[:, None]
    place_labels = jax.random.randint(key_marks, (4,), 0, STEP_TOTAL)
    fading_falloff = jax.random.uniform(key_drops, (4, FEATURE_COUNT), jnp.float32, 0.5, 0.8)
    random_spike = jnp.ones((STEP_TOTAL, FEATURE_COUNT), jnp.float32)
    for partner_rank in range(4):
        random_spike = random_spike * jnp.where(element_indices >= place_labels[partner_rank], fading_falloff[partner_rank][None, :], 1.0)
    kernel_magnitude = jnp.sqrt(jnp.expm1(-2.0 / fading_span) / jnp.expm1(-2.0 * STEP_TOTAL / fading_span))
    lag_amount_shift = element_indices.astype(jnp.float32)
    return (jagged_perturbation * jnp.exp(-lag_amount_shift / fading_span) * random_spike * kernel_magnitude).astype(jnp.bfloat16)


def block_levels(key, dims, cuts, smallest, top_value):
    def one(axis_at, parts):
        heights = jax.random.uniform(jax.random.fold_in(jax.random.fold_in(key, 6), axis_at), (parts,), jnp.float32, smallest / len(cuts), top_value / len(cuts))
        return jnp.repeat(jnp.exp(heights), dims[axis_at] // parts).reshape((-1,) + (1,) * (len(dims) - axis_at - 1))

    loudness = one(*cuts[0])
    for cut in cuts[1:]:
        loudness = loudness * one(*cut)
    return loudness


def bell_draw(key, shape, width, bound, pieces=(), held_as=jnp.bfloat16):
    values = jax.random.normal(key, shape, jnp.float32) * width
    if len(pieces) > 0:
        values = block_levels(key, shape, pieces, -0.22, 0.18) * values
    return jnp.clip(values, min=-bound, max=bound).astype(held_as)


def setup_inputs(seed: int = 0) -> dict:
    key_of = jax.random.split(jax.random.key(seed), 7)
    query_in = bell_draw(key_of[0], (STEP_TOTAL, FEATURE_COUNT), 1.0, 6.0, ((0, 8), (1, 4)))
    key_in = bell_draw(key_of[1], (STEP_TOTAL, FEATURE_COUNT), 1.0, 6.0, ((0, 8), (1, 4)))
    value_in = bell_draw(key_of[2], (STEP_TOTAL, FEATURE_COUNT), 1.0, 6.0, ((0, 8), (1, 4)))
    long_filter = draw_long_filter(jax.random.fold_in(key_of[6], 71), 0)
    short_taps = bell_draw(key_of[4], (3, KT, FEATURE_COUNT), KT ** -0.5, 3.5, ((2, 4),))
    out_grad = bell_draw(key_of[5], (STEP_TOTAL, FEATURE_COUNT), 1.0, 6.0, ((0, 8), (1, 4)))
    return dict(query_in=query_in, key_in=key_in, value_in=value_in, long_filter=long_filter, short_taps=short_taps, out_grad=out_grad)


def short_filter(padded, tap_gain, row_count):
    margin = tap_gain.shape[0] - 1
    running = tap_gain[0] * padded[margin:margin + row_count]
    for offset in range(1, margin + 1):
        running = running + tap_gain[offset] * padded[margin - offset:margin - offset + row_count]
    return running

def one_block(operands):
    query_in, key_in, value_in, long_filter, short_taps, out_grad = operands
    row_count = query_in.shape[0]
    margin = short_taps.shape[1] - 1
    tap_gain = short_taps.astype(jnp.float32)
    padded = [jnp.pad(source.astype(jnp.float32), ((margin, 0), (0, 0))) for source in (query_in, key_in, value_in)]
    filtered = [short_filter(padded[partner_rank], tap_gain[partner_rank], row_count) for partner_rank in range(3)]
    mixed_in = filtered[1] * filtered[2]
    length = 2 * row_count
    mixed_spec = jnp.fft.rfft(mixed_in, n=length, axis=0)
    filter_spec = jnp.fft.rfft(long_filter.astype(jnp.float32), n=length, axis=0)
    convolved = jnp.fft.irfft(mixed_spec * filter_spec, n=length, axis=0)[:row_count]
    output = (filtered[0] * convolved).astype(jnp.bfloat16)
    grad_in = out_grad.astype(jnp.float32)
    gate_grad = grad_in * convolved
    conv_grad = grad_in * filtered[0]
    grad_spec = jnp.fft.rfft(conv_grad, n=length, axis=0)
    mixed_grad = jnp.fft.irfft(grad_spec * jnp.conj(filter_spec), n=length, axis=0)[:row_count]
    grad_scale = 1.0 / math.sqrt(row_count)
    filter_grad = jnp.fft.irfft(grad_spec * jnp.conj(mixed_spec), n=length, axis=0)[:row_count] * grad_scale
    inner_grads = [gate_grad, mixed_grad * filtered[2], mixed_grad * filtered[1]]
    input_grads = []
    tap_grads = []
    for partner_rank in range(3):
        padded_grad = jnp.pad(inner_grads[partner_rank], ((0, margin), (0, 0)))
        running = tap_gain[partner_rank, 0] * inner_grads[partner_rank]
        for offset in range(1, margin + 1):
            running = running + tap_gain[partner_rank, offset] * padded_grad[offset:offset + row_count]
        input_grads.append(running.astype(jnp.bfloat16))
        tap_grads.append(jnp.stack([lax.optimization_barrier(jnp.sum(inner_grads[partner_rank] * padded[partner_rank][margin - offset:margin - offset + row_count], axis=0)) for offset in range(margin + 1)]))
    return (output, input_grads[0], input_grads[1], input_grads[2], filter_grad, jnp.stack(tap_grads) * grad_scale)

def reference(query_in, key_in, value_in, long_filter, short_taps, out_grad):
    row_count, channels = query_in.shape
    block_width = math.gcd(channels, 256)
    block_count = channels // block_width

    def to_blocks(array):
        return array.reshape(row_count, block_count, block_width).transpose(1, 0, 2)

    def from_blocks(array):
        return array.transpose(1, 0, 2).reshape(row_count, channels)
    tap_blocks = short_taps.reshape(3, KT, block_count, block_width).transpose(2, 0, 1, 3)
    results = lax.map(one_block, (to_blocks(query_in), to_blocks(key_in), to_blocks(value_in), to_blocks(long_filter), tap_blocks, to_blocks(out_grad)))
    taps_grad = results[5].transpose(1, 2, 0, 3).reshape(3, KT, channels)
    return (from_blocks(results[0]), from_blocks(results[1]), from_blocks(results[2]), from_blocks(results[3]), from_blocks(results[4]), taps_grad)
```

```python
from functools import lru_cache, partial
import math

import jax
import jax.numpy as jnp
import ml_dtypes
import numpy as np
from jax import lax
from jax.experimental import pallas as pl
from jax.experimental.pallas import tpu as pltpu
from jax.sharding import PartitionSpec as P

HIGHEST_PREC = lax.Precision.HIGHEST
TWO_PI = 2.0 * math.pi


def passed_along(block, axis, distance):
    devices = range(lax.axis_size(axis))
    route = [(i - distance, i) for i in devices if i - distance in devices]
    return lax.ppermute(block, axis, route)


def phase_pair(count_a, count_b, period, direction):
    product = (
        jnp.arange(count_a, dtype=jnp.int32)[:, None]
        * jnp.arange(count_b, dtype=jnp.int32)[None, :]
    )
    phase_angle = direction * TWO_PI / period * (product % period).astype(jnp.float32)
    return (jnp.cos(phase_angle), jnp.sin(phase_angle))


def rotate_pair(real_part, imag_part, cosine, sine_part):
    return (real_part * cosine - imag_part * sine_part, real_part * sine_part + imag_part * cosine)


def times_pair(first_pair, second_pair, conj_second):
    factor = -1.0 if conj_second else 1.0
    real_part = first_pair[0] * second_pair[0] - factor * first_pair[1] * second_pair[1]
    imag_part = first_pair[1] * second_pair[0] + factor * first_pair[0] * second_pair[1]
    return (real_part, imag_part)


def unpack_fields(spectrum, comp_axis, field_axis):
    collected = []
    for partner_rank in range(spectrum.shape[field_axis]):
        single = lax.index_in_dim(spectrum, partner_rank, field_axis, keepdims=True)
        collected.append(
            (
                lax.index_in_dim(single, 0, comp_axis, keepdims=True),
                lax.index_in_dim(single, 1, comp_axis, keepdims=True),
            )
        )
    return collected


def pack_fields(pairs, comp_axis, field_axis):
    return jnp.concatenate(
        [jnp.concatenate([real_part, imag_part], axis=comp_axis) for real_part, imag_part in pairs],
        axis=field_axis,
    )


def spread_forward(regroup, fields):
    row_count, field_count, channels = fields.shape
    part_count = lax.axis_size("ctx")
    block_rows = row_count // part_count
    length = 2 * part_count * row_count
    my_index = lax.axis_index("ctx")
    gathered = regroup(fields.reshape(part_count, 1, block_rows, field_count, channels))
    cosine, sine_part = phase_pair(2 * part_count, part_count, 2 * part_count, -1.0)
    first_table = jnp.stack([cosine, sine_part], axis=1)
    first_pass = jnp.einsum("kda,arfc->kdrfc", first_table, gathered, precision=HIGHEST_PREC)
    row_index = my_index * block_rows + jnp.arange(block_rows, dtype=jnp.int32)
    twist_index = jnp.arange(2 * part_count, dtype=jnp.int32)[:, None] * row_index[None, :] % length
    phase_angle = -TWO_PI / length * twist_index.astype(jnp.float32)
    cos_twist = jnp.cos(phase_angle)[:, :, None, None]
    sin_twist = jnp.sin(phase_angle)[:, :, None, None]
    real_part, imag_part = rotate_pair(first_pass[:, 0], first_pass[:, 1], cos_twist, sin_twist)
    turned = jnp.stack([real_part, imag_part], axis=1)
    arrived = regroup(turned.reshape(part_count, 1, 2, 2, block_rows, field_count, channels))
    cosine, sine_part = phase_pair(row_count, row_count, row_count, -1.0)
    second_table = jnp.stack(
        [jnp.stack([cosine, sine_part], axis=-1), jnp.stack([-sine_part, cosine], axis=-1)], axis=0
    )
    second_table = second_table.reshape(2, part_count, block_rows, row_count, 2)
    return jnp.einsum("pqsrfc,sprkd->qkdfc", arrived, second_table, precision=HIGHEST_PREC)


def spread_inverse(regroup, spectrum):
    pair_count, row_count, _, field_count, channels = spectrum.shape
    part_count = lax.axis_size("ctx")
    block_rows = row_count // part_count
    length = 2 * part_count * row_count
    my_index = lax.axis_index("ctx")
    cosine, sine_part = phase_pair(row_count, row_count, row_count, 1.0)
    second_table = jnp.stack(
        [jnp.stack([cosine, sine_part], axis=-1), jnp.stack([-sine_part, cosine], axis=-1)], axis=0
    )
    second_table = second_table.reshape(2, row_count, part_count, block_rows, 2)
    row_parts = jnp.einsum("qkdfc,dkprs->pqsrfc", spectrum, second_table, precision=HIGHEST_PREC)
    freq_index = my_index * pair_count + jnp.arange(pair_count, dtype=jnp.int32)
    twist_index = freq_index[:, None] * jnp.arange(row_count, dtype=jnp.int32)[None, :] % length
    phase_angle = TWO_PI / length * twist_index.astype(jnp.float32)
    cos_twist = (
        jnp.cos(phase_angle)
        .reshape(pair_count, part_count, block_rows)
        .transpose(1, 0, 2)[:, :, :, None, None]
    )
    sin_twist = (
        jnp.sin(phase_angle)
        .reshape(pair_count, part_count, block_rows)
        .transpose(1, 0, 2)[:, :, :, None, None]
    )
    real_part, imag_part = rotate_pair(row_parts[:, :, 0], row_parts[:, :, 1], cos_twist, sin_twist)
    turned = jnp.stack([real_part, imag_part], axis=2)
    arrived = regroup(
        turned.reshape(part_count, 1, pair_count, 2, block_rows, field_count, channels)
    )
    cosine, sine_part = phase_pair(2 * part_count, part_count, 2 * part_count, 1.0)
    first_table = (jnp.stack([cosine, -sine_part], axis=1) / length).reshape(
        part_count, pair_count, 2, part_count
    )
    values = jnp.einsum("pqsrfc,pqsa->arfc", arrived, first_table, precision=HIGHEST_PREC)
    returned = regroup(values.reshape(part_count, 1, block_rows, field_count, channels))
    return returned.reshape(row_count, field_count, channels)


def local_general(query_in, key_in, value_in, long_filter, short_taps, out_grad):
    row_count = query_in.shape[0]
    tap_count = short_taps.shape[1]
    margin = tap_count - 1
    part_count = lax.axis_size("ctx")

    def regroup(blocks):
        return lax.all_to_all(blocks, "ctx", split_axis=0, concat_axis=1, tiled=True)[0]

    to_freq = partial(spread_forward, regroup)
    from_freq = partial(spread_inverse, regroup)
    comp_axis = 2
    field_axis = 3
    inputs = jnp.stack([query_in, key_in, value_in])
    earlier = passed_along(inputs[:, row_count - margin :], "ctx", 1)
    extended = jnp.concatenate([earlier, inputs], axis=1).astype(jnp.float32)
    tap_gain = short_taps.astype(jnp.float32)
    filtered = tap_gain[:, 0, None, :] * extended[:, margin:]
    for offset in range(1, tap_count):
        filtered = (
            filtered
            + tap_gain[:, offset, None, :]
            * extended[:, margin - offset : margin - offset + row_count]
        )
    query_filt = filtered[0]
    key_filt = filtered[1]
    value_filt = filtered[2]
    mixed_in = key_filt * value_filt
    spectra = to_freq(jnp.stack([mixed_in, long_filter.astype(jnp.float32)], axis=1))
    mixed_spec, filter_spec = unpack_fields(spectra, comp_axis, field_axis)
    convolved = from_freq(
        pack_fields([times_pair(mixed_spec, filter_spec, False)], comp_axis, field_axis)
    )[:, 0]
    output = (query_filt * convolved).astype(jnp.bfloat16)
    grad_in = out_grad.astype(jnp.float32)
    gate_grad = grad_in * convolved
    conv_grad = grad_in * query_filt
    grad_spec = unpack_fields(to_freq(conv_grad[:, None, :]), comp_axis, field_axis)[0]
    returned = from_freq(
        pack_fields(
            [times_pair(grad_spec, filter_spec, True), times_pair(grad_spec, mixed_spec, True)],
            comp_axis,
            field_axis,
        )
    )
    grad_scale = 1.0 / math.sqrt(part_count * row_count)
    mixed_grad = returned[:, 0]
    filter_grad = returned[:, 1] * grad_scale
    grad_stack = jnp.stack([gate_grad, mixed_grad * value_filt, mixed_grad * key_filt])
    later_rows = passed_along(grad_stack[:, :margin], "ctx", -1)
    padded_grad = jnp.concatenate([grad_stack, later_rows], axis=1)
    input_grads = tap_gain[:, 0, None, :] * grad_stack
    for offset in range(1, tap_count):
        input_grads = (
            input_grads + tap_gain[:, offset, None, :] * padded_grad[:, offset : offset + row_count]
        )
    partial_taps = jnp.stack(
        [
            jnp.sum(grad_stack * extended[:, margin - offset : margin - offset + row_count], axis=1)
            for offset in range(tap_count)
        ],
        axis=1,
    )
    taps_grad = lax.psum(partial_taps, "ctx") * grad_scale
    return (
        output,
        input_grads[0].astype(jnp.bfloat16),
        input_grads[1].astype(jnp.bfloat16),
        input_grads[2].astype(jnp.bfloat16),
        filter_grad,
        taps_grad,
    )


RADIX = 8
FIELD_NAMES = ("query", "key", "value", "filter", "out_grad")
CLASSES = (0, 8, 4, 2, 6, 1, 5, 9, 13)
LANES = 128
PAD = 8
CHUNK = 16


def split_pair(values):
    high = values.astype(jnp.bfloat16)
    low = (values - high.astype(jnp.float32)).astype(jnp.bfloat16)
    return high, low


@lru_cache(maxsize=None)
def class_tables(rows):
    length = 2 * RADIX * rows
    back = np.arange(rows)
    forward, inverse = [], []
    for residue in CLASSES:
        product = np.outer(2 * RADIX * back + residue, back) % length
        angle = -2.0 * np.pi * product / length
        cosine, sine = np.cos(angle), np.sin(angle)
        forward.append(np.block([[cosine, -sine], [sine, cosine]]))
        weight = (1.0 if residue in (0, RADIX) else 2.0) / length
        inverse.append(weight * np.block([[cosine.T, sine.T], [-sine.T, cosine.T]]))
    tables = []
    for table in (np.stack(forward), np.stack(inverse)):
        high = table.astype(ml_dtypes.bfloat16)
        low = (table - high.astype(np.float64)).astype(ml_dtypes.bfloat16)
        tables += [high, low]
    return tables


ROOT = math.sqrt(0.5)
COS1 = math.cos(math.pi / 8)
SIN1 = math.sin(math.pi / 8)


def forward_classes(x):
    u = [x[a] + x[a + 4] for a in range(4)]
    d = [x[a] - x[a + 4] for a in range(4)]
    even, odd = u[0] + u[2], u[1] + u[3]
    dif, tot = ROOT * (d[1] - d[3]), ROOT * (d[1] + d[3])
    found = [
        (even + odd, None),
        (even - odd, None),
        (u[0] - u[2], u[3] - u[1]),
        (d[0] + dif, -d[2] - tot),
        (d[0] - dif, d[2] - tot),
    ]
    w0 = (x[0], -x[4])
    w1 = (COS1 * x[1] - SIN1 * x[5], -SIN1 * x[1] - COS1 * x[5])
    w2 = (ROOT * (x[2] - x[6]), -ROOT * (x[2] + x[6]))
    w3 = (SIN1 * x[3] - COS1 * x[7], -COS1 * x[3] - SIN1 * x[7])
    s02 = (w0[0] + w2[0], w0[1] + w2[1])
    d02 = (w0[0] - w2[0], w0[1] - w2[1])
    s13 = (w1[0] + w3[0], w1[1] + w3[1])
    d13 = (w1[0] - w3[0], w1[1] - w3[1])
    found.append((s02[0] + s13[0], s02[1] + s13[1]))
    found.append((d02[0] + d13[1], d02[1] - d13[0]))
    found.append((s02[0] - s13[0], s02[1] - s13[1]))
    found.append((d02[0] - d13[1], d02[1] + d13[0]))
    return found


def inverse_classes(z):
    (z0, _), (z8, _), (r4, i4), (r2, i2), (r6, i6) = z[:5]
    up, down = z0 + z8, z0 - z8
    even = [up + r4, down - i4, up - r4, down + i4]
    gap, tot = ROOT * (r2 - r6), ROOT * (i2 + i6)
    turn = [r2 + r6, gap - tot, i6 - i2, -gap - tot]
    (r1, i1), (r5, i5), (r9, i9), (rd, id_) = z[5:]
    s = (r1 + r9, i1 + i9)
    d = (r1 - r9, i1 - i9)
    t = (r5 + rd, i5 + id_)
    e = (r5 - rd, i5 - id_)
    s0 = (s[0] + t[0], s[1] + t[1])
    s2 = (s[0] - t[0], s[1] - t[1])
    s1 = (d[0] - e[1], d[1] + e[0])
    s3 = (d[0] + e[1], d[1] - e[0])
    q = [
        s0,
        (COS1 * s1[0] - SIN1 * s1[1], SIN1 * s1[0] + COS1 * s1[1]),
        (ROOT * (s2[0] - s2[1]), ROOT * (s2[0] + s2[1])),
        (SIN1 * s3[0] - COS1 * s3[1], COS1 * s3[0] + SIN1 * s3[1]),
    ]
    return [even[a] + turn[a] + q[a][0] for a in range(4)] + [
        even[a] - turn[a] - q[a][1] for a in range(4)
    ]


def layer_kernel(
    taps_ref, got_ref, fh_ref, fl_ref, ih_ref, il_ref, out_ref,
    qp, kp, vp, qs, ks, vs, xh, xl, zs, g0, g1, g2, sums,
):
    blocks, height, _ = got_ref.shape
    rows = height // len(FIELD_NAMES)
    total = blocks * rows
    chunks = rows // CHUNK
    f32 = jnp.float32
    zero = jnp.zeros((PAD, LANES), f32)
    for ref in (qp, kp, vp):
        ref[pl.ds(0, PAD), :] = zero
    for ref in (g0, g1, g2):
        ref[pl.ds(total, PAD), :] = zero
    gain = [[taps_ref[3 * i + j : 3 * i + j + 1, :] for j in range(3)] for i in range(3)]

    def widen(step, carry):
        b0 = pl.multiple_of(step * CHUNK, CHUNK)
        for a in range(blocks):
            for field, ref in enumerate((qp, kp, vp)):
                ref[pl.ds(PAD + a * rows + b0, CHUNK), :] = got_ref[
                    a, pl.ds(field * rows + b0, CHUNK), :
                ].astype(f32)
        return carry

    lax.fori_loop(0, chunks, widen, 0)
    for f in (0, 1):
        xh[f, pl.ds(rows, rows), :] = jnp.zeros((rows, 3 * LANES), jnp.bfloat16)
        xl[f, pl.ds(rows, rows), :] = jnp.zeros((rows, 3 * LANES), jnp.bfloat16)

    def short(ref, i, at):
        return (
            gain[i][0] * ref[pl.ds(at, CHUNK), :]
            + gain[i][1] * ref[pl.ds(at - 1, CHUNK), :]
            + gain[i][2] * ref[pl.ds(at - 2, CHUNK), :]
        )

    def enter(step, carry):
        b0 = pl.multiple_of(step * CHUNK, CHUNK)

        def put(column, values):
            for f, (real, imag) in enumerate(forward_classes(values)):
                for part, value in ((0, real), (1, imag)):
                    if value is not None:
                        high, low = split_pair(value)
                        place = (f, pl.ds(part * rows + b0, CHUNK), pl.ds(column * LANES, LANES))
                        xh[place] = high
                        xl[place] = low

        mixed = []
        for a in range(blocks):
            at = a * rows + b0
            key_filt = short(kp, 1, PAD + at)
            value_filt = short(vp, 2, PAD + at)
            ks[pl.ds(at, CHUNK), :] = key_filt
            vs[pl.ds(at, CHUNK), :] = value_filt
            mixed.append(key_filt * value_filt)
        put(0, mixed)
        put(1, [got_ref[a, pl.ds(3 * rows + b0, CHUNK), :].astype(f32) for a in range(blocks)])
        conv_grad = []
        for a in range(blocks):
            at = a * rows + b0
            query_filt = short(qp, 0, PAD + at)
            qs[pl.ds(at, CHUNK), :] = query_filt
            conv_grad.append(
                query_filt * got_ref[a, pl.ds(4 * rows + b0, CHUNK), :].astype(f32)
            )
        put(2, conv_grad)
        return carry

    lax.fori_loop(0, chunks, enter, 0)

    def three(high_table, low_table, high, low):
        return (
            jnp.dot(high_table, high, preferred_element_type=f32)
            + jnp.dot(high_table, low, preferred_element_type=f32)
            + jnp.dot(low_table, high, preferred_element_type=f32)
        )

    def turn(f, carry):
        spec = three(fh_ref[f], fl_ref[f], xh[f], xl[f])
        (mr, hr, gr), (mi, hi, gi) = [
            [spec[p * rows : (p + 1) * rows, c * LANES : (c + 1) * LANES] for c in range(3)]
            for p in range(2)
        ]
        real = jnp.concatenate([mr * hr - mi * hi, gr * hr + gi * hi, gr * mr + gi * mi], axis=1)
        imag = jnp.concatenate([mr * hi + mi * hr, gi * hr - gr * hi, gi * mr - gr * mi], axis=1)
        high, low = split_pair(jnp.concatenate([real, imag], axis=0))
        zs[f] = three(ih_ref[f], il_ref[f], high, low)
        return carry

    lax.fori_loop(0, len(CLASSES), turn, 0)
    grad_scale = 1.0 / math.sqrt(total)

    def leave(step, carry):
        b0 = pl.multiple_of(step * CHUNK, CHUNK)

        def take(column):
            lanes = pl.ds(column * LANES, LANES)
            return inverse_classes(
                [
                    (zs[f, pl.ds(b0, CHUNK), lanes], zs[f, pl.ds(rows + b0, CHUNK), lanes])
                    for f in range(len(CLASSES))
                ]
            )

        for a, conv in enumerate(take(0)):
            at = a * rows + b0
            out_ref[a, pl.ds(b0, CHUNK), :] = (qs[pl.ds(at, CHUNK), :] * conv).astype(jnp.bfloat16)
            g0[pl.ds(at, CHUNK), :] = conv * got_ref[a, pl.ds(4 * rows + b0, CHUNK), :].astype(f32)
        for a, mixed_grad in enumerate(take(1)):
            at = a * rows + b0
            g1[pl.ds(at, CHUNK), :] = mixed_grad * vs[pl.ds(at, CHUNK), :]
            g2[pl.ds(at, CHUNK), :] = mixed_grad * ks[pl.ds(at, CHUNK), :]
        for a, value in enumerate(take(2)):
            high, low = split_pair(value * grad_scale)
            out_ref[a, pl.ds(4 * rows + b0, CHUNK), :] = high
            out_ref[a, pl.ds(5 * rows + b0, CHUNK), :] = low
        return carry

    lax.fori_loop(0, chunks, leave, 0)
    sums[...] = jnp.zeros_like(sums)

    def close(step, carry):
        b0 = pl.multiple_of(step * CHUNK, CHUNK)
        for i, (grad, source) in enumerate(((g0, qp), (g1, kp), (g2, vp))):
            found = [jnp.zeros((CHUNK, LANES), f32)] * 3
            for a in range(blocks):
                at = a * rows + b0
                now = grad[pl.ds(at, CHUNK), :]
                value = (
                    gain[i][0] * now
                    + gain[i][1] * grad[pl.ds(at + 1, CHUNK), :]
                    + gain[i][2] * grad[pl.ds(at + 2, CHUNK), :]
                )
                out_ref[a, pl.ds((1 + i) * rows + b0, CHUNK), :] = value.astype(jnp.bfloat16)
                for j in range(3):
                    found[j] = found[j] + now * source[pl.ds(PAD + at - j, CHUNK), :]
            for j in range(3):
                sums[3 * i + j] += found[j][:8] + found[j][8:]
        return carry

    lax.fori_loop(0, chunks, close, 0)
    place = lax.broadcasted_iota(jnp.int32, (CHUNK, LANES), 0)
    taps = jnp.zeros((CHUNK, LANES), f32)
    for n in range(9):
        line = jnp.sum(sums[n], axis=0, keepdims=True) * grad_scale
        taps = jnp.where(place == n, line, taps)
    high, low = split_pair(taps)
    for a in range(blocks):
        out_ref[a, pl.ds(6 * rows, CHUNK), :] = high
        out_ref[a, pl.ds(6 * rows + CHUNK, CHUNK), :] = low


def whole_vmem(count):
    return [pl.BlockSpec(memory_space=pltpu.VMEM)] * count


def pack_kernel(*refs):
    *sources, out_ref = refs
    rows = sources[0].shape[0]
    for a in range(out_ref.shape[0]):
        for field, ref in enumerate(sources):
            out_ref[a, pl.ds(field * rows, rows), :] = ref[:, a * LANES : (a + 1) * LANES]


def unpack_kernel(got_ref, output, query_grad, key_grad, value_grad, filter_grad, taps_grad):
    rows = output.shape[0]
    for a in range(got_ref.shape[0]):
        lanes = slice(a * LANES, (a + 1) * LANES)
        for field, ref in enumerate((output, query_grad, key_grad, value_grad)):
            ref[:, lanes] = got_ref[a, pl.ds(field * rows, rows), :]
        high, low = [got_ref[a, pl.ds(n * rows, rows), :].astype(jnp.float32) for n in (4, 5)]
        filter_grad[:, lanes] = high + low
        high, low = [
            got_ref[a, pl.ds(6 * rows + n * CHUNK, CHUNK), :].astype(jnp.float32) for n in (0, 1)
        ]
        taps_grad[:, lanes] = high + low


def local_fast(query_in, key_in, value_in, long_filter, short_taps, out_grad):
    rows, channels = query_in.shape
    blocks = lax.axis_size("ctx")
    total = blocks * rows
    f32, bf16 = jnp.float32, jnp.bfloat16
    shape = jax.ShapeDtypeStruct
    packed = pl.pallas_call(
        pack_kernel,
        out_shape=shape((blocks, 5 * rows, LANES), bf16),
        in_specs=whole_vmem(5),
        out_specs=whole_vmem(1)[0],
        name="pack",
    )(query_in, key_in, value_in, long_filter, out_grad)
    got = lax.all_to_all(packed, "ctx", 0, 0)
    gain = lax.dynamic_slice_in_dim(
        short_taps.reshape(9, channels), lax.axis_index("ctx") * LANES, LANES, 1
    ).astype(f32)
    tables = class_tables(rows)
    count = len(CLASSES)
    height = 6 * rows + 2 * CHUNK
    done = pl.pallas_call(
        layer_kernel,
        out_shape=shape((blocks, height, LANES), bf16),
        in_specs=whole_vmem(6),
        out_specs=whole_vmem(1)[0],
        scratch_shapes=[pltpu.VMEM((total + PAD, LANES), f32)] * 3
        + [pltpu.VMEM((total, LANES), f32)] * 3
        + [pltpu.VMEM((count, 2 * rows, 3 * LANES), bf16)] * 2
        + [pltpu.VMEM((count, 2 * rows, 3 * LANES), f32)]
        + [pltpu.VMEM((total + PAD, LANES), f32)] * 3
        + [pltpu.VMEM((9, 8, LANES), f32)],
        compiler_params=pltpu.CompilerParams(vmem_limit_bytes=40 * 1024 * 1024),
        name="layer",
    )(gain, got, *tables)
    back = lax.all_to_all(done, "ctx", 0, 0)
    result = pl.pallas_call(
        unpack_kernel,
        out_shape=[shape((rows, channels), bf16)] * 4
        + [shape((rows, channels), f32), shape((CHUNK, channels), f32)],
        in_specs=whole_vmem(1),
        out_specs=whole_vmem(6),
        name="unpack",
    )(back)
    return (*result[:5], result[5][:9].reshape(3, 3, channels))


def local(query_in, key_in, value_in, long_filter, short_taps, out_grad):
    rows, channels = query_in.shape
    blocks = lax.axis_size("ctx")
    taps = short_taps.shape[:2]
    if blocks == RADIX and channels == blocks * LANES and rows == LANES and taps == (3, 3):
        return local_fast(query_in, key_in, value_in, long_filter, short_taps, out_grad)
    return local_general(query_in, key_in, value_in, long_filter, short_taps, out_grad)


def solution(mesh):
    placed = (
        P("ctx", "tp"),
        P("ctx", "tp"),
        P("ctx", "tp"),
        P("ctx", "tp"),
        P(None, None, "tp"),
        P("ctx", "tp"),
    )
    return jax.shard_map(
        local,
        mesh=mesh,
        in_specs=placed,
        out_specs=(
            P("ctx", "tp"),
            P("ctx", "tp"),
            P("ctx", "tp"),
            P("ctx", "tp"),
            P("ctx", "tp"),
            P(None, None, "tp"),
        ),
        check_vma=False,
    )
```

```python
from functools import lru_cache, partial
import math

import jax
import jax.numpy as jnp
import ml_dtypes
import numpy as np
from jax import lax
from jax.experimental import pallas as pl
from jax.experimental.pallas import tpu as pltpu
from jax.sharding import PartitionSpec as P

HIGHEST_PREC = lax.Precision.HIGHEST
TWO_PI = 2.0 * math.pi


def passed_along(block, axis, distance):
    devices = range(lax.axis_size(axis))
    route = [(i - distance, i) for i in devices if i - distance in devices]
    return lax.ppermute(block, axis, route)


def phase_pair(count_a, count_b, period, direction):
    product = (
        jnp.arange(count_a, dtype=jnp.int32)[:, None]
        * jnp.arange(count_b, dtype=jnp.int32)[None, :]
    )
    phase_angle = direction * TWO_PI / period * (product % period).astype(jnp.float32)
    return (jnp.cos(phase_angle), jnp.sin(phase_angle))


def rotate_pair(real_part, imag_part, cosine, sine_part):
    return (real_part * cosine - imag_part * sine_part, real_part * sine_part + imag_part * cosine)


def times_pair(first_pair, second_pair, conj_second):
    factor = -1.0 if conj_second else 1.0
    real_part = first_pair[0] * second_pair[0] - factor * first_pair[1] * second_pair[1]
    imag_part = first_pair[1] * second_pair[0] + factor * first_pair[0] * second_pair[1]
    return (real_part, imag_part)


def unpack_fields(spectrum, comp_axis, field_axis):
    collected = []
    for partner_rank in range(spectrum.shape[field_axis]):
        single = lax.index_in_dim(spectrum, partner_rank, field_axis, keepdims=True)
        collected.append(
            (
                lax.index_in_dim(single, 0, comp_axis, keepdims=True),
                lax.index_in_dim(single, 1, comp_axis, keepdims=True),
            )
        )
    return collected


def pack_fields(pairs, comp_axis, field_axis):
    return jnp.concatenate(
        [jnp.concatenate([real_part, imag_part], axis=comp_axis) for real_part, imag_part in pairs],
        axis=field_axis,
    )


def spread_forward(regroup, fields):
    row_count, field_count, channels = fields.shape
    part_count = lax.axis_size("ctx")
    block_rows = row_count // part_count
    length = 2 * part_count * row_count
    my_index = lax.axis_index("ctx")
    gathered = regroup(fields.reshape(part_count, 1, block_rows, field_count, channels))
    cosine, sine_part = phase_pair(2 * part_count, part_count, 2 * part_count, -1.0)
    first_table = jnp.stack([cosine, sine_part], axis=1)
    first_pass = jnp.einsum("kda,arfc->kdrfc", first_table, gathered, precision=HIGHEST_PREC)
    row_index = my_index * block_rows + jnp.arange(block_rows, dtype=jnp.int32)
    twist_index = jnp.arange(2 * part_count, dtype=jnp.int32)[:, None] * row_index[None, :] % length
    phase_angle = -TWO_PI / length * twist_index.astype(jnp.float32)
    cos_twist = jnp.cos(phase_angle)[:, :, None, None]
    sin_twist = jnp.sin(phase_angle)[:, :, None, None]
    real_part, imag_part = rotate_pair(first_pass[:, 0], first_pass[:, 1], cos_twist, sin_twist)
    turned = jnp.stack([real_part, imag_part], axis=1)
    arrived = regroup(turned.reshape(part_count, 1, 2, 2, block_rows, field_count, channels))
    cosine, sine_part = phase_pair(row_count, row_count, row_count, -1.0)
    second_table = jnp.stack(
        [jnp.stack([cosine, sine_part], axis=-1), jnp.stack([-sine_part, cosine], axis=-1)], axis=0
    )
    second_table = second_table.reshape(2, part_count, block_rows, row_count, 2)
    return jnp.einsum("pqsrfc,sprkd->qkdfc", arrived, second_table, precision=HIGHEST_PREC)


def spread_inverse(regroup, spectrum):
    pair_count, row_count, _, field_count, channels = spectrum.shape
    part_count = lax.axis_size("ctx")
    block_rows = row_count // part_count
    length = 2 * part_count * row_count
    my_index = lax.axis_index("ctx")
    cosine, sine_part = phase_pair(row_count, row_count, row_count, 1.0)
    second_table = jnp.stack(
        [jnp.stack([cosine, sine_part], axis=-1), jnp.stack([-sine_part, cosine], axis=-1)], axis=0
    )
    second_table = second_table.reshape(2, row_count, part_count, block_rows, 2)
    row_parts = jnp.einsum("qkdfc,dkprs->pqsrfc", spectrum, second_table, precision=HIGHEST_PREC)
    freq_index = my_index * pair_count + jnp.arange(pair_count, dtype=jnp.int32)
    twist_index = freq_index[:, None] * jnp.arange(row_count, dtype=jnp.int32)[None, :] % length
    phase_angle = TWO_PI / length * twist_index.astype(jnp.float32)
    cos_twist = (
        jnp.cos(phase_angle)
        .reshape(pair_count, part_count, block_rows)
        .transpose(1, 0, 2)[:, :, :, None, None]
    )
    sin_twist = (
        jnp.sin(phase_angle)
        .reshape(pair_count, part_count, block_rows)
        .transpose(1, 0, 2)[:, :, :, None, None]
    )
    real_part, imag_part = rotate_pair(row_parts[:, :, 0], row_parts[:, :, 1], cos_twist, sin_twist)
    turned = jnp.stack([real_part, imag_part], axis=2)
    arrived = regroup(
        turned.reshape(part_count, 1, pair_count, 2, block_rows, field_count, channels)
    )
    cosine, sine_part = phase_pair(2 * part_count, part_count, 2 * part_count, 1.0)
    first_table = (jnp.stack([cosine, -sine_part], axis=1) / length).reshape(
        part_count, pair_count, 2, part_count
    )
    values = jnp.einsum("pqsrfc,pqsa->arfc", arrived, first_table, precision=HIGHEST_PREC)
    returned = regroup(values.reshape(part_count, 1, block_rows, field_count, channels))
    return returned.reshape(row_count, field_count, channels)


def local_general(query_in, key_in, value_in, long_filter, short_taps, out_grad):
    row_count = query_in.shape[0]
    tap_count = short_taps.shape[1]
    margin = tap_count - 1
    part_count = lax.axis_size("ctx")

    def regroup(blocks):
        return lax.all_to_all(blocks, "ctx", split_axis=0, concat_axis=1, tiled=True)[0]

    to_freq = partial(spread_forward, regroup)
    from_freq = partial(spread_inverse, regroup)
    comp_axis = 2
    field_axis = 3
    inputs = jnp.stack([query_in, key_in, value_in])
    earlier = passed_along(inputs[:, row_count - margin :], "ctx", 1)
    extended = jnp.concatenate([earlier, inputs], axis=1).astype(jnp.float32)
    tap_gain = short_taps.astype(jnp.float32)
    filtered = tap_gain[:, 0, None, :] * extended[:, margin:]
    for offset in range(1, tap_count):
        filtered = (
            filtered
            + tap_gain[:, offset, None, :]
            * extended[:, margin - offset : margin - offset + row_count]
        )
    query_filt = filtered[0]
    key_filt = filtered[1]
    value_filt = filtered[2]
    mixed_in = key_filt * value_filt
    spectra = to_freq(jnp.stack([mixed_in, long_filter.astype(jnp.float32)], axis=1))
    mixed_spec, filter_spec = unpack_fields(spectra, comp_axis, field_axis)
    convolved = from_freq(
        pack_fields([times_pair(mixed_spec, filter_spec, False)], comp_axis, field_axis)
    )[:, 0]
    output = (query_filt * convolved).astype(jnp.bfloat16)
    grad_in = out_grad.astype(jnp.float32)
    gate_grad = grad_in * convolved
    conv_grad = grad_in * query_filt
    grad_spec = unpack_fields(to_freq(conv_grad[:, None, :]), comp_axis, field_axis)[0]
    returned = from_freq(
        pack_fields(
            [times_pair(grad_spec, filter_spec, True), times_pair(grad_spec, mixed_spec, True)],
            comp_axis,
            field_axis,
        )
    )
    grad_scale = 1.0 / math.sqrt(part_count * row_count)
    mixed_grad = returned[:, 0]
    filter_grad = returned[:, 1] * grad_scale
    grad_stack = jnp.stack([gate_grad, mixed_grad * value_filt, mixed_grad * key_filt])
    later_rows = passed_along(grad_stack[:, :margin], "ctx", -1)
    padded_grad = jnp.concatenate([grad_stack, later_rows], axis=1)
    input_grads = tap_gain[:, 0, None, :] * grad_stack
    for offset in range(1, tap_count):
        input_grads = (
            input_grads + tap_gain[:, offset, None, :] * padded_grad[:, offset : offset + row_count]
        )
    partial_taps = jnp.stack(
        [
            jnp.sum(grad_stack * extended[:, margin - offset : margin - offset + row_count], axis=1)
            for offset in range(tap_count)
        ],
        axis=1,
    )
    taps_grad = lax.psum(partial_taps, "ctx") * grad_scale
    return (
        output,
        input_grads[0].astype(jnp.bfloat16),
        input_grads[1].astype(jnp.bfloat16),
        input_grads[2].astype(jnp.bfloat16),
        filter_grad,
        taps_grad,
    )


RADIX = 8
FIELDS = 5
CLASSES = (0, 8, 4, 2, 6, 1, 5, 9, 13)
LANES = 128
PAD = 8
CHUNK = 16
CURVE = 15.0
REACH = 120.0
SLOPE = 2.0 * REACH / math.log2(1.0 + CURVE)
TINY = 1e-30


def split_pair(values):
    high = values.astype(jnp.bfloat16)
    low = (values - high.astype(jnp.float32)).astype(jnp.bfloat16)
    return high, low


@lru_cache(maxsize=None)
def class_tables(rows):
    length = 2 * RADIX * rows
    back = np.arange(rows)
    forward, inverse = [], []
    for residue in CLASSES:
        product = np.outer(2 * RADIX * back + residue, back) % length
        angle = -2.0 * np.pi * product / length
        cosine, sine = np.cos(angle), np.sin(angle)
        forward.append(np.block([[cosine, -sine], [sine, cosine]]))
        weight = (1.0 if residue in (0, RADIX) else 2.0) / length
        inverse.append(weight * np.block([[cosine.T, sine.T], [-sine.T, cosine.T]]))
    tables = []
    for table in (np.stack(forward), np.stack(inverse)):
        high = table.astype(ml_dtypes.bfloat16)
        low = (table - high.astype(np.float64)).astype(ml_dtypes.bfloat16)
        tables += [high, low]
    return tables


ROOT = math.sqrt(0.5)
COS1 = math.cos(math.pi / 8)
SIN1 = math.sin(math.pi / 8)


def forward_classes(x):
    u = [x[a] + x[a + 4] for a in range(4)]
    d = [x[a] - x[a + 4] for a in range(4)]
    even, odd = u[0] + u[2], u[1] + u[3]
    dif, tot = ROOT * (d[1] - d[3]), ROOT * (d[1] + d[3])
    found = [
        (even + odd, None),
        (even - odd, None),
        (u[0] - u[2], u[3] - u[1]),
        (d[0] + dif, -d[2] - tot),
        (d[0] - dif, d[2] - tot),
    ]
    w0 = (x[0], -x[4])
    w1 = (COS1 * x[1] - SIN1 * x[5], -SIN1 * x[1] - COS1 * x[5])
    w2 = (ROOT * (x[2] - x[6]), -ROOT * (x[2] + x[6]))
    w3 = (SIN1 * x[3] - COS1 * x[7], -COS1 * x[3] - SIN1 * x[7])
    s02 = (w0[0] + w2[0], w0[1] + w2[1])
    d02 = (w0[0] - w2[0], w0[1] - w2[1])
    s13 = (w1[0] + w3[0], w1[1] + w3[1])
    d13 = (w1[0] - w3[0], w1[1] - w3[1])
    found.append((s02[0] + s13[0], s02[1] + s13[1]))
    found.append((d02[0] + d13[1], d02[1] - d13[0]))
    found.append((s02[0] - s13[0], s02[1] - s13[1]))
    found.append((d02[0] - d13[1], d02[1] + d13[0]))
    return found


def inverse_classes(z):
    (z0, _), (z8, _), (r4, i4), (r2, i2), (r6, i6) = z[:5]
    up, down = z0 + z8, z0 - z8
    even = [up + r4, down - i4, up - r4, down + i4]
    gap, tot = ROOT * (r2 - r6), ROOT * (i2 + i6)
    turn = [r2 + r6, gap - tot, i6 - i2, -gap - tot]
    (r1, i1), (r5, i5), (r9, i9), (rd, id_) = z[5:]
    s = (r1 + r9, i1 + i9)
    d = (r1 - r9, i1 - i9)
    t = (r5 + rd, i5 + id_)
    e = (r5 - rd, i5 - id_)
    s0 = (s[0] + t[0], s[1] + t[1])
    s2 = (s[0] - t[0], s[1] - t[1])
    s1 = (d[0] - e[1], d[1] + e[0])
    s3 = (d[0] + e[1], d[1] - e[0])
    q = [
        s0,
        (COS1 * s1[0] - SIN1 * s1[1], SIN1 * s1[0] + COS1 * s1[1]),
        (ROOT * (s2[0] - s2[1]), ROOT * (s2[0] + s2[1])),
        (SIN1 * s3[0] - COS1 * s3[1], COS1 * s3[0] + SIN1 * s3[1]),
    ]
    return [even[a] + turn[a] + q[a][0] for a in range(4)] + [
        even[a] - turn[a] - q[a][1] for a in range(4)
    ]


def log_code(values, inverse_scale):
    share = 1.0 + CURVE * (jnp.abs(values) * inverse_scale)
    code = jnp.exp2(jnp.log2(share) * SLOPE - REACH)
    return jnp.where(values < 0.0, -code, code).astype(jnp.bfloat16)


def log_decode(code, scale):
    code = code.astype(jnp.float32)
    share = jnp.exp2((jnp.log2(jnp.abs(code)) + REACH) * (1.0 / SLOPE)) - 1.0
    values = share * (scale * (1.0 / CURVE))
    return jnp.where(code < 0.0, -values, values)


def layer_kernel(
    taps_ref, got_ref, fh_any, fl_any, ih_any, il_any, out_ref,
    qp, kp, vp, qs, ks, vs, xh, xl, zs, conv, mgrad, fgrad, peak, sums, head,
    fh_ref, fl_ref, ih_ref, il_ref, table_sem,
):
    blocks, height, _ = got_ref.shape
    rows = height // FIELDS
    total = blocks * rows
    chunks = rows // CHUNK
    f32 = jnp.float32
    copies = [
        pltpu.make_async_copy(src, dst, table_sem.at[n])
        for n, (src, dst) in enumerate(
            ((fh_any, fh_ref), (fl_any, fl_ref), (ih_any, ih_ref), (il_any, il_ref))
        )
    ]
    for copy in copies:
        copy.start()
    zero = jnp.zeros((PAD, LANES), f32)
    for ref in (qp, kp, vp):
        ref[pl.ds(0, PAD), :] = zero
    gain = [[taps_ref[3 * i + j : 3 * i + j + 1, :] for j in range(3)] for i in range(3)]

    def widen(step, carry):
        b0 = pl.multiple_of(step * CHUNK, CHUNK)
        for a in range(blocks):
            for field, ref in enumerate((qp, kp, vp)):
                ref[pl.ds(PAD + a * rows + b0, CHUNK), :] = got_ref[
                    a, pl.ds(field * rows + b0, CHUNK), :
                ].astype(f32)
        return carry

    lax.fori_loop(0, chunks, widen, 0)
    for f in (0, 1):
        xh[f, pl.ds(rows, rows), :] = jnp.zeros((rows, 3 * LANES), jnp.bfloat16)
        xl[f, pl.ds(rows, rows), :] = jnp.zeros((rows, 3 * LANES), jnp.bfloat16)

    def short(ref, i, at):
        return (
            gain[i][0] * ref[pl.ds(at, CHUNK), :]
            + gain[i][1] * ref[pl.ds(at - 1, CHUNK), :]
            + gain[i][2] * ref[pl.ds(at - 2, CHUNK), :]
        )

    def enter(step, carry):
        b0 = pl.multiple_of(step * CHUNK, CHUNK)

        def put(column, values):
            for f, (real, imag) in enumerate(forward_classes(values)):
                for part, value in ((0, real), (1, imag)):
                    if value is not None:
                        high, low = split_pair(value)
                        place = (f, pl.ds(part * rows + b0, CHUNK), pl.ds(column * LANES, LANES))
                        xh[place] = high
                        xl[place] = low

        mixed = []
        for a in range(blocks):
            at = a * rows + b0
            key_filt = short(kp, 1, PAD + at)
            value_filt = short(vp, 2, PAD + at)
            ks[pl.ds(at, CHUNK), :] = key_filt
            vs[pl.ds(at, CHUNK), :] = value_filt
            mixed.append(key_filt * value_filt)
        put(0, mixed)
        put(1, [got_ref[a, pl.ds(3 * rows + b0, CHUNK), :].astype(f32) for a in range(blocks)])
        conv_grad = []
        for a in range(blocks):
            at = a * rows + b0
            query_filt = short(qp, 0, PAD + at)
            conv_grad.append(
                query_filt * got_ref[a, pl.ds(4 * rows + b0, CHUNK), :].astype(f32)
            )
        put(2, conv_grad)
        return carry

    lax.fori_loop(0, chunks, enter, 0)
    for copy in copies:
        copy.wait()

    def three(high_table, low_table, high, low):
        return (
            jnp.dot(high_table, high, preferred_element_type=f32)
            + jnp.dot(high_table, low, preferred_element_type=f32)
            + jnp.dot(low_table, high, preferred_element_type=f32)
        )

    def turn(f, carry):
        spec = three(fh_ref[f], fl_ref[f], xh[f], xl[f])
        (mr, hr, gr), (mi, hi, gi) = [
            [spec[p * rows : (p + 1) * rows, c * LANES : (c + 1) * LANES] for c in range(3)]
            for p in range(2)
        ]
        real = jnp.concatenate([mr * hr - mi * hi, gr * hr + gi * hi, gr * mr + gi * mi], axis=1)
        imag = jnp.concatenate([mr * hi + mi * hr, gi * hr - gr * hi, gi * mr - gr * mi], axis=1)
        high, low = split_pair(jnp.concatenate([real, imag], axis=0))
        zs[f] = three(ih_ref[f], il_ref[f], high, low)
        return carry

    lax.fori_loop(0, len(CLASSES), turn, 0)
    peak[...] = jnp.zeros_like(peak)
    sums[...] = jnp.zeros_like(sums)

    def leave(step, carry):
        b0 = pl.multiple_of(step * CHUNK, CHUNK)

        def take(column, ref):
            lanes = pl.ds(column * LANES, LANES)
            found = inverse_classes(
                [
                    (zs[f, pl.ds(b0, CHUNK), lanes], zs[f, pl.ds(rows + b0, CHUNK), lanes])
                    for f in range(len(CLASSES))
                ]
            )
            for a, value in enumerate(found):
                ref[pl.ds(a * rows + b0, CHUNK), :] = value
                size = jnp.abs(value)
                peak[column, a] = jnp.maximum(peak[column, a], jnp.maximum(size[:8], size[8:]))
            return found

        def add(i, source, grads):
            found = [jnp.zeros((CHUNK, LANES), f32)] * 3
            for a, now in enumerate(grads):
                for j in range(3):
                    found[j] = found[j] + now * source[pl.ds(PAD + a * rows + b0 - j, CHUNK), :]
            for j in range(3):
                sums[3 * i + j] += found[j][:8] + found[j][8:]

        found = take(0, conv)
        add(0, qp, [
            value * got_ref[a, pl.ds(4 * rows + b0, CHUNK), :].astype(f32)
            for a, value in enumerate(found)
        ])
        found = take(1, mgrad)
        add(1, kp, [
            value * vs[pl.ds(a * rows + b0, CHUNK), :] for a, value in enumerate(found)
        ])
        add(2, vp, [
            value * ks[pl.ds(a * rows + b0, CHUNK), :] for a, value in enumerate(found)
        ])
        take(2, fgrad)
        return carry

    lax.fori_loop(0, chunks, leave, 0)
    grad_scale = 1.0 / math.sqrt(total)
    head[pl.ds(0, 48), :] = jnp.zeros((48, LANES), f32)
    for n in range(9):
        at = 32 + n if n < 8 else 22
        head[pl.ds(at, 1), :] = jnp.sum(sums[n], axis=0, keepdims=True) * grad_scale
    head[pl.ds(40, 8), :] = split_pair(head[pl.ds(32, 8), :])[1].astype(f32)
    for a in range(blocks):
        first = a * rows
        for i, ref in enumerate((qp, kp, vp)):
            head[pl.ds(2 * i, 2), :] = ref[pl.ds(PAD + first - 2, 2), :]
        for column, ref in enumerate((conv, mgrad, fgrad)):
            top = jnp.max(peak[column, a], axis=0, keepdims=True)
            scale = jnp.maximum(top * (1.0 + 2.0**-7), TINY).astype(jnp.bfloat16).astype(f32)
            head[pl.ds(6 + column, 1), :] = scale
            out_ref[a, pl.ds(column * rows, rows), :] = log_code(
                ref[pl.ds(first, rows), :], 1.0 / scale
            )
        if a + 1 < blocks:
            after = first + rows
            grad_in = got_ref[a + 1, pl.ds(4 * rows, CHUNK), :].astype(f32)[:2]
            head[pl.ds(16, 2), :] = conv[pl.ds(after, 2), :] * grad_in
            head[pl.ds(18, 2), :] = mgrad[pl.ds(after, 2), :] * vs[pl.ds(after, 2), :]
            head[pl.ds(20, 2), :] = mgrad[pl.ds(after, 2), :] * ks[pl.ds(after, 2), :]
        else:
            head[pl.ds(16, 6), :] = jnp.zeros((6, LANES), f32)
        head[pl.ds(24, 8), :] = split_pair(head[pl.ds(16, 8), :])[1].astype(f32)
        out_ref[a, pl.ds(3 * rows, 48), :] = head[...].astype(jnp.bfloat16)


def whole_vmem(count):
    return [pl.BlockSpec(memory_space=pltpu.VMEM)] * count


def pack_kernel(*refs):
    *sources, out_ref = refs
    rows = sources[0].shape[0]
    for a in range(out_ref.shape[0]):
        for field, ref in enumerate(sources):
            out_ref[a, pl.ds(field * rows, rows), :] = ref[:, a * LANES : (a + 1) * LANES]


def finish_kernel(
    got_ref, query_ref, key_ref, value_ref, cot_ref, taps_ref,
    output, query_grad, key_grad, value_grad, filter_grad, taps_grad,
    wide, grads,
):
    rows = output.shape[0]
    f32, bf16 = jnp.float32, jnp.bfloat16
    for a in range(got_ref.shape[0]):
        lanes = slice(a * LANES, (a + 1) * LANES)
        head = got_ref[a, pl.ds(3 * rows, 48), :].astype(f32)
        conv, mixed_grad, filt = [
            log_decode(got_ref[a, pl.ds(n * rows, rows), :], head[6 + n : 7 + n]) for n in range(3)
        ]
        filter_grad[:, lanes] = filt * (1.0 / math.sqrt(got_ref.shape[0] * rows))
        taps = head[32:40] + head[40:48]
        for n in range(8):
            taps_grad[n // 3, n % 3 : n % 3 + 1, lanes] = taps[n : n + 1]
        pairs = head[16:24] + head[24:32]
        taps_grad[2, 2:3, lanes] = pairs[6:7]
        filtered = []
        gain = []
        for i, ref in enumerate((query_ref, key_ref, value_ref)):
            gain.append([taps_ref[i, j : j + 1, lanes].astype(f32) for j in range(3)])
            wide[i, pl.ds(PAD - 2, 2), :] = head[2 * i : 2 * i + 2]
            wide[i, pl.ds(PAD, rows), :] = ref[:, lanes].astype(f32)
            filtered.append(
                gain[i][0] * wide[i, pl.ds(PAD, rows), :]
                + gain[i][1] * wide[i, pl.ds(PAD - 1, rows), :]
                + gain[i][2] * wide[i, pl.ds(PAD - 2, rows), :]
            )
        output[:, lanes] = (filtered[0] * conv).astype(bf16)
        inner = (
            conv * cot_ref[:, lanes].astype(f32),
            mixed_grad * filtered[2],
            mixed_grad * filtered[1],
        )
        for i, ref in enumerate((query_grad, key_grad, value_grad)):
            grads[i, pl.ds(0, rows), :] = inner[i]
            grads[i, pl.ds(rows, 2), :] = pairs[2 * i : 2 * i + 2]
            ref[:, lanes] = (
                gain[i][0] * inner[i]
                + gain[i][1] * grads[i, pl.ds(1, rows), :]
                + gain[i][2] * grads[i, pl.ds(2, rows), :]
            ).astype(bf16)


def local_fast(query_in, key_in, value_in, long_filter, short_taps, out_grad):
    rows, channels = query_in.shape
    blocks = lax.axis_size("ctx")
    total = blocks * rows
    f32, bf16 = jnp.float32, jnp.bfloat16
    shape = jax.ShapeDtypeStruct
    packed = pl.pallas_call(
        pack_kernel,
        out_shape=shape((blocks, FIELDS * rows, LANES), bf16),
        in_specs=whole_vmem(5),
        out_specs=whole_vmem(1)[0],
        name="pack",
    )(query_in, key_in, value_in, long_filter, out_grad)
    got = lax.all_to_all(packed, "ctx", 0, 0)
    gain = lax.dynamic_slice_in_dim(
        short_taps.reshape(9, channels), lax.axis_index("ctx") * LANES, LANES, 1
    ).astype(f32)
    tables = class_tables(rows)
    count = len(CLASSES)
    done = pl.pallas_call(
        layer_kernel,
        out_shape=shape((blocks, 3 * rows + 48, LANES), bf16),
        in_specs=whole_vmem(2) + [pl.BlockSpec(memory_space=pl.ANY)] * 4,
        out_specs=whole_vmem(1)[0],
        scratch_shapes=[pltpu.VMEM((total + PAD, LANES), f32)] * 3
        + [pltpu.VMEM((total, LANES), f32)] * 3
        + [pltpu.VMEM((count, 2 * rows, 3 * LANES), bf16)] * 2
        + [pltpu.VMEM((count, 2 * rows, 3 * LANES), f32)]
        + [pltpu.VMEM((total, LANES), f32)] * 3
        + [
            pltpu.VMEM((3, blocks, 8, LANES), f32),
            pltpu.VMEM((9, 8, LANES), f32),
            pltpu.VMEM((48, LANES), f32),
        ]
        + [pltpu.VMEM((count, 2 * rows, 2 * rows), bf16)] * 4
        + [pltpu.SemaphoreType.DMA((4,))],
        compiler_params=pltpu.CompilerParams(vmem_limit_bytes=48 * 1024 * 1024),
        name="layer",
    )(gain, got, *tables)
    back = lax.all_to_all(done, "ctx", 0, 0)
    return tuple(
        pl.pallas_call(
            finish_kernel,
            out_shape=[shape((rows, channels), bf16)] * 4
            + [shape((rows, channels), f32), shape((3, 3, channels), f32)],
            in_specs=whole_vmem(6),
            out_specs=whole_vmem(6),
            scratch_shapes=[
                pltpu.VMEM((3, PAD + rows, LANES), f32),
                pltpu.VMEM((3, rows + PAD, LANES), f32),
            ],
            name="finish",
        )(back, query_in, key_in, value_in, out_grad, short_taps)
    )


def local(query_in, key_in, value_in, long_filter, short_taps, out_grad):
    rows, channels = query_in.shape
    blocks = lax.axis_size("ctx")
    taps = short_taps.shape[:2]
    if blocks == RADIX and channels == blocks * LANES and rows == LANES and taps == (3, 3):
        return local_fast(query_in, key_in, value_in, long_filter, short_taps, out_grad)
    return local_general(query_in, key_in, value_in, long_filter, short_taps, out_grad)


def solution(mesh):
    placed = (
        P("ctx", "tp"),
        P("ctx", "tp"),
        P("ctx", "tp"),
        P("ctx", "tp"),
        P(None, None, "tp"),
        P("ctx", "tp"),
    )
    return jax.shard_map(
        local,
        mesh=mesh,
        in_specs=placed,
        out_specs=(
            P("ctx", "tp"),
            P("ctx", "tp"),
            P("ctx", "tp"),
            P("ctx", "tp"),
            P("ctx", "tp"),
            P(None, None, "tp"),
        ),
        check_vma=False,
    )
```

```python
from functools import lru_cache, partial
import math

import jax
import jax.numpy as jnp
import ml_dtypes
import numpy as np
from jax import lax
from jax.experimental import pallas as pl
from jax.experimental.pallas import tpu as pltpu
from jax.sharding import PartitionSpec as P

HIGHEST_PREC = lax.Precision.HIGHEST
TWO_PI = 2.0 * math.pi


def passed_along(block, axis, distance):
    devices = range(lax.axis_size(axis))
    route = [(i - distance, i) for i in devices if i - distance in devices]
    return lax.ppermute(block, axis, route)


def phase_pair(count_a, count_b, period, direction):
    product = (
        jnp.arange(count_a, dtype=jnp.int32)[:, None]
        * jnp.arange(count_b, dtype=jnp.int32)[None, :]
    )
    phase_angle = direction * TWO_PI / period * (product % period).astype(jnp.float32)
    return (jnp.cos(phase_angle), jnp.sin(phase_angle))


def rotate_pair(real_part, imag_part, cosine, sine_part):
    return (real_part * cosine - imag_part * sine_part, real_part * sine_part + imag_part * cosine)


def times_pair(first_pair, second_pair, conj_second):
    factor = -1.0 if conj_second else 1.0
    real_part = first_pair[0] * second_pair[0] - factor * first_pair[1] * second_pair[1]
    imag_part = first_pair[1] * second_pair[0] + factor * first_pair[0] * second_pair[1]
    return (real_part, imag_part)


def unpack_fields(spectrum, comp_axis, field_axis):
    collected = []
    for partner_rank in range(spectrum.shape[field_axis]):
        single = lax.index_in_dim(spectrum, partner_rank, field_axis, keepdims=True)
        collected.append(
            (
                lax.index_in_dim(single, 0, comp_axis, keepdims=True),
                lax.index_in_dim(single, 1, comp_axis, keepdims=True),
            )
        )
    return collected


def pack_fields(pairs, comp_axis, field_axis):
    return jnp.concatenate(
        [jnp.concatenate([real_part, imag_part], axis=comp_axis) for real_part, imag_part in pairs],
        axis=field_axis,
    )


def spread_forward(regroup, fields):
    row_count, field_count, channels = fields.shape
    part_count = lax.axis_size("ctx")
    block_rows = row_count // part_count
    length = 2 * part_count * row_count
    my_index = lax.axis_index("ctx")
    gathered = regroup(fields.reshape(part_count, 1, block_rows, field_count, channels))
    cosine, sine_part = phase_pair(2 * part_count, part_count, 2 * part_count, -1.0)
    first_table = jnp.stack([cosine, sine_part], axis=1)
    first_pass = jnp.einsum("kda,arfc->kdrfc", first_table, gathered, precision=HIGHEST_PREC)
    row_index = my_index * block_rows + jnp.arange(block_rows, dtype=jnp.int32)
    twist_index = jnp.arange(2 * part_count, dtype=jnp.int32)[:, None] * row_index[None, :] % length
    phase_angle = -TWO_PI / length * twist_index.astype(jnp.float32)
    cos_twist = jnp.cos(phase_angle)[:, :, None, None]
    sin_twist = jnp.sin(phase_angle)[:, :, None, None]
    real_part, imag_part = rotate_pair(first_pass[:, 0], first_pass[:, 1], cos_twist, sin_twist)
    turned = jnp.stack([real_part, imag_part], axis=1)
    arrived = regroup(turned.reshape(part_count, 1, 2, 2, block_rows, field_count, channels))
    cosine, sine_part = phase_pair(row_count, row_count, row_count, -1.0)
    second_table = jnp.stack(
        [jnp.stack([cosine, sine_part], axis=-1), jnp.stack([-sine_part, cosine], axis=-1)], axis=0
    )
    second_table = second_table.reshape(2, part_count, block_rows, row_count, 2)
    return jnp.einsum("pqsrfc,sprkd->qkdfc", arrived, second_table, precision=HIGHEST_PREC)


def spread_inverse(regroup, spectrum):
    pair_count, row_count, _, field_count, channels = spectrum.shape
    part_count = lax.axis_size("ctx")
    block_rows = row_count // part_count
    length = 2 * part_count * row_count
    my_index = lax.axis_index("ctx")
    cosine, sine_part = phase_pair(row_count, row_count, row_count, 1.0)
    second_table = jnp.stack(
        [jnp.stack([cosine, sine_part], axis=-1), jnp.stack([-sine_part, cosine], axis=-1)], axis=0
    )
    second_table = second_table.reshape(2, row_count, part_count, block_rows, 2)
    row_parts = jnp.einsum("qkdfc,dkprs->pqsrfc", spectrum, second_table, precision=HIGHEST_PREC)
    freq_index = my_index * pair_count + jnp.arange(pair_count, dtype=jnp.int32)
    twist_index = freq_index[:, None] * jnp.arange(row_count, dtype=jnp.int32)[None, :] % length
    phase_angle = TWO_PI / length * twist_index.astype(jnp.float32)
    cos_twist = (
        jnp.cos(phase_angle)
        .reshape(pair_count, part_count, block_rows)
        .transpose(1, 0, 2)[:, :, :, None, None]
    )
    sin_twist = (
        jnp.sin(phase_angle)
        .reshape(pair_count, part_count, block_rows)
        .transpose(1, 0, 2)[:, :, :, None, None]
    )
    real_part, imag_part = rotate_pair(row_parts[:, :, 0], row_parts[:, :, 1], cos_twist, sin_twist)
    turned = jnp.stack([real_part, imag_part], axis=2)
    arrived = regroup(
        turned.reshape(part_count, 1, pair_count, 2, block_rows, field_count, channels)
    )
    cosine, sine_part = phase_pair(2 * part_count, part_count, 2 * part_count, 1.0)
    first_table = (jnp.stack([cosine, -sine_part], axis=1) / length).reshape(
        part_count, pair_count, 2, part_count
    )
    values = jnp.einsum("pqsrfc,pqsa->arfc", arrived, first_table, precision=HIGHEST_PREC)
    returned = regroup(values.reshape(part_count, 1, block_rows, field_count, channels))
    return returned.reshape(row_count, field_count, channels)


def local_general(query_in, key_in, value_in, long_filter, short_taps, out_grad):
    row_count = query_in.shape[0]
    tap_count = short_taps.shape[1]
    margin = tap_count - 1
    part_count = lax.axis_size("ctx")

    def regroup(blocks):
        return lax.all_to_all(blocks, "ctx", split_axis=0, concat_axis=1, tiled=True)[0]

    to_freq = partial(spread_forward, regroup)
    from_freq = partial(spread_inverse, regroup)
    comp_axis = 2
    field_axis = 3
    inputs = jnp.stack([query_in, key_in, value_in])
    earlier = passed_along(inputs[:, row_count - margin :], "ctx", 1)
    extended = jnp.concatenate([earlier, inputs], axis=1).astype(jnp.float32)
    tap_gain = short_taps.astype(jnp.float32)
    filtered = tap_gain[:, 0, None, :] * extended[:, margin:]
    for offset in range(1, tap_count):
        filtered = (
            filtered
            + tap_gain[:, offset, None, :]
            * extended[:, margin - offset : margin - offset + row_count]
        )
    query_filt = filtered[0]
    key_filt = filtered[1]
    value_filt = filtered[2]
    mixed_in = key_filt * value_filt
    spectra = to_freq(jnp.stack([mixed_in, long_filter.astype(jnp.float32)], axis=1))
    mixed_spec, filter_spec = unpack_fields(spectra, comp_axis, field_axis)
    convolved = from_freq(
        pack_fields([times_pair(mixed_spec, filter_spec, False)], comp_axis, field_axis)
    )[:, 0]
    output = (query_filt * convolved).astype(jnp.bfloat16)
    grad_in = out_grad.astype(jnp.float32)
    gate_grad = grad_in * convolved
    conv_grad = grad_in * query_filt
    grad_spec = unpack_fields(to_freq(conv_grad[:, None, :]), comp_axis, field_axis)[0]
    returned = from_freq(
        pack_fields(
            [times_pair(grad_spec, filter_spec, True), times_pair(grad_spec, mixed_spec, True)],
            comp_axis,
            field_axis,
        )
    )
    grad_scale = 1.0 / math.sqrt(part_count * row_count)
    mixed_grad = returned[:, 0]
    filter_grad = returned[:, 1] * grad_scale
    grad_stack = jnp.stack([gate_grad, mixed_grad * value_filt, mixed_grad * key_filt])
    later_rows = passed_along(grad_stack[:, :margin], "ctx", -1)
    padded_grad = jnp.concatenate([grad_stack, later_rows], axis=1)
    input_grads = tap_gain[:, 0, None, :] * grad_stack
    for offset in range(1, tap_count):
        input_grads = (
            input_grads + tap_gain[:, offset, None, :] * padded_grad[:, offset : offset + row_count]
        )
    partial_taps = jnp.stack(
        [
            jnp.sum(grad_stack * extended[:, margin - offset : margin - offset + row_count], axis=1)
            for offset in range(tap_count)
        ],
        axis=1,
    )
    taps_grad = lax.psum(partial_taps, "ctx") * grad_scale
    return (
        output,
        input_grads[0].astype(jnp.bfloat16),
        input_grads[1].astype(jnp.bfloat16),
        input_grads[2].astype(jnp.bfloat16),
        filter_grad,
        taps_grad,
    )


RADIX = 8
FIELDS = 5
CLASSES = (4, 2, 6, 1, 5, 9, 13)
LANES = 128
PAD = 8
CHUNK = 16
PLACES = (0, 6, 2, 5, 3, 7, 4, 1)
CURVE = 15.0
REACH = 120.0
SLOPE = 2.0 * REACH / math.log2(1.0 + CURVE)
TINY = 1e-30


def split_pair(values):
    high = values.astype(jnp.bfloat16)
    low = (values - high.astype(jnp.float32)).astype(jnp.bfloat16)
    return high, low


@lru_cache(maxsize=None)
def class_tables(rows):
    length = 2 * RADIX * rows
    back = np.arange(rows)

    def waves(residue, count):
        angle = 2.0 * np.pi * (np.outer(2 * RADIX * np.arange(count) + residue, back) % length) / length
        return np.cos(angle), np.sin(angle)

    half = rows // 2
    cos0, sin0 = waves(0, half)
    cos8, sin8 = waves(RADIX, half)
    none = np.zeros((half, rows))
    middle = (1.0 - 2.0 * (back % 2))[None, :]
    imag0 = np.concatenate([middle, -sin0[1:]])
    first = np.block([[cos0, none], [none, cos8], [imag0, none], [none, -sin8]])
    weight = np.full((2 * rows, 1), 2.0)
    weight[0] = weight[rows] = 1.0
    cosine, sine = waves(0, rows)
    other = np.block([[cosine, sine], [-sine, cosine]])
    tables = []
    for table in (np.stack([first, other]), np.stack([(weight * first).T, 2.0 * other.T]) / length):
        high = table.astype(ml_dtypes.bfloat16)
        low = (table - high.astype(np.float64)).astype(ml_dtypes.bfloat16)
        tables.append(np.stack([high, low]))
    turns = np.zeros((rows, LANES), np.float32)
    for n, residue in enumerate(CLASSES):
        turns[:, 2 * n], turns[:, 2 * n + 1] = [wave[0] for wave in waves(residue, 1)]
    return (*tables, turns)


ROOT = math.sqrt(0.5)
COS1 = math.cos(math.pi / 8)
SIN1 = math.sin(math.pi / 8)


def forward_classes(x):
    u = [x[a] + x[a + 4] for a in range(4)]
    d = [x[a] - x[a + 4] for a in range(4)]
    even, odd = u[0] + u[2], u[1] + u[3]
    dif, tot = ROOT * (d[1] - d[3]), ROOT * (d[1] + d[3])
    found = [
        (even + odd, even - odd),
        (u[0] - u[2], u[3] - u[1]),
        (d[0] + dif, -d[2] - tot),
        (d[0] - dif, d[2] - tot),
    ]
    w0 = (x[0], -x[4])
    w1 = (COS1 * x[1] - SIN1 * x[5], -SIN1 * x[1] - COS1 * x[5])
    w2 = (ROOT * (x[2] - x[6]), -ROOT * (x[2] + x[6]))
    w3 = (SIN1 * x[3] - COS1 * x[7], -COS1 * x[3] - SIN1 * x[7])
    s02 = (w0[0] + w2[0], w0[1] + w2[1])
    d02 = (w0[0] - w2[0], w0[1] - w2[1])
    s13 = (w1[0] + w3[0], w1[1] + w3[1])
    d13 = (w1[0] - w3[0], w1[1] - w3[1])
    found.append((s02[0] + s13[0], s02[1] + s13[1]))
    found.append((d02[0] + d13[1], d02[1] - d13[0]))
    found.append((s02[0] - s13[0], s02[1] - s13[1]))
    found.append((d02[0] - d13[1], d02[1] + d13[0]))
    return found


def inverse_classes(z):
    (z0, z8), (r4, i4), (r2, i2), (r6, i6) = z[:4]
    up, down = z0 + z8, z0 - z8
    even = [up + r4, down - i4, up - r4, down + i4]
    gap, tot = ROOT * (r2 - r6), ROOT * (i2 + i6)
    turn = [r2 + r6, gap - tot, i6 - i2, -gap - tot]
    (r1, i1), (r5, i5), (r9, i9), (rd, id_) = z[4:]
    s = (r1 + r9, i1 + i9)
    d = (r1 - r9, i1 - i9)
    t = (r5 + rd, i5 + id_)
    e = (r5 - rd, i5 - id_)
    s0 = (s[0] + t[0], s[1] + t[1])
    s2 = (s[0] - t[0], s[1] - t[1])
    s1 = (d[0] - e[1], d[1] + e[0])
    s3 = (d[0] + e[1], d[1] - e[0])
    q = [
        s0,
        (COS1 * s1[0] - SIN1 * s1[1], SIN1 * s1[0] + COS1 * s1[1]),
        (ROOT * (s2[0] - s2[1]), ROOT * (s2[0] + s2[1])),
        (SIN1 * s3[0] - COS1 * s3[1], COS1 * s3[0] + SIN1 * s3[1]),
    ]
    return [even[a] + turn[a] + q[a][0] for a in range(4)] + [
        even[a] - turn[a] - q[a][1] for a in range(4)
    ]


def log_code(values, inverse_scale):
    share = 1.0 + CURVE * (jnp.abs(values) * inverse_scale)
    code = jnp.exp2(jnp.log2(share) * SLOPE - REACH)
    return jnp.where(values < 0.0, -code, code).astype(jnp.bfloat16)


def log_decode(code, scale):
    code = code.astype(jnp.float32)
    share = jnp.exp2((jnp.log2(jnp.abs(code)) + REACH) * (1.0 / SLOPE)) - 1.0
    values = share * (scale * (1.0 / CURVE))
    return jnp.where(code < 0.0, -values, values)


def table_dot(table_ref, f, both):
    half = both.shape[1] // 2
    which = min(f, 1)
    found = jnp.dot(table_ref[0, which], both, preferred_element_type=jnp.float32)
    rest = jnp.dot(table_ref[1, which], both[:, :half], preferred_element_type=jnp.float32)
    return found[:, :half] + (found[:, half:] + rest)


def times_spec(first, second, conj_second, packed):
    (ar, ai), (br, bi) = first, second
    inner = ai * bi
    cross = ai * br - ar * bi if conj_second else ai * br + ar * bi
    if packed:
        line = lax.broadcasted_iota(jnp.int32, inner.shape, 0) == 0
        cross = jnp.where(line, inner, cross)
        inner = jnp.where(line, 0.0, inner)
    return (ar * br + inner if conj_second else ar * br - inner), cross


def spec_parts(spec, rows, column):
    lanes = slice(column * LANES, (column + 1) * LANES)
    return spec[:rows, lanes], spec[rows:, lanes]


def side_by_side(products):
    pairs = [split_pair(jnp.concatenate(pair, axis=0)) for pair in products]
    return jnp.concatenate([high for high, _ in pairs] + [low for _, low in pairs], axis=1)


def put_classes(ref, column, columns, rows, b0, values, turn):
    for f, pair in enumerate(forward_classes(values)):
        if f > 0:
            cosine, sine = [turn[2 * f - 2 + n, pl.ds(b0, CHUNK), :] for n in range(2)]
            pair = (pair[0] * cosine + pair[1] * sine, pair[1] * cosine - pair[0] * sine)
        for part, value in enumerate(pair):
            high, low = split_pair(value)
            at = pl.ds(part * rows + b0, CHUNK)
            ref[f, at, pl.ds(column * LANES, LANES)] = high
            ref[f, at, pl.ds((columns + column) * LANES, LANES)] = low


def take_classes(ref, column, rows, b0, turn):
    lanes = pl.ds(column * LANES, LANES)
    found = []
    for f in range(ref.shape[0]):
        pair = ref[f, pl.ds(b0, CHUNK), lanes], ref[f, pl.ds(rows + b0, CHUNK), lanes]
        if f > 0:
            cosine, sine = [turn[2 * f - 2 + n, pl.ds(b0, CHUNK), :] for n in range(2)]
            pair = (pair[0] * cosine - pair[1] * sine, pair[1] * cosine + pair[0] * sine)
        found.append(pair)
    return inverse_classes(found)


def short_filter(gain, ref, at):
    return (
        gain[0] * ref[pl.ds(at, CHUNK), :]
        + gain[1] * ref[pl.ds(at - 1, CHUNK), :]
        + gain[2] * ref[pl.ds(at - 2, CHUNK), :]
    )


def widen(me_ref, got, targets, rows):
    def body(step, carry):
        b0 = pl.multiple_of(step * CHUNK, CHUNK)
        for k, ref in zip(PLACES, got):
            at = pl.multiple_of((me_ref[0] ^ k) * rows + b0, CHUNK)
            for field, (target, pad) in enumerate(targets):
                target[pl.ds(pad + at, CHUNK), :] = ref[pl.ds(field * rows + b0, CHUNK), :].astype(
                    jnp.float32
                )
        return carry

    lax.fori_loop(0, rows // CHUNK, body, 0)


def gains(taps_ref):
    return [[taps_ref[3 * i + j : 3 * i + j + 1, :] for j in range(3)] for i in range(3)]


def layer_kernel(me_ref, gain_ref, turn, forward_ref, inverse_ref, *refs):
    got, outs = refs[:RADIX], refs[RADIX : 2 * RADIX]
    qp, kp, vp, hs, cot, ks, vs, xs, zs, conv, mgrad, fgrad, peak, sums, head = refs[2 * RADIX :]
    rows = got[0].shape[0] // FIELDS
    total = RADIX * rows
    f32 = jnp.float32
    gain = gains(gain_ref)
    for ref in (qp, kp, vp):
        ref[pl.ds(0, PAD), :] = jnp.zeros((PAD, LANES), f32)
    for ref in (cot, ks, vs, conv, mgrad):
        ref[pl.ds(total, PAD), :] = jnp.zeros((PAD, LANES), f32)
    widen(me_ref, got, ((qp, PAD), (kp, PAD), (vp, PAD), (hs, 0), (cot, 0)), rows)

    def enter(step, carry):
        b0 = pl.multiple_of(step * CHUNK, CHUNK)
        mixed = []
        for a in range(RADIX):
            at = a * rows + b0
            key_filt = short_filter(gain[1], kp, PAD + at)
            value_filt = short_filter(gain[2], vp, PAD + at)
            ks[pl.ds(at, CHUNK), :] = key_filt
            vs[pl.ds(at, CHUNK), :] = value_filt
            mixed.append(key_filt * value_filt)
        put_classes(xs, 0, 3, rows, b0, mixed, turn)
        filt = [hs[pl.ds(a * rows + b0, CHUNK), :] for a in range(RADIX)]
        put_classes(xs, 1, 3, rows, b0, filt, turn)
        conv_grad = []
        for a in range(RADIX):
            at = a * rows + b0
            conv_grad.append(short_filter(gain[0], qp, PAD + at) * cot[pl.ds(at, CHUNK), :])
        put_classes(xs, 2, 3, rows, b0, conv_grad, turn)
        return carry

    lax.fori_loop(0, rows // CHUNK, enter, 0)
    for f in range(xs.shape[0]):
        spec = table_dot(forward_ref, f, xs[f])
        mixed, filt, grad = [spec_parts(spec, rows, c) for c in range(3)]
        products = [
            times_spec(mixed, filt, False, f == 0),
            times_spec(grad, filt, True, f == 0),
            times_spec(grad, mixed, True, f == 0),
        ]
        zs[f] = table_dot(inverse_ref, f, side_by_side(products))
    peak[...] = jnp.zeros_like(peak)
    sums[...] = jnp.zeros_like(sums)

    def leave(step, carry):
        b0 = pl.multiple_of(step * CHUNK, CHUNK)

        def take(column, ref):
            found = take_classes(zs, column, rows, b0, turn)
            for a, value in enumerate(found):
                ref[pl.ds(a * rows + b0, CHUNK), :] = value
                size = jnp.abs(value)
                peak[column, a] = jnp.maximum(peak[column, a], jnp.maximum(size[:8], size[8:]))
            return found

        def add(i, source, values, other):
            found = [jnp.zeros((CHUNK, LANES), f32)] * 3
            for a, value in enumerate(values):
                at = a * rows + b0
                now = value * other[pl.ds(at, CHUNK), :]
                for j in range(3):
                    found[j] = found[j] + now * source[pl.ds(PAD + at - j, CHUNK), :]
            for j in range(3):
                sums[3 * i + j] += found[j][:8] + found[j][8:]

        add(0, qp, take(0, conv), cot)
        found = take(1, mgrad)
        add(1, kp, found, vs)
        add(2, vp, found, ks)
        take(2, fgrad)
        return carry

    lax.fori_loop(0, rows // CHUNK, leave, 0)
    grad_scale = 1.0 / math.sqrt(total)
    head[...] = jnp.zeros_like(head)
    for n in range(9):
        at = 32 + n if n < 8 else 22
        head[pl.ds(at, 1), :] = jnp.sum(sums[n], axis=0, keepdims=True) * grad_scale
    head[pl.ds(40, 8), :] = split_pair(head[pl.ds(32, 8), :])[1].astype(f32)
    for k, out_ref in zip(PLACES, outs):
        a = me_ref[0] ^ k
        first = pl.multiple_of(a * rows, rows)
        after = first + rows
        for i, ref in enumerate((qp, kp, vp)):
            head[pl.ds(2 * i, 2), :] = ref[pl.ds(first + PAD - 2, 2), :]
        for column, ref in enumerate((conv, mgrad, fgrad)):
            top = jnp.max(peak[column, a], axis=0, keepdims=True)
            scale = jnp.maximum(top * (1.0 + 2.0**-7), TINY).astype(jnp.bfloat16).astype(f32)
            head[pl.ds(6 + column, 1), :] = scale
            out_ref[pl.ds(column * rows, rows), :] = log_code(
                ref[pl.ds(first, rows), :], 1.0 / scale
            )
        for i, (ref, other) in enumerate(((conv, cot), (mgrad, vs), (mgrad, ks))):
            head[pl.ds(16 + 2 * i, 2), :] = ref[pl.ds(after, 2), :] * other[pl.ds(after, 2), :]
        head[pl.ds(24, 8), :] = split_pair(head[pl.ds(16, 8), :])[1].astype(f32)
        out_ref[pl.ds(3 * rows, 48), :] = head[...].astype(jnp.bfloat16)


def prepare_kernel(
    me_ref, turns_ref, forward_any, inverse_any, taps_any, _, turn, forward_ref, inverse_ref, gain_ref, wide_ref,
):
    lane = pl.ds(pl.multiple_of(me_ref[0] * LANES, LANES), LANES)
    forward_ref[...] = forward_any[...]
    inverse_ref[...] = inverse_any[...]
    for n in range(turn.shape[0]):
        turn[n] = jnp.broadcast_to(turns_ref[:, n : n + 1], turn.shape[1:])
    for i in range(3):
        for j in range(3):
            at = 3 * i + j
            wide_ref[at : at + 1, :] = taps_any[i, j : j + 1, :].astype(jnp.float32)
            gain_ref[at : at + 1, :] = taps_any[i, j : j + 1, lane].astype(jnp.float32)


def whole_vmem(count):
    return [pl.BlockSpec(memory_space=pltpu.VMEM)] * count


def whole_any(count):
    return [pl.BlockSpec(memory_space=pl.ANY)] * count


IN_SMEM = pl.BlockSpec(memory_space=pltpu.SMEM)


def pack_kernel(me_ref, *refs):
    sources, outs = refs[:FIELDS], refs[FIELDS:]
    rows = sources[0].shape[0]
    for k, out_ref in zip(PLACES, outs):
        lane = pl.multiple_of((me_ref[0] ^ k) * LANES, LANES)
        for field, source in enumerate(sources):
            out_ref[pl.ds(field * rows, rows), :] = source[:, pl.ds(lane, LANES)]


def finish_kernel(me_ref, *refs):
    got, (query_ref, key_ref, value_ref, cot_ref, taps_ref), outs = (
        refs[:RADIX],
        refs[RADIX : RADIX + 5],
        refs[RADIX + 5 :],
    )
    output, query_grad, key_grad, value_grad, filter_grad, taps_grad, wide, grads = outs
    rows = output.shape[0]
    f32, bf16 = jnp.float32, jnp.bfloat16
    for k, got_ref in zip(PLACES, got):
        lanes = pl.ds(pl.multiple_of((me_ref[0] ^ k) * LANES, LANES), LANES)
        head = got_ref[pl.ds(3 * rows, 48), :].astype(f32)
        conv, mixed_grad, filt = [
            log_decode(got_ref[pl.ds(n * rows, rows), :], head[6 + n : 7 + n]) for n in range(3)
        ]
        filter_grad[:, lanes] = filt * (1.0 / math.sqrt(RADIX * rows))
        taps = head[32:40] + head[40:48]
        for n in range(8):
            taps_grad[n // 3, n % 3 : n % 3 + 1, lanes] = taps[n : n + 1]
        pairs = head[16:24] + head[24:32]
        taps_grad[2, 2:3, lanes] = pairs[6:7]
        filtered = []
        gain = []
        for i, ref in enumerate((query_ref, key_ref, value_ref)):
            gain.append([taps_ref[3 * i + j : 3 * i + j + 1, lanes] for j in range(3)])
            wide[i, pl.ds(PAD - 2, 2), :] = head[2 * i : 2 * i + 2]
            wide[i, pl.ds(PAD, rows), :] = ref[:, lanes].astype(f32)
            filtered.append(
                gain[i][0] * wide[i, pl.ds(PAD, rows), :]
                + gain[i][1] * wide[i, pl.ds(PAD - 1, rows), :]
                + gain[i][2] * wide[i, pl.ds(PAD - 2, rows), :]
            )
        output[:, lanes] = (filtered[0] * conv).astype(bf16)
        inner = (
            conv * cot_ref[:, lanes].astype(f32),
            mixed_grad * filtered[2],
            mixed_grad * filtered[1],
        )
        for i, ref in enumerate((query_grad, key_grad, value_grad)):
            grads[i, pl.ds(0, rows), :] = inner[i]
            grads[i, pl.ds(rows, 2), :] = pairs[2 * i : 2 * i + 2]
            ref[:, lanes] = (
                gain[i][0] * inner[i]
                + gain[i][1] * grads[i, pl.ds(1, rows), :]
                + gain[i][2] * grads[i, pl.ds(2, rows), :]
            ).astype(bf16)


def swap_blocks(blocks):
    devices = range(RADIX)
    return [
        lax.ppermute(block, "ctx", [(i, i ^ k) for i in devices]) if k else block
        for k, block in zip(PLACES, blocks)
    ]


def held(arrays, space):
    return [pltpu.with_memory_space_constraint(jnp.asarray(one), space) for one in arrays]


def local_fast(query_in, key_in, value_in, long_filter, short_taps, out_grad):
    rows, channels = query_in.shape
    total = RADIX * rows
    f32, bf16 = jnp.float32, jnp.bfloat16
    shape = jax.ShapeDtypeStruct
    me = lax.axis_index("ctx").astype(jnp.int32).reshape(1)
    packed = pl.pallas_call(
        pack_kernel,
        out_shape=[pltpu.VMEM((FIELDS * rows, LANES), bf16)] * RADIX,
        in_specs=[IN_SMEM] + whole_vmem(FIELDS),
        out_specs=whole_vmem(RADIX),
        name="pack",
    )(me, query_in, key_in, value_in, long_filter, out_grad)
    got = swap_blocks(packed)
    forward, inverse, turns = class_tables(rows)
    count = 1 + len(CLASSES)
    ready = pl.pallas_call(
        prepare_kernel,
        out_shape=[
            pltpu.VMEM((2 * len(CLASSES), rows, LANES), f32),
            pltpu.VMEM(forward.shape, bf16),
            pltpu.VMEM(inverse.shape, bf16),
            pltpu.VMEM((16, LANES), f32),
            pltpu.VMEM((16, channels), f32),
        ],
        in_specs=[IN_SMEM] + whole_vmem(5),
        out_specs=whole_vmem(5),
        name="prepare",
    )(me, *held((turns, forward, inverse), pltpu.HBM), short_taps, *held(got[1:2], pltpu.VMEM))
    ready = held(ready, pltpu.VMEM)
    done = pl.pallas_call(
        layer_kernel,
        out_shape=[pltpu.VMEM((3 * rows + 48, LANES), bf16)] * RADIX,
        in_specs=[IN_SMEM] + whole_vmem(4 + RADIX),
        out_specs=whole_vmem(RADIX),
        scratch_shapes=[pltpu.VMEM((total + PAD, LANES), f32)] * 7
        + [
            pltpu.VMEM((count, 2 * rows, 6 * LANES), bf16),
            pltpu.VMEM((count, 2 * rows, 3 * LANES), f32),
        ]
        + [pltpu.VMEM((total + PAD, LANES), f32)] * 3
        + [
            pltpu.VMEM((3, RADIX, 8, LANES), f32),
            pltpu.VMEM((9, 8, LANES), f32),
            pltpu.VMEM((48, LANES), f32),
        ],
        compiler_params=pltpu.CompilerParams(vmem_limit_bytes=32 * 1024 * 1024),
        name="layer",
    )(me, ready[3], *ready[:3], *held(got, pltpu.VMEM))
    back = swap_blocks(done)
    return tuple(
        pl.pallas_call(
            finish_kernel,
            out_shape=[shape((rows, channels), bf16)] * 4
            + [shape((rows, channels), f32), shape((3, 3, channels), f32)],
            in_specs=[IN_SMEM] + whole_vmem(RADIX + 5),
            out_specs=whole_vmem(6),
            scratch_shapes=[
                pltpu.VMEM((3, PAD + rows, LANES), f32),
                pltpu.VMEM((3, rows + PAD, LANES), f32),
            ],
            name="finish",
        )(me, *held(back, pltpu.VMEM), query_in, key_in, value_in, out_grad, ready[4])
    )


def local(query_in, key_in, value_in, long_filter, short_taps, out_grad):
    rows, channels = query_in.shape
    blocks = lax.axis_size("ctx")
    taps = short_taps.shape[:2]
    if blocks == RADIX and channels == blocks * LANES and rows == LANES and taps == (3, 3):
        return local_fast(query_in, key_in, value_in, long_filter, short_taps, out_grad)
    return local_general(query_in, key_in, value_in, long_filter, short_taps, out_grad)


def solution(mesh):
    placed = (
        P("ctx", "tp"),
        P("ctx", "tp"),
        P("ctx", "tp"),
        P("ctx", "tp"),
        P(None, None, "tp"),
        P("ctx", "tp"),
    )
    return jax.shard_map(
        local,
        mesh=mesh,
        in_specs=placed,
        out_specs=(
            P("ctx", "tp"),
            P("ctx", "tp"),
            P("ctx", "tp"),
            P("ctx", "tp"),
            P("ctx", "tp"),
            P(None, None, "tp"),
        ),
        check_vma=False,
    )
```

```python
from functools import lru_cache, partial
import math

import jax
import jax.numpy as jnp
import ml_dtypes
import numpy as np
from jax import lax
from jax.experimental import pallas as pl
from jax.experimental.pallas import tpu as pltpu
from jax.sharding import PartitionSpec as P

HIGHEST_PREC = lax.Precision.HIGHEST
TWO_PI = 2.0 * math.pi


def passed_along(block, axis, distance):
    devices = range(lax.axis_size(axis))
    route = [(i - distance, i) for i in devices if i - distance in devices]
    return lax.ppermute(block, axis, route)


def phase_pair(count_a, count_b, period, direction):
    product = (
        jnp.arange(count_a, dtype=jnp.int32)[:, None]
        * jnp.arange(count_b, dtype=jnp.int32)[None, :]
    )
    phase_angle = direction * TWO_PI / period * (product % period).astype(jnp.float32)
    return (jnp.cos(phase_angle), jnp.sin(phase_angle))


def rotate_pair(real_part, imag_part, cosine, sine_part):
    return (real_part * cosine - imag_part * sine_part, real_part * sine_part + imag_part * cosine)


def times_pair(first_pair, second_pair, conj_second):
    factor = -1.0 if conj_second else 1.0
    real_part = first_pair[0] * second_pair[0] - factor * first_pair[1] * second_pair[1]
    imag_part = first_pair[1] * second_pair[0] + factor * first_pair[0] * second_pair[1]
    return (real_part, imag_part)


def unpack_fields(spectrum, comp_axis, field_axis):
    collected = []
    for partner_rank in range(spectrum.shape[field_axis]):
        single = lax.index_in_dim(spectrum, partner_rank, field_axis, keepdims=True)
        collected.append(
            (
                lax.index_in_dim(single, 0, comp_axis, keepdims=True),
                lax.index_in_dim(single, 1, comp_axis, keepdims=True),
            )
        )
    return collected


def pack_fields(pairs, comp_axis, field_axis):
    return jnp.concatenate(
        [jnp.concatenate([real_part, imag_part], axis=comp_axis) for real_part, imag_part in pairs],
        axis=field_axis,
    )


def spread_forward(regroup, fields):
    row_count, field_count, channels = fields.shape
    part_count = lax.axis_size("ctx")
    block_rows = row_count // part_count
    length = 2 * part_count * row_count
    my_index = lax.axis_index("ctx")
    gathered = regroup(fields.reshape(part_count, 1, block_rows, field_count, channels))
    cosine, sine_part = phase_pair(2 * part_count, part_count, 2 * part_count, -1.0)
    first_table = jnp.stack([cosine, sine_part], axis=1)
    first_pass = jnp.einsum("kda,arfc->kdrfc", first_table, gathered, precision=HIGHEST_PREC)
    row_index = my_index * block_rows + jnp.arange(block_rows, dtype=jnp.int32)
    twist_index = jnp.arange(2 * part_count, dtype=jnp.int32)[:, None] * row_index[None, :] % length
    phase_angle = -TWO_PI / length * twist_index.astype(jnp.float32)
    cos_twist = jnp.cos(phase_angle)[:, :, None, None]
    sin_twist = jnp.sin(phase_angle)[:, :, None, None]
    real_part, imag_part = rotate_pair(first_pass[:, 0], first_pass[:, 1], cos_twist, sin_twist)
    turned = jnp.stack([real_part, imag_part], axis=1)
    arrived = regroup(turned.reshape(part_count, 1, 2, 2, block_rows, field_count, channels))
    cosine, sine_part = phase_pair(row_count, row_count, row_count, -1.0)
    second_table = jnp.stack(
        [jnp.stack([cosine, sine_part], axis=-1), jnp.stack([-sine_part, cosine], axis=-1)], axis=0
    )
    second_table = second_table.reshape(2, part_count, block_rows, row_count, 2)
    return jnp.einsum("pqsrfc,sprkd->qkdfc", arrived, second_table, precision=HIGHEST_PREC)


def spread_inverse(regroup, spectrum):
    pair_count, row_count, _, field_count, channels = spectrum.shape
    part_count = lax.axis_size("ctx")
    block_rows = row_count // part_count
    length = 2 * part_count * row_count
    my_index = lax.axis_index("ctx")
    cosine, sine_part = phase_pair(row_count, row_count, row_count, 1.0)
    second_table = jnp.stack(
        [jnp.stack([cosine, sine_part], axis=-1), jnp.stack([-sine_part, cosine], axis=-1)], axis=0
    )
    second_table = second_table.reshape(2, row_count, part_count, block_rows, 2)
    row_parts = jnp.einsum("qkdfc,dkprs->pqsrfc", spectrum, second_table, precision=HIGHEST_PREC)
    freq_index = my_index * pair_count + jnp.arange(pair_count, dtype=jnp.int32)
    twist_index = freq_index[:, None] * jnp.arange(row_count, dtype=jnp.int32)[None, :] % length
    phase_angle = TWO_PI / length * twist_index.astype(jnp.float32)
    cos_twist = (
        jnp.cos(phase_angle)
        .reshape(pair_count, part_count, block_rows)
        .transpose(1, 0, 2)[:, :, :, None, None]
    )
    sin_twist = (
        jnp.sin(phase_angle)
        .reshape(pair_count, part_count, block_rows)
        .transpose(1, 0, 2)[:, :, :, None, None]
    )
    real_part, imag_part = rotate_pair(row_parts[:, :, 0], row_parts[:, :, 1], cos_twist, sin_twist)
    turned = jnp.stack([real_part, imag_part], axis=2)
    arrived = regroup(
        turned.reshape(part_count, 1, pair_count, 2, block_rows, field_count, channels)
    )
    cosine, sine_part = phase_pair(2 * part_count, part_count, 2 * part_count, 1.0)
    first_table = (jnp.stack([cosine, -sine_part], axis=1) / length).reshape(
        part_count, pair_count, 2, part_count
    )
    values = jnp.einsum("pqsrfc,pqsa->arfc", arrived, first_table, precision=HIGHEST_PREC)
    returned = regroup(values.reshape(part_count, 1, block_rows, field_count, channels))
    return returned.reshape(row_count, field_count, channels)


def local_general(query_in, key_in, value_in, long_filter, short_taps, out_grad):
    row_count = query_in.shape[0]
    tap_count = short_taps.shape[1]
    margin = tap_count - 1
    part_count = lax.axis_size("ctx")

    def regroup(blocks):
        return lax.all_to_all(blocks, "ctx", split_axis=0, concat_axis=1, tiled=True)[0]

    to_freq = partial(spread_forward, regroup)
    from_freq = partial(spread_inverse, regroup)
    comp_axis = 2
    field_axis = 3
    inputs = jnp.stack([query_in, key_in, value_in])
    earlier = passed_along(inputs[:, row_count - margin :], "ctx", 1)
    extended = jnp.concatenate([earlier, inputs], axis=1).astype(jnp.float32)
    tap_gain = short_taps.astype(jnp.float32)
    filtered = tap_gain[:, 0, None, :] * extended[:, margin:]
    for offset in range(1, tap_count):
        filtered = (
            filtered
            + tap_gain[:, offset, None, :]
            * extended[:, margin - offset : margin - offset + row_count]
        )
    query_filt = filtered[0]
    key_filt = filtered[1]
    value_filt = filtered[2]
    mixed_in = key_filt * value_filt
    spectra = to_freq(jnp.stack([mixed_in, long_filter.astype(jnp.float32)], axis=1))
    mixed_spec, filter_spec = unpack_fields(spectra, comp_axis, field_axis)
    convolved = from_freq(
        pack_fields([times_pair(mixed_spec, filter_spec, False)], comp_axis, field_axis)
    )[:, 0]
    output = (query_filt * convolved).astype(jnp.bfloat16)
    grad_in = out_grad.astype(jnp.float32)
    gate_grad = grad_in * convolved
    conv_grad = grad_in * query_filt
    grad_spec = unpack_fields(to_freq(conv_grad[:, None, :]), comp_axis, field_axis)[0]
    returned = from_freq(
        pack_fields(
            [times_pair(grad_spec, filter_spec, True), times_pair(grad_spec, mixed_spec, True)],
            comp_axis,
            field_axis,
        )
    )
    grad_scale = 1.0 / math.sqrt(part_count * row_count)
    mixed_grad = returned[:, 0]
    filter_grad = returned[:, 1] * grad_scale
    grad_stack = jnp.stack([gate_grad, mixed_grad * value_filt, mixed_grad * key_filt])
    later_rows = passed_along(grad_stack[:, :margin], "ctx", -1)
    padded_grad = jnp.concatenate([grad_stack, later_rows], axis=1)
    input_grads = tap_gain[:, 0, None, :] * grad_stack
    for offset in range(1, tap_count):
        input_grads = (
            input_grads + tap_gain[:, offset, None, :] * padded_grad[:, offset : offset + row_count]
        )
    partial_taps = jnp.stack(
        [
            jnp.sum(grad_stack * extended[:, margin - offset : margin - offset + row_count], axis=1)
            for offset in range(tap_count)
        ],
        axis=1,
    )
    taps_grad = lax.psum(partial_taps, "ctx") * grad_scale
    return (
        output,
        input_grads[0].astype(jnp.bfloat16),
        input_grads[1].astype(jnp.bfloat16),
        input_grads[2].astype(jnp.bfloat16),
        filter_grad,
        taps_grad,
    )


RADIX = 8
FIELDS = 5
CLASSES = (4, 2, 6, 1, 5, 9, 13)
LANES = 128
PAD = 8
CHUNK = 16
PLACES = (0, 6, 2, 5, 3, 7, 4, 1)
EARLY = 4
CURVE = 15.0
REACH = 120.0
SLOPE = 2.0 * REACH / math.log2(1.0 + CURVE)
TINY = 1e-30


def split_pair(values):
    high = values.astype(jnp.bfloat16)
    low = (values - high.astype(jnp.float32)).astype(jnp.bfloat16)
    return high, low


@lru_cache(maxsize=None)
def class_tables(rows):
    length = 2 * RADIX * rows
    back = np.arange(rows)

    def waves(residue, count):
        angle = 2.0 * np.pi * (np.outer(2 * RADIX * np.arange(count) + residue, back) % length) / length
        return np.cos(angle), np.sin(angle)

    half = rows // 2
    cos0, sin0 = waves(0, half)
    cos8, sin8 = waves(RADIX, half)
    none = np.zeros((half, rows))
    middle = (1.0 - 2.0 * (back % 2))[None, :]
    imag0 = np.concatenate([middle, -sin0[1:]])
    first = np.block([[cos0, none], [none, cos8], [imag0, none], [none, -sin8]])
    weight = np.full((2 * rows, 1), 2.0)
    weight[0] = weight[rows] = 1.0
    cosine, sine = waves(0, rows)
    other = np.block([[cosine, sine], [-sine, cosine]])
    tables = []
    for table in (np.stack([first, other]), np.stack([(weight * first).T, 2.0 * other.T]) / length):
        high = table.astype(ml_dtypes.bfloat16)
        low = (table - high.astype(np.float64)).astype(ml_dtypes.bfloat16)
        tables.append(np.stack([high, low]))
    turns = np.zeros((rows, LANES), np.float32)
    for n, residue in enumerate(CLASSES):
        turns[:, 2 * n], turns[:, 2 * n + 1] = [wave[0] for wave in waves(residue, 1)]
    return (*tables, turns)


ROOT = math.sqrt(0.5)
COS1 = math.cos(math.pi / 8)
SIN1 = math.sin(math.pi / 8)


def forward_classes(x):
    u = [x[a] + x[a + 4] for a in range(4)]
    d = [x[a] - x[a + 4] for a in range(4)]
    even, odd = u[0] + u[2], u[1] + u[3]
    dif, tot = ROOT * (d[1] - d[3]), ROOT * (d[1] + d[3])
    found = [
        (even + odd, even - odd),
        (u[0] - u[2], u[3] - u[1]),
        (d[0] + dif, -d[2] - tot),
        (d[0] - dif, d[2] - tot),
    ]
    w0 = (x[0], -x[4])
    w1 = (COS1 * x[1] - SIN1 * x[5], -SIN1 * x[1] - COS1 * x[5])
    w2 = (ROOT * (x[2] - x[6]), -ROOT * (x[2] + x[6]))
    w3 = (SIN1 * x[3] - COS1 * x[7], -COS1 * x[3] - SIN1 * x[7])
    s02 = (w0[0] + w2[0], w0[1] + w2[1])
    d02 = (w0[0] - w2[0], w0[1] - w2[1])
    s13 = (w1[0] + w3[0], w1[1] + w3[1])
    d13 = (w1[0] - w3[0], w1[1] - w3[1])
    found.append((s02[0] + s13[0], s02[1] + s13[1]))
    found.append((d02[0] + d13[1], d02[1] - d13[0]))
    found.append((s02[0] - s13[0], s02[1] - s13[1]))
    found.append((d02[0] - d13[1], d02[1] + d13[0]))
    return found


def inverse_classes(z):
    (z0, z8), (r4, i4), (r2, i2), (r6, i6) = z[:4]
    up, down = z0 + z8, z0 - z8
    even = [up + r4, down - i4, up - r4, down + i4]
    gap, tot = ROOT * (r2 - r6), ROOT * (i2 + i6)
    turn = [r2 + r6, gap - tot, i6 - i2, -gap - tot]
    (r1, i1), (r5, i5), (r9, i9), (rd, id_) = z[4:]
    s = (r1 + r9, i1 + i9)
    d = (r1 - r9, i1 - i9)
    t = (r5 + rd, i5 + id_)
    e = (r5 - rd, i5 - id_)
    s0 = (s[0] + t[0], s[1] + t[1])
    s2 = (s[0] - t[0], s[1] - t[1])
    s1 = (d[0] - e[1], d[1] + e[0])
    s3 = (d[0] + e[1], d[1] - e[0])
    q = [
        s0,
        (COS1 * s1[0] - SIN1 * s1[1], SIN1 * s1[0] + COS1 * s1[1]),
        (ROOT * (s2[0] - s2[1]), ROOT * (s2[0] + s2[1])),
        (SIN1 * s3[0] - COS1 * s3[1], COS1 * s3[0] + SIN1 * s3[1]),
    ]
    return [even[a] + turn[a] + q[a][0] for a in range(4)] + [
        even[a] - turn[a] - q[a][1] for a in range(4)
    ]


def log_code(values, inverse_scale):
    share = 1.0 + CURVE * (jnp.abs(values) * inverse_scale)
    code = jnp.exp2(jnp.log2(share) * SLOPE - REACH)
    return jnp.where(values < 0.0, -code, code).astype(jnp.bfloat16)


def log_decode(code, scale):
    code = code.astype(jnp.float32)
    share = jnp.exp2((jnp.log2(jnp.abs(code)) + REACH) * (1.0 / SLOPE)) - 1.0
    values = share * (scale * (1.0 / CURVE))
    return jnp.where(code < 0.0, -values, values)


def table_dot(table_ref, f, both):
    half = both.shape[1] // 2
    which = min(f, 1)
    found = jnp.dot(table_ref[0, which], both, preferred_element_type=jnp.float32)
    rest = jnp.dot(table_ref[1, which], both[:, :half], preferred_element_type=jnp.float32)
    return found[:, :half] + (found[:, half:] + rest)


def times_spec(first, second, conj_second, packed):
    (ar, ai), (br, bi) = first, second
    inner = ai * bi
    cross = ai * br - ar * bi if conj_second else ai * br + ar * bi
    if packed:
        line = lax.broadcasted_iota(jnp.int32, inner.shape, 0) == 0
        cross = jnp.where(line, inner, cross)
        inner = jnp.where(line, 0.0, inner)
    return (ar * br + inner if conj_second else ar * br - inner), cross


def spec_parts(spec, rows, column):
    lanes = slice(column * LANES, (column + 1) * LANES)
    return spec[:rows, lanes], spec[rows:, lanes]


def side_by_side(products):
    pairs = [split_pair(jnp.concatenate(pair, axis=0)) for pair in products]
    return jnp.concatenate([high for high, _ in pairs] + [low for _, low in pairs], axis=1)


def put_classes(ref, column, columns, rows, b0, values, turn):
    for f, pair in enumerate(forward_classes(values)):
        if f > 0:
            cosine, sine = [turn[2 * f - 2 + n, pl.ds(b0, CHUNK), :] for n in range(2)]
            pair = (pair[0] * cosine + pair[1] * sine, pair[1] * cosine - pair[0] * sine)
        for part, value in enumerate(pair):
            high, low = split_pair(value)
            at = pl.ds(part * rows + b0, CHUNK)
            ref[f, at, pl.ds(column * LANES, LANES)] = high
            ref[f, at, pl.ds((columns + column) * LANES, LANES)] = low


def take_classes(ref, column, rows, b0, turn):
    lanes = pl.ds(column * LANES, LANES)
    found = []
    for f in range(ref.shape[0]):
        pair = ref[f, pl.ds(b0, CHUNK), lanes], ref[f, pl.ds(rows + b0, CHUNK), lanes]
        if f > 0:
            cosine, sine = [turn[2 * f - 2 + n, pl.ds(b0, CHUNK), :] for n in range(2)]
            pair = (pair[0] * cosine - pair[1] * sine, pair[1] * cosine + pair[0] * sine)
        found.append(pair)
    return inverse_classes(found)


def short_filter(gain, ref, at):
    return (
        gain[0] * ref[pl.ds(at, CHUNK), :]
        + gain[1] * ref[pl.ds(at - 1, CHUNK), :]
        + gain[2] * ref[pl.ds(at - 2, CHUNK), :]
    )


def widen(me_ref, got, targets, rows):
    def body(step, carry):
        b0 = pl.multiple_of(step * CHUNK, CHUNK)
        for k, ref in zip(PLACES, got):
            at = pl.multiple_of((me_ref[0] ^ k) * rows + b0, CHUNK)
            for field, (target, pad) in enumerate(targets):
                target[pl.ds(pad + at, CHUNK), :] = ref[pl.ds(field * rows + b0, CHUNK), :].astype(
                    jnp.float32
                )
        return carry

    lax.fori_loop(0, rows // CHUNK, body, 0)


def gains(taps_ref):
    return [[taps_ref[3 * i + j : 3 * i + j + 1, :] for j in range(3)] for i in range(3)]


def layer_kernel(me_ref, gain_ref, turn, forward_ref, inverse_ref, *refs):
    got, outs = refs[:RADIX], refs[RADIX : 2 * RADIX]
    qp, kp, vp, hs, cot, ks, vs, xs, zs, conv, mgrad, fgrad, peak, sums, head = refs[2 * RADIX :]
    rows = got[0].shape[0] // FIELDS
    total = RADIX * rows
    f32 = jnp.float32
    gain = gains(gain_ref)
    for ref in (qp, kp, vp):
        ref[pl.ds(0, PAD), :] = jnp.zeros((PAD, LANES), f32)
    for ref in (cot, ks, vs, conv, mgrad):
        ref[pl.ds(total, PAD), :] = jnp.zeros((PAD, LANES), f32)
    widen(me_ref, got, ((qp, PAD), (kp, PAD), (vp, PAD), (hs, 0), (cot, 0)), rows)

    def enter(step, carry):
        b0 = pl.multiple_of(step * CHUNK, CHUNK)
        mixed = []
        for a in range(RADIX):
            at = a * rows + b0
            key_filt = short_filter(gain[1], kp, PAD + at)
            value_filt = short_filter(gain[2], vp, PAD + at)
            ks[pl.ds(at, CHUNK), :] = key_filt
            vs[pl.ds(at, CHUNK), :] = value_filt
            mixed.append(key_filt * value_filt)
        put_classes(xs, 0, 3, rows, b0, mixed, turn)
        filt = [hs[pl.ds(a * rows + b0, CHUNK), :] for a in range(RADIX)]
        put_classes(xs, 1, 3, rows, b0, filt, turn)
        conv_grad = []
        for a in range(RADIX):
            at = a * rows + b0
            conv_grad.append(short_filter(gain[0], qp, PAD + at) * cot[pl.ds(at, CHUNK), :])
        put_classes(xs, 2, 3, rows, b0, conv_grad, turn)
        return carry

    lax.fori_loop(0, rows // CHUNK, enter, 0)
    for f in range(xs.shape[0]):
        zs[f] = table_dot(forward_ref, f, xs[f])
    for f in range(xs.shape[0]):
        mixed, filt, grad = [spec_parts(zs[f], rows, c) for c in range(3)]
        products = [
            times_spec(mixed, filt, False, f == 0),
            times_spec(grad, filt, True, f == 0),
            times_spec(grad, mixed, True, f == 0),
        ]
        xs[f] = side_by_side(products)
    for f in range(xs.shape[0]):
        zs[f] = table_dot(inverse_ref, f, xs[f])
    peak[...] = jnp.zeros_like(peak)
    sums[...] = jnp.zeros_like(sums)

    def leave(step, carry):
        b0 = pl.multiple_of(step * CHUNK, CHUNK)

        def take(column, ref):
            found = take_classes(zs, column, rows, b0, turn)
            for a, value in enumerate(found):
                ref[pl.ds(a * rows + b0, CHUNK), :] = value
                size = jnp.abs(value)
                peak[column, a] = jnp.maximum(peak[column, a], jnp.maximum(size[:8], size[8:]))
            return found

        def add(i, source, values, other):
            found = [jnp.zeros((CHUNK, LANES), f32)] * 3
            for a, value in enumerate(values):
                at = a * rows + b0
                now = value * other[pl.ds(at, CHUNK), :]
                for j in range(3):
                    found[j] = found[j] + now * source[pl.ds(PAD + at - j, CHUNK), :]
            for j in range(3):
                sums[3 * i + j] += found[j][:8] + found[j][8:]

        add(0, qp, take(0, conv), cot)
        found = take(1, mgrad)
        add(1, kp, found, vs)
        add(2, vp, found, ks)
        take(2, fgrad)
        return carry

    lax.fori_loop(0, rows // CHUNK, leave, 0)
    grad_scale = 1.0 / math.sqrt(total)
    head[...] = jnp.zeros_like(head)
    for n in range(9):
        at = 32 + n if n < 8 else 22
        head[pl.ds(at, 1), :] = jnp.sum(sums[n], axis=0, keepdims=True) * grad_scale
    head[pl.ds(40, 8), :] = split_pair(head[pl.ds(32, 8), :])[1].astype(f32)
    for k, out_ref in zip(PLACES, outs):
        a = me_ref[0] ^ k
        first = pl.multiple_of(a * rows, rows)
        after = first + rows
        for i, ref in enumerate((qp, kp, vp)):
            head[pl.ds(2 * i, 2), :] = ref[pl.ds(first + PAD - 2, 2), :]
        for column, ref in enumerate((conv, mgrad, fgrad)):
            top = jnp.max(peak[column, a], axis=0, keepdims=True)
            scale = jnp.maximum(top * (1.0 + 2.0**-7), TINY).astype(jnp.bfloat16).astype(f32)
            head[pl.ds(6 + column, 1), :] = scale
            out_ref[pl.ds(column * rows, rows), :] = log_code(
                ref[pl.ds(first, rows), :], 1.0 / scale
            )
        for i, (ref, other) in enumerate(((conv, cot), (mgrad, vs), (mgrad, ks))):
            head[pl.ds(16 + 2 * i, 2), :] = ref[pl.ds(after, 2), :] * other[pl.ds(after, 2), :]
        head[pl.ds(24, 8), :] = split_pair(head[pl.ds(16, 8), :])[1].astype(f32)
        out_ref[pl.ds(3 * rows, 48), :] = head[...].astype(jnp.bfloat16)


def prepare_kernel(
    me_ref, turns_ref, forward_any, inverse_any, taps_any, _, query_ref, key_ref, value_ref, cot_ref,
    turn, forward_ref, inverse_ref, gain_ref, wide_ref, early_ref, wide,
):
    lane = pl.ds(pl.multiple_of(me_ref[0] * LANES, LANES), LANES)
    forward_ref[...] = forward_any[...]
    inverse_ref[...] = inverse_any[...]
    for n in range(turn.shape[0]):
        turn[n] = jnp.broadcast_to(turns_ref[:, n : n + 1], turn.shape[1:])
    for i in range(3):
        for j in range(3):
            at = 3 * i + j
            wide_ref[at : at + 1, :] = taps_any[i, j : j + 1, :].astype(jnp.float32)
            gain_ref[at : at + 1, :] = taps_any[i, j : j + 1, lane].astype(jnp.float32)
    rows = cot_ref.shape[0]
    for i, ref in enumerate((query_ref, key_ref, value_ref)):
        wide[pl.ds(0, PAD), :] = jnp.zeros((PAD, wide.shape[1]), jnp.float32)
        wide[pl.ds(PAD, rows), :] = ref[...].astype(jnp.float32)
        early_ref[i] = (
            wide_ref[3 * i : 3 * i + 1, :] * wide[pl.ds(PAD, rows), :]
            + wide_ref[3 * i + 1 : 3 * i + 2, :] * wide[pl.ds(PAD - 1, rows), :]
            + wide_ref[3 * i + 2 : 3 * i + 3, :] * wide[pl.ds(PAD - 2, rows), :]
        )
    early_ref[3] = cot_ref[...].astype(jnp.float32)


def whole_vmem(count):
    return [pl.BlockSpec(memory_space=pltpu.VMEM)] * count


def whole_any(count):
    return [pl.BlockSpec(memory_space=pl.ANY)] * count


IN_SMEM = pl.BlockSpec(memory_space=pltpu.SMEM)


def pack_kernel(places, me_ref, *refs):
    sources, outs, land, sem = refs[:FIELDS], refs[FIELDS:-2], refs[-2], refs[-1]
    rows = sources[0].shape[0]
    copies = [
        pltpu.make_async_copy(source, land.at[field], sem.at[field])
        for field, source in enumerate(sources)
    ]
    for copy in copies:
        copy.start()
    for field, copy in enumerate(copies):
        copy.wait()
        for k, out_ref in zip(places, outs):
            lane = pl.multiple_of((me_ref[0] ^ k) * LANES, LANES)
            out_ref[pl.ds(field * rows, rows), :] = land[field, :, pl.ds(lane, LANES)]


def finish_blocks(me_ref, places, got, wide_ref, early_ref, outs, grads, stage, stage_filter, sem):
    rows = early_ref.shape[1]
    f32, bf16 = jnp.float32, jnp.bfloat16
    copies = []
    for n, (k, got_ref) in enumerate(zip(places, got)):
        lanes = pl.ds(pl.multiple_of((me_ref[0] ^ k) * LANES, LANES), LANES)
        head = got_ref[pl.ds(3 * rows, 48), :].astype(f32)
        conv, mixed_grad, filt = [
            log_decode(got_ref[pl.ds(c * rows, rows), :], head[6 + c : 7 + c]) for c in range(3)
        ]
        stage_filter[n] = filt * (1.0 / math.sqrt(RADIX * rows))
        pairs = head[16:24] + head[24:32]
        line = lax.broadcasted_iota(jnp.int32, (PAD, LANES), 0)
        filtered = []
        gain = []
        for i in range(3):
            gain.append([wide_ref[3 * i + j : 3 * i + j + 1, lanes] for j in range(3)])
            before, last = head[2 * i : 2 * i + 1], head[2 * i + 1 : 2 * i + 2]
            top = early_ref[i, 0:PAD, lanes] + jnp.where(
                line == 0,
                gain[i][1] * last + gain[i][2] * before,
                jnp.where(line == 1, gain[i][2] * last, 0.0),
            )
            filtered.append(jnp.concatenate([top, early_ref[i, PAD:, lanes]], axis=0))
        stage[n, 0] = (filtered[0] * conv).astype(bf16)
        inner = (
            conv * early_ref[3, :, lanes],
            mixed_grad * filtered[2],
            mixed_grad * filtered[1],
        )
        for i in range(3):
            grads[i, pl.ds(0, rows), :] = inner[i]
            grads[i, pl.ds(rows, 2), :] = pairs[2 * i : 2 * i + 2]
            stage[n, 1 + i] = (
                gain[i][0] * inner[i]
                + gain[i][1] * grads[i, pl.ds(1, rows), :]
                + gain[i][2] * grads[i, pl.ds(2, rows), :]
            ).astype(bf16)
        for c, out in enumerate(outs):
            source = stage.at[n, c] if c < 4 else stage_filter.at[n]
            copies.append(pltpu.make_async_copy(source, out.at[:, lanes], sem.at[len(copies)]))
            copies[-1].start()
    return copies


def finish_kernel(me_ref, *refs):
    got, (wide_ref, early_ref), outs, scratch = refs[:EARLY], refs[EARLY : EARLY + 2], refs[EARLY + 2 : EARLY + 7], refs[EARLY + 7 :]
    for copy in finish_blocks(me_ref, PLACES[:EARLY], got, wide_ref, early_ref, outs, *scratch):
        copy.wait()


def finish_last_kernel(me_ref, *refs):
    got, (wide_ref, early_ref), outs, taps_grad, scratch = (
        refs[:RADIX],
        refs[RADIX : RADIX + 2],
        refs[RADIX + 7 : RADIX + 12],
        refs[RADIX + 12],
        refs[RADIX + 13 :],
    )
    rows = early_ref.shape[1]
    copies = finish_blocks(
        me_ref, PLACES[EARLY:], got[EARLY:], wide_ref, early_ref, outs, *scratch
    )
    for k, got_ref in zip(PLACES, got):
        lanes = pl.ds(pl.multiple_of((me_ref[0] ^ k) * LANES, LANES), LANES)
        head = got_ref[pl.ds(3 * rows, 48), :].astype(jnp.float32)
        taps = head[32:40] + head[40:48]
        for n in range(8):
            taps_grad[n // 3, n % 3 : n % 3 + 1, lanes] = taps[n : n + 1]
        taps_grad[2, 2:3, lanes] = head[22:23] + head[30:31]
    for copy in copies:
        copy.wait()


def swap_blocks(blocks):
    devices = range(RADIX)
    return [
        lax.ppermute(block, "ctx", [(i, i ^ k) for i in devices]) if k else block
        for k, block in zip(PLACES, blocks)
    ]


def held(arrays, space):
    return [pltpu.with_memory_space_constraint(jnp.asarray(one), space) for one in arrays]


def local_fast(query_in, key_in, value_in, long_filter, short_taps, out_grad):
    rows, channels = query_in.shape
    total = RADIX * rows
    f32, bf16 = jnp.float32, jnp.bfloat16
    shape = jax.ShapeDtypeStruct
    inputs = held((query_in, key_in, value_in, out_grad), pltpu.HBM)
    small = pltpu.CompilerParams(vmem_limit_bytes=12 * 1024 * 1024)
    me = lax.axis_index("ctx").astype(jnp.int32).reshape(1)
    sources = held((query_in, key_in, value_in, long_filter, out_grad), pltpu.HBM)

    def pack(places):
        return pl.pallas_call(
            partial(pack_kernel, places),
            out_shape=[pltpu.VMEM((FIELDS * rows, LANES), bf16)] * len(places),
            in_specs=[IN_SMEM] + whole_any(FIELDS),
            out_specs=whole_vmem(len(places)),
            scratch_shapes=[
                pltpu.VMEM((FIELDS, rows, channels), bf16),
                pltpu.SemaphoreType.DMA((FIELDS,)),
            ],
            compiler_params=small,
            name="pack",
        )(me, *sources)

    packed = pack(PLACES)
    got = swap_blocks(packed)
    forward, inverse, turns = class_tables(rows)
    count = 1 + len(CLASSES)
    ready = pl.pallas_call(
        prepare_kernel,
        out_shape=[
            pltpu.VMEM((2 * len(CLASSES), rows, LANES), f32),
            pltpu.VMEM(forward.shape, bf16),
            pltpu.VMEM(inverse.shape, bf16),
            pltpu.VMEM((16, LANES), f32),
            pltpu.VMEM((16, channels), f32),
            pltpu.VMEM((4, rows, channels), f32),
        ],
        in_specs=[IN_SMEM] + whole_vmem(9),
        out_specs=whole_vmem(6),
        scratch_shapes=[pltpu.VMEM((PAD + rows, channels), f32)],
        compiler_params=small,
        name="prepare",
    )(me, *held((turns, forward, inverse), pltpu.HBM), short_taps, *held(got[1:2], pltpu.VMEM), *inputs)
    ready = held(ready, pltpu.VMEM)
    done = pl.pallas_call(
        layer_kernel,
        out_shape=[pltpu.VMEM((3 * rows + 48, LANES), bf16)] * RADIX,
        in_specs=[IN_SMEM] + whole_vmem(4 + RADIX),
        out_specs=whole_vmem(RADIX),
        scratch_shapes=[pltpu.VMEM((total + PAD, LANES), f32)] * 7
        + [
            pltpu.VMEM((count, 2 * rows, 6 * LANES), bf16),
            pltpu.VMEM((count, 2 * rows, 3 * LANES), f32),
        ]
        + [pltpu.VMEM((total + PAD, LANES), f32)] * 3
        + [
            pltpu.VMEM((3, RADIX, 8, LANES), f32),
            pltpu.VMEM((9, 8, LANES), f32),
            pltpu.VMEM((48, LANES), f32),
        ],
        compiler_params=pltpu.CompilerParams(vmem_limit_bytes=20 * 1024 * 1024),
        name="layer",
    )(me, ready[3], *ready[:3], *held(got, pltpu.VMEM))
    back = held(swap_blocks(done), pltpu.VMEM)
    results = [shape((rows, channels), bf16)] * 4 + [shape((rows, channels), f32)]

    def finish_scratch(count):
        return [
            pltpu.VMEM((3, rows + PAD, LANES), f32),
            pltpu.VMEM((count, 4, rows, LANES), bf16),
            pltpu.VMEM((count, rows, LANES), f32),
            pltpu.SemaphoreType.DMA((5 * count,)),
        ]

    begun = pl.pallas_call(
        finish_kernel,
        out_shape=results,
        in_specs=[IN_SMEM] + whole_vmem(EARLY + 2),
        out_specs=whole_any(5),
        scratch_shapes=finish_scratch(EARLY),
        compiler_params=small,
        name="finish",
    )(me, *back[:EARLY], *ready[4:])
    return tuple(
        pl.pallas_call(
            finish_last_kernel,
            out_shape=results + [shape((3, 3, channels), f32)],
            in_specs=[IN_SMEM] + whole_vmem(RADIX + 2) + whole_any(5),
            out_specs=whole_any(5) + whole_vmem(1),
            scratch_shapes=finish_scratch(RADIX - EARLY),
            input_output_aliases={RADIX + 3 + n: n for n in range(5)},
            compiler_params=small,
            name="finish_last",
        )(me, *back, *ready[4:], *begun)
    )


def local(query_in, key_in, value_in, long_filter, short_taps, out_grad):
    rows, channels = query_in.shape
    blocks = lax.axis_size("ctx")
    taps = short_taps.shape[:2]
    if blocks == RADIX and channels == blocks * LANES and rows == LANES and taps == (3, 3):
        return local_fast(query_in, key_in, value_in, long_filter, short_taps, out_grad)
    return local_general(query_in, key_in, value_in, long_filter, short_taps, out_grad)


def solution(mesh):
    placed = (
        P("ctx", "tp"),
        P("ctx", "tp"),
        P("ctx", "tp"),
        P("ctx", "tp"),
        P(None, None, "tp"),
        P("ctx", "tp"),
    )
    return jax.shard_map(
        local,
        mesh=mesh,
        in_specs=placed,
        out_specs=(
            P("ctx", "tp"),
            P("ctx", "tp"),
            P("ctx", "tp"),
            P("ctx", "tp"),
            P("ctx", "tp"),
            P(None, None, "tp"),
        ),
        check_vma=False,
    )
```

```python
from functools import lru_cache, partial
import math

import jax
import jax.numpy as jnp
import ml_dtypes
import numpy as np
from jax import lax
from jax.experimental import pallas as pl
from jax.experimental.pallas import tpu as pltpu
from jax.sharding import PartitionSpec as P

HIGHEST_PREC = lax.Precision.HIGHEST
TWO_PI = 2.0 * math.pi


def passed_along(block, axis, distance):
    devices = range(lax.axis_size(axis))
    route = [(i - distance, i) for i in devices if i - distance in devices]
    return lax.ppermute(block, axis, route)


def phase_pair(count_a, count_b, period, direction):
    product = (
        jnp.arange(count_a, dtype=jnp.int32)[:, None]
        * jnp.arange(count_b, dtype=jnp.int32)[None, :]
    )
    phase_angle = direction * TWO_PI / period * (product % period).astype(jnp.float32)
    return (jnp.cos(phase_angle), jnp.sin(phase_angle))


def rotate_pair(real_part, imag_part, cosine, sine_part):
    return (real_part * cosine - imag_part * sine_part, real_part * sine_part + imag_part * cosine)


def times_pair(first_pair, second_pair, conj_second):
    factor = -1.0 if conj_second else 1.0
    real_part = first_pair[0] * second_pair[0] - factor * first_pair[1] * second_pair[1]
    imag_part = first_pair[1] * second_pair[0] + factor * first_pair[0] * second_pair[1]
    return (real_part, imag_part)


def unpack_fields(spectrum, comp_axis, field_axis):
    collected = []
    for partner_rank in range(spectrum.shape[field_axis]):
        single = lax.index_in_dim(spectrum, partner_rank, field_axis, keepdims=True)
        collected.append(
            (
                lax.index_in_dim(single, 0, comp_axis, keepdims=True),
                lax.index_in_dim(single, 1, comp_axis, keepdims=True),
            )
        )
    return collected


def pack_fields(pairs, comp_axis, field_axis):
    return jnp.concatenate(
        [jnp.concatenate([real_part, imag_part], axis=comp_axis) for real_part, imag_part in pairs],
        axis=field_axis,
    )


def spread_forward(regroup, fields):
    row_count, field_count, channels = fields.shape
    part_count = lax.axis_size("ctx")
    block_rows = row_count // part_count
    length = 2 * part_count * row_count
    my_index = lax.axis_index("ctx")
    gathered = regroup(fields.reshape(part_count, 1, block_rows, field_count, channels))
    cosine, sine_part = phase_pair(2 * part_count, part_count, 2 * part_count, -1.0)
    first_table = jnp.stack([cosine, sine_part], axis=1)
    first_pass = jnp.einsum("kda,arfc->kdrfc", first_table, gathered, precision=HIGHEST_PREC)
    row_index = my_index * block_rows + jnp.arange(block_rows, dtype=jnp.int32)
    twist_index = jnp.arange(2 * part_count, dtype=jnp.int32)[:, None] * row_index[None, :] % length
    phase_angle = -TWO_PI / length * twist_index.astype(jnp.float32)
    cos_twist = jnp.cos(phase_angle)[:, :, None, None]
    sin_twist = jnp.sin(phase_angle)[:, :, None, None]
    real_part, imag_part = rotate_pair(first_pass[:, 0], first_pass[:, 1], cos_twist, sin_twist)
    turned = jnp.stack([real_part, imag_part], axis=1)
    arrived = regroup(turned.reshape(part_count, 1, 2, 2, block_rows, field_count, channels))
    cosine, sine_part = phase_pair(row_count, row_count, row_count, -1.0)
    second_table = jnp.stack(
        [jnp.stack([cosine, sine_part], axis=-1), jnp.stack([-sine_part, cosine], axis=-1)], axis=0
    )
    second_table = second_table.reshape(2, part_count, block_rows, row_count, 2)
    return jnp.einsum("pqsrfc,sprkd->qkdfc", arrived, second_table, precision=HIGHEST_PREC)


def spread_inverse(regroup, spectrum):
    pair_count, row_count, _, field_count, channels = spectrum.shape
    part_count = lax.axis_size("ctx")
    block_rows = row_count // part_count
    length = 2 * part_count * row_count
    my_index = lax.axis_index("ctx")
    cosine, sine_part = phase_pair(row_count, row_count, row_count, 1.0)
    second_table = jnp.stack(
        [jnp.stack([cosine, sine_part], axis=-1), jnp.stack([-sine_part, cosine], axis=-1)], axis=0
    )
    second_table = second_table.reshape(2, row_count, part_count, block_rows, 2)
    row_parts = jnp.einsum("qkdfc,dkprs->pqsrfc", spectrum, second_table, precision=HIGHEST_PREC)
    freq_index = my_index * pair_count + jnp.arange(pair_count, dtype=jnp.int32)
    twist_index = freq_index[:, None] * jnp.arange(row_count, dtype=jnp.int32)[None, :] % length
    phase_angle = TWO_PI / length * twist_index.astype(jnp.float32)
    cos_twist = (
        jnp.cos(phase_angle)
        .reshape(pair_count, part_count, block_rows)
        .transpose(1, 0, 2)[:, :, :, None, None]
    )
    sin_twist = (
        jnp.sin(phase_angle)
        .reshape(pair_count, part_count, block_rows)
        .transpose(1, 0, 2)[:, :, :, None, None]
    )
    real_part, imag_part = rotate_pair(row_parts[:, :, 0], row_parts[:, :, 1], cos_twist, sin_twist)
    turned = jnp.stack([real_part, imag_part], axis=2)
    arrived = regroup(
        turned.reshape(part_count, 1, pair_count, 2, block_rows, field_count, channels)
    )
    cosine, sine_part = phase_pair(2 * part_count, part_count, 2 * part_count, 1.0)
    first_table = (jnp.stack([cosine, -sine_part], axis=1) / length).reshape(
        part_count, pair_count, 2, part_count
    )
    values = jnp.einsum("pqsrfc,pqsa->arfc", arrived, first_table, precision=HIGHEST_PREC)
    returned = regroup(values.reshape(part_count, 1, block_rows, field_count, channels))
    return returned.reshape(row_count, field_count, channels)


def local_general(query_in, key_in, value_in, long_filter, short_taps, out_grad):
    row_count = query_in.shape[0]
    tap_count = short_taps.shape[1]
    margin = tap_count - 1
    part_count = lax.axis_size("ctx")

    def regroup(blocks):
        return lax.all_to_all(blocks, "ctx", split_axis=0, concat_axis=1, tiled=True)[0]

    to_freq = partial(spread_forward, regroup)
    from_freq = partial(spread_inverse, regroup)
    comp_axis = 2
    field_axis = 3
    inputs = jnp.stack([query_in, key_in, value_in])
    earlier = passed_along(inputs[:, row_count - margin :], "ctx", 1)
    extended = jnp.concatenate([earlier, inputs], axis=1).astype(jnp.float32)
    tap_gain = short_taps.astype(jnp.float32)
    filtered = tap_gain[:, 0, None, :] * extended[:, margin:]
    for offset in range(1, tap_count):
        filtered = (
            filtered
            + tap_gain[:, offset, None, :]
            * extended[:, margin - offset : margin - offset + row_count]
        )
    query_filt = filtered[0]
    key_filt = filtered[1]
    value_filt = filtered[2]
    mixed_in = key_filt * value_filt
    spectra = to_freq(jnp.stack([mixed_in, long_filter.astype(jnp.float32)], axis=1))
    mixed_spec, filter_spec = unpack_fields(spectra, comp_axis, field_axis)
    convolved = from_freq(
        pack_fields([times_pair(mixed_spec, filter_spec, False)], comp_axis, field_axis)
    )[:, 0]
    output = (query_filt * convolved).astype(jnp.bfloat16)
    grad_in = out_grad.astype(jnp.float32)
    gate_grad = grad_in * convolved
    conv_grad = grad_in * query_filt
    grad_spec = unpack_fields(to_freq(conv_grad[:, None, :]), comp_axis, field_axis)[0]
    returned = from_freq(
        pack_fields(
            [times_pair(grad_spec, filter_spec, True), times_pair(grad_spec, mixed_spec, True)],
            comp_axis,
            field_axis,
        )
    )
    grad_scale = 1.0 / math.sqrt(part_count * row_count)
    mixed_grad = returned[:, 0]
    filter_grad = returned[:, 1] * grad_scale
    grad_stack = jnp.stack([gate_grad, mixed_grad * value_filt, mixed_grad * key_filt])
    later_rows = passed_along(grad_stack[:, :margin], "ctx", -1)
    padded_grad = jnp.concatenate([grad_stack, later_rows], axis=1)
    input_grads = tap_gain[:, 0, None, :] * grad_stack
    for offset in range(1, tap_count):
        input_grads = (
            input_grads + tap_gain[:, offset, None, :] * padded_grad[:, offset : offset + row_count]
        )
    partial_taps = jnp.stack(
        [
            jnp.sum(grad_stack * extended[:, margin - offset : margin - offset + row_count], axis=1)
            for offset in range(tap_count)
        ],
        axis=1,
    )
    taps_grad = lax.psum(partial_taps, "ctx") * grad_scale
    return (
        output,
        input_grads[0].astype(jnp.bfloat16),
        input_grads[1].astype(jnp.bfloat16),
        input_grads[2].astype(jnp.bfloat16),
        filter_grad,
        taps_grad,
    )


RADIX = 8
FIELDS = 5
CLASSES = (4, 2, 6, 1, 5, 9, 13)
LANES = 128
PAD = 8
CHUNK = 16
SENT = (0, 6, 2, 5, 3, 4, 7, 1)
BACK = (0, 6, 2, 5, 3, 4, 7, 1)
FINISHED = (0, 4, 6, 8)
CURVE = 15.0
REACH = 120.0
SLOPE = 2.0 * REACH / math.log2(1.0 + CURVE)
TINY = 1e-30


def split_pair(values):
    high = values.astype(jnp.bfloat16)
    low = (values - high.astype(jnp.float32)).astype(jnp.bfloat16)
    return high, low


@lru_cache(maxsize=None)
def class_tables(rows):
    length = 2 * RADIX * rows
    back = np.arange(rows)

    def waves(residue, count):
        angle = 2.0 * np.pi * (np.outer(2 * RADIX * np.arange(count) + residue, back) % length) / length
        return np.cos(angle), np.sin(angle)

    half = rows // 2
    cos0, sin0 = waves(0, half)
    cos8, sin8 = waves(RADIX, half)
    none = np.zeros((half, rows))
    middle = (1.0 - 2.0 * (back % 2))[None, :]
    imag0 = np.concatenate([middle, -sin0[1:]])
    first = np.block([[cos0, none], [none, cos8], [imag0, none], [none, -sin8]])
    weight = np.full((2 * rows, 1), 2.0)
    weight[0] = weight[rows] = 1.0
    cosine, sine = waves(0, rows)
    other = np.block([[cosine, sine], [-sine, cosine]])
    tables = []
    for table in (np.stack([first, other]), np.stack([(weight * first).T, 2.0 * other.T]) / length):
        high = table.astype(ml_dtypes.bfloat16)
        low = (table - high.astype(np.float64)).astype(ml_dtypes.bfloat16)
        tables.append(np.stack([high, low]))
    turns = np.zeros((rows, LANES), np.float32)
    for n, residue in enumerate(CLASSES):
        turns[:, 2 * n], turns[:, 2 * n + 1] = [wave[0] for wave in waves(residue, 1)]
    return (*tables, turns)


ROOT = math.sqrt(0.5)
COS1 = math.cos(math.pi / 8)
SIN1 = math.sin(math.pi / 8)


def forward_classes(x):
    u = [x[a] + x[a + 4] for a in range(4)]
    d = [x[a] - x[a + 4] for a in range(4)]
    even, odd = u[0] + u[2], u[1] + u[3]
    dif, tot = ROOT * (d[1] - d[3]), ROOT * (d[1] + d[3])
    found = [
        (even + odd, even - odd),
        (u[0] - u[2], u[3] - u[1]),
        (d[0] + dif, -d[2] - tot),
        (d[0] - dif, d[2] - tot),
    ]
    w0 = (x[0], -x[4])
    w1 = (COS1 * x[1] - SIN1 * x[5], -SIN1 * x[1] - COS1 * x[5])
    w2 = (ROOT * (x[2] - x[6]), -ROOT * (x[2] + x[6]))
    w3 = (SIN1 * x[3] - COS1 * x[7], -COS1 * x[3] - SIN1 * x[7])
    s02 = (w0[0] + w2[0], w0[1] + w2[1])
    d02 = (w0[0] - w2[0], w0[1] - w2[1])
    s13 = (w1[0] + w3[0], w1[1] + w3[1])
    d13 = (w1[0] - w3[0], w1[1] - w3[1])
    found.append((s02[0] + s13[0], s02[1] + s13[1]))
    found.append((d02[0] + d13[1], d02[1] - d13[0]))
    found.append((s02[0] - s13[0], s02[1] - s13[1]))
    found.append((d02[0] - d13[1], d02[1] + d13[0]))
    return found


def inverse_classes(z):
    (z0, z8), (r4, i4), (r2, i2), (r6, i6) = z[:4]
    up, down = z0 + z8, z0 - z8
    even = [up + r4, down - i4, up - r4, down + i4]
    gap, tot = ROOT * (r2 - r6), ROOT * (i2 + i6)
    turn = [r2 + r6, gap - tot, i6 - i2, -gap - tot]
    (r1, i1), (r5, i5), (r9, i9), (rd, id_) = z[4:]
    s = (r1 + r9, i1 + i9)
    d = (r1 - r9, i1 - i9)
    t = (r5 + rd, i5 + id_)
    e = (r5 - rd, i5 - id_)
    s0 = (s[0] + t[0], s[1] + t[1])
    s2 = (s[0] - t[0], s[1] - t[1])
    s1 = (d[0] - e[1], d[1] + e[0])
    s3 = (d[0] + e[1], d[1] - e[0])
    q = [
        s0,
        (COS1 * s1[0] - SIN1 * s1[1], SIN1 * s1[0] + COS1 * s1[1]),
        (ROOT * (s2[0] - s2[1]), ROOT * (s2[0] + s2[1])),
        (SIN1 * s3[0] - COS1 * s3[1], COS1 * s3[0] + SIN1 * s3[1]),
    ]
    return [even[a] + turn[a] + q[a][0] for a in range(4)] + [
        even[a] - turn[a] - q[a][1] for a in range(4)
    ]


def log_code(values, inverse_scale):
    share = 1.0 + CURVE * (jnp.abs(values) * inverse_scale)
    code = jnp.exp2(jnp.log2(share) * SLOPE - REACH)
    return jnp.where(values < 0.0, -code, code).astype(jnp.bfloat16)


def log_decode(code, scale):
    code = code.astype(jnp.float32)
    share = jnp.exp2((jnp.log2(jnp.abs(code)) + REACH) * (1.0 / SLOPE)) - 1.0
    values = share * (scale * (1.0 / CURVE))
    return jnp.where(code < 0.0, -values, values)


def table_dot(table_ref, f, both):
    half = both.shape[1] // 2
    which = min(f, 1)
    found = jnp.dot(table_ref[0, which], both, preferred_element_type=jnp.float32)
    rest = jnp.dot(table_ref[1, which], both[:, :half], preferred_element_type=jnp.float32)
    return found[:, :half] + (found[:, half:] + rest)


def times_spec(first, second, conj_second, packed):
    (ar, ai), (br, bi) = first, second
    inner = ai * bi
    cross = ai * br - ar * bi if conj_second else ai * br + ar * bi
    if packed:
        line = lax.broadcasted_iota(jnp.int32, inner.shape, 0) == 0
        cross = jnp.where(line, inner, cross)
        inner = jnp.where(line, 0.0, inner)
    return (ar * br + inner if conj_second else ar * br - inner), cross


def spec_parts(spec, rows, column):
    lanes = slice(column * LANES, (column + 1) * LANES)
    return spec[:rows, lanes], spec[rows:, lanes]


def side_by_side(products):
    pairs = [split_pair(jnp.concatenate(pair, axis=0)) for pair in products]
    return jnp.concatenate([high for high, _ in pairs] + [low for _, low in pairs], axis=1)


def put_classes(ref, column, columns, rows, b0, values, turn):
    for f, pair in enumerate(forward_classes(values)):
        if f > 0:
            cosine, sine = [turn[2 * f - 2 + n, pl.ds(b0, CHUNK), :] for n in range(2)]
            pair = (pair[0] * cosine + pair[1] * sine, pair[1] * cosine - pair[0] * sine)
        for part, value in enumerate(pair):
            high, low = split_pair(value)
            at = pl.ds(part * rows + b0, CHUNK)
            ref[f, at, pl.ds(column * LANES, LANES)] = high
            ref[f, at, pl.ds((columns + column) * LANES, LANES)] = low


def take_classes(ref, column, rows, b0, turn):
    lanes = pl.ds(column * LANES, LANES)
    found = []
    for f in range(ref.shape[0]):
        pair = ref[f, pl.ds(b0, CHUNK), lanes], ref[f, pl.ds(rows + b0, CHUNK), lanes]
        if f > 0:
            cosine, sine = [turn[2 * f - 2 + n, pl.ds(b0, CHUNK), :] for n in range(2)]
            pair = (pair[0] * cosine - pair[1] * sine, pair[1] * cosine + pair[0] * sine)
        found.append(pair)
    return inverse_classes(found)


def short_filter(gain, ref, at):
    return (
        gain[0] * ref[pl.ds(at, CHUNK), :]
        + gain[1] * ref[pl.ds(at - 1, CHUNK), :]
        + gain[2] * ref[pl.ds(at - 2, CHUNK), :]
    )


def widen(me_ref, got, targets, rows):
    def body(step, carry):
        b0 = pl.multiple_of(step * CHUNK, CHUNK)
        for k, ref in zip(SENT, got):
            at = pl.multiple_of((me_ref[0] ^ k) * rows + b0, CHUNK)
            for field, (target, pad) in enumerate(targets):
                target[pl.ds(pad + at, CHUNK), :] = ref[pl.ds(field * rows + b0, CHUNK), :].astype(
                    jnp.float32
                )
        return carry

    lax.fori_loop(0, rows // CHUNK, body, 0, unroll=8)


def gains(taps_ref):
    return [[taps_ref[3 * i + j : 3 * i + j + 1, :] for j in range(3)] for i in range(3)]


def layer_kernel(me_ref, gain_ref, turn, forward_ref, inverse_ref, *refs):
    got, outs = refs[:RADIX], refs[RADIX : 2 * RADIX]
    qp, kp, vp, hs, cot, ks, vs, xs, xs_grad, spec, spec_grad, ys_conv, ys, zs_conv, zs, conv, mgrad, fgrad, peak, sums, head = refs[2 * RADIX :]
    rows = got[0].shape[0] // FIELDS
    total = RADIX * rows
    f32 = jnp.float32
    gain = gains(gain_ref)
    for ref in (qp, kp, vp):
        ref[pl.ds(0, PAD), :] = jnp.zeros((PAD, LANES), f32)
    for ref in (cot, ks, vs, conv, mgrad):
        ref[pl.ds(total, PAD), :] = jnp.zeros((PAD, LANES), f32)
    widen(me_ref, got, ((qp, PAD), (kp, PAD), (vp, PAD), (hs, 0), (cot, 0)), rows)

    chunks = range(0, rows, CHUNK)
    classes = range(xs.shape[0])
    for b0 in chunks:
        mixed = []
        for a in range(RADIX):
            at = a * rows + b0
            key_filt = short_filter(gain[1], kp, PAD + at)
            value_filt = short_filter(gain[2], vp, PAD + at)
            ks[pl.ds(at, CHUNK), :] = key_filt
            vs[pl.ds(at, CHUNK), :] = value_filt
            mixed.append(key_filt * value_filt)
        put_classes(xs, 0, 2, rows, b0, mixed, turn)
        filt = [hs[pl.ds(a * rows + b0, CHUNK), :] for a in range(RADIX)]
        put_classes(xs, 1, 2, rows, b0, filt, turn)
    for f, b0 in zip(classes, chunks):
        spec[f] = table_dot(forward_ref, f, xs[f])
        conv_grad = []
        for a in range(RADIX):
            at = a * rows + b0
            conv_grad.append(short_filter(gain[0], qp, PAD + at) * cot[pl.ds(at, CHUNK), :])
        put_classes(xs_grad, 0, 1, rows, b0, conv_grad, turn)
    for f in classes:
        spec_grad[f] = table_dot(forward_ref, f, xs_grad[f])
        mixed, filt = [spec_parts(spec[f], rows, c) for c in range(2)]
        ys_conv[f] = side_by_side([times_spec(mixed, filt, False, f == 0)])
    for f in classes:
        zs_conv[f] = table_dot(inverse_ref, f, ys_conv[f])
        mixed, filt = [spec_parts(spec[f], rows, c) for c in range(2)]
        grad = spec_parts(spec_grad[f], rows, 0)
        ys[f] = side_by_side([times_spec(grad, one, True, f == 0) for one in (filt, mixed)])
    peak[...] = jnp.zeros_like(peak)
    sums[...] = jnp.zeros_like(sums)

    def take(column, b0, ref, source, place):
        found = take_classes(source, place, rows, b0, turn)
        for a, value in enumerate(found):
            ref[pl.ds(a * rows + b0, CHUNK), :] = value
            size = jnp.abs(value)
            peak[column, a] = jnp.maximum(peak[column, a], jnp.maximum(size[:8], size[8:]))
        return found

    def add(i, b0, source, values, other):
        found = [jnp.zeros((CHUNK, LANES), f32)] * 3
        for a, value in enumerate(values):
            at = a * rows + b0
            now = value * other[pl.ds(at, CHUNK), :]
            for j in range(3):
                found[j] = found[j] + now * source[pl.ds(PAD + at - j, CHUNK), :]
        for j in range(3):
            sums[3 * i + j] += found[j][:8] + found[j][8:]

    for f, b0 in zip(classes, chunks):
        zs[f] = table_dot(inverse_ref, f, ys[f])
        add(0, b0, qp, take(0, b0, conv, zs_conv, 0), cot)
    for b0 in chunks:
        found = take(1, b0, mgrad, zs, 0)
        add(1, b0, kp, found, vs)
        add(2, b0, vp, found, ks)
        take(2, b0, fgrad, zs, 1)
    grad_scale = 1.0 / math.sqrt(total)
    head[...] = jnp.zeros_like(head)
    for n in range(9):
        at = 32 + n if n < 8 else 22
        head[pl.ds(at, 1), :] = jnp.sum(sums[n], axis=0, keepdims=True) * grad_scale
    head[pl.ds(40, 8), :] = split_pair(head[pl.ds(32, 8), :])[1].astype(f32)
    for k, out_ref in zip(BACK, outs):
        a = me_ref[0] ^ k
        first = pl.multiple_of(a * rows, rows)
        after = first + rows
        for i, ref in enumerate((qp, kp, vp)):
            head[pl.ds(2 * i, 2), :] = ref[pl.ds(first + PAD - 2, 2), :]
        for column, ref in enumerate((conv, mgrad, fgrad)):
            top = jnp.max(peak[column, a], axis=0, keepdims=True)
            scale = jnp.maximum(top * (1.0 + 2.0**-7), TINY).astype(jnp.bfloat16).astype(f32)
            head[pl.ds(6 + column, 1), :] = scale
            out_ref[pl.ds(column * rows, rows), :] = log_code(
                ref[pl.ds(first, rows), :], 1.0 / scale
            )
        for i, (ref, other) in enumerate(((conv, cot), (mgrad, vs), (mgrad, ks))):
            head[pl.ds(16 + 2 * i, 2), :] = ref[pl.ds(after, 2), :] * other[pl.ds(after, 2), :]
        head[pl.ds(24, 8), :] = split_pair(head[pl.ds(16, 8), :])[1].astype(f32)
        out_ref[pl.ds(3 * rows, 48), :] = head[...].astype(jnp.bfloat16)


def prepare_kernel(
    me_ref, turns_ref, forward_any, inverse_any, taps_any, _, query_ref, key_ref, value_ref, cot_ref,
    turn, forward_ref, inverse_ref, gain_ref, wide_ref, early_ref, wide,
):
    lane = pl.ds(pl.multiple_of(me_ref[0] * LANES, LANES), LANES)
    forward_ref[...] = forward_any[...]
    inverse_ref[...] = inverse_any[...]
    for n in range(turn.shape[0]):
        turn[n] = jnp.broadcast_to(turns_ref[:, n : n + 1], turn.shape[1:])
    for i in range(3):
        for j in range(3):
            at = 3 * i + j
            wide_ref[at : at + 1, :] = taps_any[i, j : j + 1, :].astype(jnp.float32)
            gain_ref[at : at + 1, :] = taps_any[i, j : j + 1, lane].astype(jnp.float32)
    rows = cot_ref.shape[0]
    for i, ref in enumerate((query_ref, key_ref, value_ref)):
        wide[pl.ds(0, PAD), :] = jnp.zeros((PAD, wide.shape[1]), jnp.float32)
        wide[pl.ds(PAD, rows), :] = ref[...].astype(jnp.float32)
        early_ref[i] = (
            wide_ref[3 * i : 3 * i + 1, :] * wide[pl.ds(PAD, rows), :]
            + wide_ref[3 * i + 1 : 3 * i + 2, :] * wide[pl.ds(PAD - 1, rows), :]
            + wide_ref[3 * i + 2 : 3 * i + 3, :] * wide[pl.ds(PAD - 2, rows), :]
        )
    early_ref[3] = cot_ref[...].astype(jnp.float32)


def whole_vmem(count):
    return [pl.BlockSpec(memory_space=pltpu.VMEM)] * count


def whole_any(count):
    return [pl.BlockSpec(memory_space=pl.ANY)] * count


IN_SMEM = pl.BlockSpec(memory_space=pltpu.SMEM)


def pack_kernel(places, me_ref, *refs):
    sources, outs, land, sem = refs[:FIELDS], refs[FIELDS:-2], refs[-2], refs[-1]
    rows = sources[0].shape[0]
    copies = [
        pltpu.make_async_copy(source, land.at[field], sem.at[field])
        for field, source in enumerate(sources)
    ]
    for copy in copies:
        copy.start()
    for field, copy in enumerate(copies):
        copy.wait()
        for k, out_ref in zip(places, outs):
            lane = pl.multiple_of((me_ref[0] ^ k) * LANES, LANES)
            out_ref[pl.ds(field * rows, rows), :] = land[field, :, pl.ds(lane, LANES)]


def finish_blocks(me_ref, places, got, wide_ref, early_ref, outs, grads, stage, stage_filter, stage_taps, sem):
    rows = early_ref.shape[1]
    f32, bf16 = jnp.float32, jnp.bfloat16
    copies = []
    for n, (k, got_ref) in enumerate(zip(places, got)):
        lanes = pl.ds(pl.multiple_of((me_ref[0] ^ k) * LANES, LANES), LANES)
        head = got_ref[pl.ds(3 * rows, 48), :].astype(f32)
        conv, mixed_grad, filt = [
            log_decode(got_ref[pl.ds(c * rows, rows), :], head[6 + c : 7 + c]) for c in range(3)
        ]
        stage_filter[n] = filt * (1.0 / math.sqrt(RADIX * rows))
        pairs = head[16:24] + head[24:32]
        taps = head[32:40] + head[40:48]
        for c in range(9):
            stage_taps[n, c // 3, c % 3 : c % 3 + 1, :] = taps[c : c + 1] if c < 8 else pairs[6:7]
        line = lax.broadcasted_iota(jnp.int32, (PAD, LANES), 0)
        filtered = []
        gain = []
        for i in range(3):
            gain.append([wide_ref[3 * i + j : 3 * i + j + 1, lanes] for j in range(3)])
            before, last = head[2 * i : 2 * i + 1], head[2 * i + 1 : 2 * i + 2]
            top = early_ref[i, 0:PAD, lanes] + jnp.where(
                line == 0,
                gain[i][1] * last + gain[i][2] * before,
                jnp.where(line == 1, gain[i][2] * last, 0.0),
            )
            filtered.append(jnp.concatenate([top, early_ref[i, PAD:, lanes]], axis=0))
        stage[n, 0] = (filtered[0] * conv).astype(bf16)
        inner = (
            conv * early_ref[3, :, lanes],
            mixed_grad * filtered[2],
            mixed_grad * filtered[1],
        )
        for i in range(3):
            grads[i, pl.ds(0, rows), :] = inner[i]
            grads[i, pl.ds(rows, 2), :] = pairs[2 * i : 2 * i + 2]
            stage[n, 1 + i] = (
                gain[i][0] * inner[i]
                + gain[i][1] * grads[i, pl.ds(1, rows), :]
                + gain[i][2] * grads[i, pl.ds(2, rows), :]
            ).astype(bf16)
        for c, out in enumerate(outs):
            source = stage.at[n, c] if c < 4 else (stage_filter, stage_taps)[c - 4].at[n]
            target = out.at[:, lanes] if c < 5 else out.at[:, :, lanes]
            copies.append(pltpu.make_async_copy(source, target, sem.at[len(copies)]))
            copies[-1].start()
    return copies


def finish_kernel(places, begun, me_ref, *refs):
    count = len(places)
    got, (wide_ref, early_ref), refs = refs[:count], refs[count : count + 2], refs[count + 2 + begun :]
    for copy in finish_blocks(me_ref, places, got, wide_ref, early_ref, refs[:6], *refs[6:]):
        copy.wait()


def swap_blocks(places, blocks):
    devices = range(RADIX)
    return [
        lax.ppermute(block, "ctx", [(i, i ^ k) for i in devices]) if k else block
        for k, block in zip(places, blocks)
    ]


def held(arrays, space):
    return [pltpu.with_memory_space_constraint(jnp.asarray(one), space) for one in arrays]


def local_fast(query_in, key_in, value_in, long_filter, short_taps, out_grad):
    rows, channels = query_in.shape
    total = RADIX * rows
    f32, bf16 = jnp.float32, jnp.bfloat16
    shape = jax.ShapeDtypeStruct
    inputs = held((query_in, key_in, value_in, out_grad), pltpu.HBM)
    small = pltpu.CompilerParams(vmem_limit_bytes=12 * 1024 * 1024)
    me = lax.axis_index("ctx").astype(jnp.int32).reshape(1)
    sources = held((query_in, key_in, value_in, long_filter, out_grad), pltpu.HBM)

    def pack(places):
        return pl.pallas_call(
            partial(pack_kernel, places),
            out_shape=[pltpu.VMEM((FIELDS * rows, LANES), bf16)] * len(places),
            in_specs=[IN_SMEM] + whole_any(FIELDS),
            out_specs=whole_vmem(len(places)),
            scratch_shapes=[
                pltpu.VMEM((FIELDS, rows, channels), bf16),
                pltpu.SemaphoreType.DMA((FIELDS,)),
            ],
            compiler_params=small,
            name="pack",
        )(me, *sources)

    packed = pack(SENT)
    got = swap_blocks(SENT, packed)
    forward, inverse, turns = class_tables(rows)
    count = 1 + len(CLASSES)
    ready = pl.pallas_call(
        prepare_kernel,
        out_shape=[
            pltpu.VMEM((2 * len(CLASSES), rows, LANES), f32),
            pltpu.VMEM(forward.shape, bf16),
            pltpu.VMEM(inverse.shape, bf16),
            pltpu.VMEM((16, LANES), f32),
            pltpu.VMEM((16, channels), f32),
            pltpu.VMEM((4, rows, channels), f32),
        ],
        in_specs=[IN_SMEM] + whole_vmem(9),
        out_specs=whole_vmem(6),
        scratch_shapes=[pltpu.VMEM((PAD + rows, channels), f32)],
        compiler_params=small,
        name="prepare",
    )(me, *held((turns, forward, inverse), pltpu.HBM), short_taps, *held(got[1:2], pltpu.VMEM), *inputs)
    ready = held(ready, pltpu.VMEM)
    done = pl.pallas_call(
        layer_kernel,
        out_shape=[pltpu.VMEM((3 * rows + 48, LANES), bf16)] * RADIX,
        in_specs=[IN_SMEM] + whole_vmem(4 + RADIX),
        out_specs=whole_vmem(RADIX),
        scratch_shapes=[pltpu.VMEM((total + PAD, LANES), f32)] * 7
        + [
            pltpu.VMEM((count, 2 * rows, columns * LANES), kind)
            for columns, kind in (
                (4, bf16), (2, bf16), (2, f32), (1, f32), (2, bf16), (4, bf16), (1, f32), (2, f32)
            )
        ]
        + [pltpu.VMEM((total + PAD, LANES), f32)] * 3
        + [
            pltpu.VMEM((3, RADIX, 8, LANES), f32),
            pltpu.VMEM((9, 8, LANES), f32),
            pltpu.VMEM((48, LANES), f32),
        ],
        compiler_params=pltpu.CompilerParams(vmem_limit_bytes=20 * 1024 * 1024),
        name="layer",
    )(me, ready[3], *ready[:3], *held(got, pltpu.VMEM))
    back = held(swap_blocks(BACK, done), pltpu.VMEM)
    results = [shape((rows, channels), bf16)] * 4 + [
        shape((rows, channels), f32),
        shape((3, 3, channels), f32),
    ]

    begun = []
    for first, last in zip(FINISHED, FINISHED[1:]):
        count = last - first
        begun = pl.pallas_call(
            partial(finish_kernel, BACK[first:last], len(begun)),
            out_shape=results,
            in_specs=[IN_SMEM] + whole_vmem(count + 2) + whole_any(len(begun)),
            out_specs=whole_any(6),
            scratch_shapes=[
                pltpu.VMEM((3, rows + PAD, LANES), f32),
                pltpu.VMEM((count, 4, rows, LANES), bf16),
                pltpu.VMEM((count, rows, LANES), f32),
                pltpu.VMEM((count, 3, 3, LANES), f32),
                pltpu.SemaphoreType.DMA((6 * count,)),
            ],
            input_output_aliases={count + 3 + n: n for n in range(len(begun))},
            compiler_params=small,
            name="finish",
        )(me, *back[first:last], *ready[4:], *begun)
    return tuple(begun)


def local(query_in, key_in, value_in, long_filter, short_taps, out_grad):
    rows, channels = query_in.shape
    blocks = lax.axis_size("ctx")
    taps = short_taps.shape[:2]
    if blocks == RADIX and channels == blocks * LANES and rows == LANES and taps == (3, 3):
        return local_fast(query_in, key_in, value_in, long_filter, short_taps, out_grad)
    return local_general(query_in, key_in, value_in, long_filter, short_taps, out_grad)


def solution(mesh):
    placed = (
        P("ctx", "tp"),
        P("ctx", "tp"),
        P("ctx", "tp"),
        P("ctx", "tp"),
        P(None, None, "tp"),
        P("ctx", "tp"),
    )
    return jax.shard_map(
        local,
        mesh=mesh,
        in_specs=placed,
        out_specs=(
            P("ctx", "tp"),
            P("ctx", "tp"),
            P("ctx", "tp"),
            P("ctx", "tp"),
            P("ctx", "tp"),
            P(None, None, "tp"),
        ),
        check_vma=False,
    )
```

```python
from functools import lru_cache, partial, reduce
import math

import jax
import jax.numpy as jnp
import ml_dtypes
import numpy as np
from jax import lax
from jax.experimental import pallas as pl
from jax.experimental.pallas import tpu as pltpu
from jax.sharding import PartitionSpec as P

HIGHEST_PREC = lax.Precision.HIGHEST
TWO_PI = 2.0 * math.pi


def passed_along(block, axis, distance):
    devices = range(lax.axis_size(axis))
    route = [(i - distance, i) for i in devices if i - distance in devices]
    return lax.ppermute(block, axis, route)


def phase_pair(count_a, count_b, period, direction):
    product = (
        jnp.arange(count_a, dtype=jnp.int32)[:, None]
        * jnp.arange(count_b, dtype=jnp.int32)[None, :]
    )
    phase_angle = direction * TWO_PI / period * (product % period).astype(jnp.float32)
    return (jnp.cos(phase_angle), jnp.sin(phase_angle))


def rotate_pair(real_part, imag_part, cosine, sine_part):
    return (real_part * cosine - imag_part * sine_part, real_part * sine_part + imag_part * cosine)


def times_pair(first_pair, second_pair, conj_second):
    factor = -1.0 if conj_second else 1.0
    real_part = first_pair[0] * second_pair[0] - factor * first_pair[1] * second_pair[1]
    imag_part = first_pair[1] * second_pair[0] + factor * first_pair[0] * second_pair[1]
    return (real_part, imag_part)


def unpack_fields(spectrum, comp_axis, field_axis):
    collected = []
    for partner_rank in range(spectrum.shape[field_axis]):
        single = lax.index_in_dim(spectrum, partner_rank, field_axis, keepdims=True)
        collected.append(
            (
                lax.index_in_dim(single, 0, comp_axis, keepdims=True),
                lax.index_in_dim(single, 1, comp_axis, keepdims=True),
            )
        )
    return collected


def pack_fields(pairs, comp_axis, field_axis):
    return jnp.concatenate(
        [jnp.concatenate([real_part, imag_part], axis=comp_axis) for real_part, imag_part in pairs],
        axis=field_axis,
    )


def spread_forward(regroup, fields):
    row_count, field_count, channels = fields.shape
    part_count = lax.axis_size("ctx")
    block_rows = row_count // part_count
    length = 2 * part_count * row_count
    my_index = lax.axis_index("ctx")
    gathered = regroup(fields.reshape(part_count, 1, block_rows, field_count, channels))
    cosine, sine_part = phase_pair(2 * part_count, part_count, 2 * part_count, -1.0)
    first_table = jnp.stack([cosine, sine_part], axis=1)
    first_pass = jnp.einsum("kda,arfc->kdrfc", first_table, gathered, precision=HIGHEST_PREC)
    row_index = my_index * block_rows + jnp.arange(block_rows, dtype=jnp.int32)
    twist_index = jnp.arange(2 * part_count, dtype=jnp.int32)[:, None] * row_index[None, :] % length
    phase_angle = -TWO_PI / length * twist_index.astype(jnp.float32)
    cos_twist = jnp.cos(phase_angle)[:, :, None, None]
    sin_twist = jnp.sin(phase_angle)[:, :, None, None]
    real_part, imag_part = rotate_pair(first_pass[:, 0], first_pass[:, 1], cos_twist, sin_twist)
    turned = jnp.stack([real_part, imag_part], axis=1)
    arrived = regroup(turned.reshape(part_count, 1, 2, 2, block_rows, field_count, channels))
    cosine, sine_part = phase_pair(row_count, row_count, row_count, -1.0)
    second_table = jnp.stack(
        [jnp.stack([cosine, sine_part], axis=-1), jnp.stack([-sine_part, cosine], axis=-1)], axis=0
    )
    second_table = second_table.reshape(2, part_count, block_rows, row_count, 2)
    return jnp.einsum("pqsrfc,sprkd->qkdfc", arrived, second_table, precision=HIGHEST_PREC)


def spread_inverse(regroup, spectrum):
    pair_count, row_count, _, field_count, channels = spectrum.shape
    part_count = lax.axis_size("ctx")
    block_rows = row_count // part_count
    length = 2 * part_count * row_count
    my_index = lax.axis_index("ctx")
    cosine, sine_part = phase_pair(row_count, row_count, row_count, 1.0)
    second_table = jnp.stack(
        [jnp.stack([cosine, sine_part], axis=-1), jnp.stack([-sine_part, cosine], axis=-1)], axis=0
    )
    second_table = second_table.reshape(2, row_count, part_count, block_rows, 2)
    row_parts = jnp.einsum("qkdfc,dkprs->pqsrfc", spectrum, second_table, precision=HIGHEST_PREC)
    freq_index = my_index * pair_count + jnp.arange(pair_count, dtype=jnp.int32)
    twist_index = freq_index[:, None] * jnp.arange(row_count, dtype=jnp.int32)[None, :] % length
    phase_angle = TWO_PI / length * twist_index.astype(jnp.float32)
    cos_twist = (
        jnp.cos(phase_angle)
        .reshape(pair_count, part_count, block_rows)
        .transpose(1, 0, 2)[:, :, :, None, None]
    )
    sin_twist = (
        jnp.sin(phase_angle)
        .reshape(pair_count, part_count, block_rows)
        .transpose(1, 0, 2)[:, :, :, None, None]
    )
    real_part, imag_part = rotate_pair(row_parts[:, :, 0], row_parts[:, :, 1], cos_twist, sin_twist)
    turned = jnp.stack([real_part, imag_part], axis=2)
    arrived = regroup(
        turned.reshape(part_count, 1, pair_count, 2, block_rows, field_count, channels)
    )
    cosine, sine_part = phase_pair(2 * part_count, part_count, 2 * part_count, 1.0)
    first_table = (jnp.stack([cosine, -sine_part], axis=1) / length).reshape(
        part_count, pair_count, 2, part_count
    )
    values = jnp.einsum("pqsrfc,pqsa->arfc", arrived, first_table, precision=HIGHEST_PREC)
    returned = regroup(values.reshape(part_count, 1, block_rows, field_count, channels))
    return returned.reshape(row_count, field_count, channels)


def local_general(query_in, key_in, value_in, long_filter, short_taps, out_grad):
    row_count = query_in.shape[0]
    tap_count = short_taps.shape[1]
    margin = tap_count - 1
    part_count = lax.axis_size("ctx")

    def regroup(blocks):
        return lax.all_to_all(blocks, "ctx", split_axis=0, concat_axis=1, tiled=True)[0]

    to_freq = partial(spread_forward, regroup)
    from_freq = partial(spread_inverse, regroup)
    comp_axis = 2
    field_axis = 3
    inputs = jnp.stack([query_in, key_in, value_in])
    earlier = passed_along(inputs[:, row_count - margin :], "ctx", 1)
    extended = jnp.concatenate([earlier, inputs], axis=1).astype(jnp.float32)
    tap_gain = short_taps.astype(jnp.float32)
    filtered = tap_gain[:, 0, None, :] * extended[:, margin:]
    for offset in range(1, tap_count):
        filtered = (
            filtered
            + tap_gain[:, offset, None, :]
            * extended[:, margin - offset : margin - offset + row_count]
        )
    query_filt = filtered[0]
    key_filt = filtered[1]
    value_filt = filtered[2]
    mixed_in = key_filt * value_filt
    spectra = to_freq(jnp.stack([mixed_in, long_filter.astype(jnp.float32)], axis=1))
    mixed_spec, filter_spec = unpack_fields(spectra, comp_axis, field_axis)
    convolved = from_freq(
        pack_fields([times_pair(mixed_spec, filter_spec, False)], comp_axis, field_axis)
    )[:, 0]
    output = (query_filt * convolved).astype(jnp.bfloat16)
    grad_in = out_grad.astype(jnp.float32)
    gate_grad = grad_in * convolved
    conv_grad = grad_in * query_filt
    grad_spec = unpack_fields(to_freq(conv_grad[:, None, :]), comp_axis, field_axis)[0]
    returned = from_freq(
        pack_fields(
            [times_pair(grad_spec, filter_spec, True), times_pair(grad_spec, mixed_spec, True)],
            comp_axis,
            field_axis,
        )
    )
    grad_scale = 1.0 / math.sqrt(part_count * row_count)
    mixed_grad = returned[:, 0]
    filter_grad = returned[:, 1] * grad_scale
    grad_stack = jnp.stack([gate_grad, mixed_grad * value_filt, mixed_grad * key_filt])
    later_rows = passed_along(grad_stack[:, :margin], "ctx", -1)
    padded_grad = jnp.concatenate([grad_stack, later_rows], axis=1)
    input_grads = tap_gain[:, 0, None, :] * grad_stack
    for offset in range(1, tap_count):
        input_grads = (
            input_grads + tap_gain[:, offset, None, :] * padded_grad[:, offset : offset + row_count]
        )
    partial_taps = jnp.stack(
        [
            jnp.sum(grad_stack * extended[:, margin - offset : margin - offset + row_count], axis=1)
            for offset in range(tap_count)
        ],
        axis=1,
    )
    taps_grad = lax.psum(partial_taps, "ctx") * grad_scale
    return (
        output,
        input_grads[0].astype(jnp.bfloat16),
        input_grads[1].astype(jnp.bfloat16),
        input_grads[2].astype(jnp.bfloat16),
        filter_grad,
        taps_grad,
    )


RADIX = 8
FIELDS = 5
CLASSES = (4, 2, 6, 1, 5, 9, 13)
LANES = 128
PAD = 8
CHUNK = 16
SENT = (0, 6, 2, 5, 3, 4, 7, 1)
BACK = (0, 6, 2, 5, 3, 4, 7, 1)
FINISHED = (0, 4, 6, 8)
CURVE = 15.0
REACH = 120.0
SLOPE = 2.0 * REACH / math.log2(1.0 + CURVE)
TINY = 1e-30
HEAD = 32
TAPS_AT = (10, 11, 12, 13, 14, 15, 28, 29, 30)


def split_pair(values):
    high = values.astype(jnp.bfloat16)
    low = (values - high.astype(jnp.float32)).astype(jnp.bfloat16)
    return high, low


@lru_cache(maxsize=None)
def class_tables(rows):
    length = 2 * RADIX * rows
    back = np.arange(rows)

    def waves(residue, count):
        angle = 2.0 * np.pi * (np.outer(2 * RADIX * np.arange(count) + residue, back) % length) / length
        return np.cos(angle), np.sin(angle)

    half = rows // 2
    cos0, sin0 = waves(0, half)
    cos8, sin8 = waves(RADIX, half)
    none = np.zeros((half, rows))
    middle = (1.0 - 2.0 * (back % 2))[None, :]
    imag0 = np.concatenate([middle, -sin0[1:]])
    forward = [np.block([[cos0, none], [none, cos8], [imag0, none], [none, -sin8]])]
    weight = np.full((2 * rows, 1), 2.0)
    weight[0] = weight[rows] = 1.0
    inverse = [(weight * forward[0]).T]
    for residue in CLASSES:
        cosine, sine = waves(residue, rows)
        forward.append(np.block([[cosine, sine], [-sine, cosine]]))
        inverse.append(2.0 * forward[-1].T)
    tables = []
    for table in (np.stack(forward), np.stack(inverse) / length):
        high = table.astype(ml_dtypes.bfloat16)
        low = (table - high.astype(np.float64)).astype(ml_dtypes.bfloat16)
        tables.append(np.stack([high, low]))
    return tables


ROOT = math.sqrt(0.5)
COS1 = math.cos(math.pi / 8)
SIN1 = math.sin(math.pi / 8)


def forward_classes(x):
    u = [x[a] + x[a + 4] for a in range(4)]
    d = [x[a] - x[a + 4] for a in range(4)]
    even, odd = u[0] + u[2], u[1] + u[3]
    dif, tot = ROOT * (d[1] - d[3]), ROOT * (d[1] + d[3])
    found = [
        (even + odd, even - odd),
        (u[0] - u[2], u[3] - u[1]),
        (d[0] + dif, -d[2] - tot),
        (d[0] - dif, d[2] - tot),
    ]
    w0 = (x[0], -x[4])
    w1 = (COS1 * x[1] - SIN1 * x[5], -SIN1 * x[1] - COS1 * x[5])
    w2 = (ROOT * (x[2] - x[6]), -ROOT * (x[2] + x[6]))
    w3 = (SIN1 * x[3] - COS1 * x[7], -COS1 * x[3] - SIN1 * x[7])
    s02 = (w0[0] + w2[0], w0[1] + w2[1])
    d02 = (w0[0] - w2[0], w0[1] - w2[1])
    s13 = (w1[0] + w3[0], w1[1] + w3[1])
    d13 = (w1[0] - w3[0], w1[1] - w3[1])
    found.append((s02[0] + s13[0], s02[1] + s13[1]))
    found.append((d02[0] + d13[1], d02[1] - d13[0]))
    found.append((s02[0] - s13[0], s02[1] - s13[1]))
    found.append((d02[0] - d13[1], d02[1] + d13[0]))
    return found


def inverse_classes(z):
    (z0, z8), (r4, i4), (r2, i2), (r6, i6) = z[:4]
    up, down = z0 + z8, z0 - z8
    even = [up + r4, down - i4, up - r4, down + i4]
    gap, tot = ROOT * (r2 - r6), ROOT * (i2 + i6)
    turn = [r2 + r6, gap - tot, i6 - i2, -gap - tot]
    (r1, i1), (r5, i5), (r9, i9), (rd, id_) = z[4:]
    s = (r1 + r9, i1 + i9)
    d = (r1 - r9, i1 - i9)
    t = (r5 + rd, i5 + id_)
    e = (r5 - rd, i5 - id_)
    s0 = (s[0] + t[0], s[1] + t[1])
    s2 = (s[0] - t[0], s[1] - t[1])
    s1 = (d[0] - e[1], d[1] + e[0])
    s3 = (d[0] + e[1], d[1] - e[0])
    q = [
        s0,
        (COS1 * s1[0] - SIN1 * s1[1], SIN1 * s1[0] + COS1 * s1[1]),
        (ROOT * (s2[0] - s2[1]), ROOT * (s2[0] + s2[1])),
        (SIN1 * s3[0] - COS1 * s3[1], COS1 * s3[0] + SIN1 * s3[1]),
    ]
    return [even[a] + turn[a] + q[a][0] for a in range(4)] + [
        even[a] - turn[a] - q[a][1] for a in range(4)
    ]


def log_code(values, inverse_scale):
    share = 1.0 + CURVE * (jnp.abs(values) * inverse_scale)
    code = jnp.exp2(jnp.log2(share) * SLOPE - REACH)
    return jnp.where(values < 0.0, -code, code).astype(jnp.bfloat16)


def code_scale(peak):
    return jnp.maximum(peak * (1.0 + 2.0**-7), TINY).astype(jnp.bfloat16).astype(jnp.float32)


def log_decode(code, scale):
    code = code.astype(jnp.float32)
    share = jnp.exp2((jnp.log2(jnp.abs(code)) + REACH) * (1.0 / SLOPE)) - 1.0
    values = share * (scale * (1.0 / CURVE))
    return jnp.where(code < 0.0, -values, values)


def table_dot(table_ref, f, both):
    half = both.shape[1] // 2
    found = jnp.dot(table_ref[0, f], both, preferred_element_type=jnp.float32)
    rest = jnp.dot(table_ref[1, f], both[:, :half], preferred_element_type=jnp.float32)
    return found[:, :half] + (found[:, half:] + rest)


def times_spec(first, second, conj_second, packed):
    (ar, ai), (br, bi) = first, second
    inner = ai * bi
    cross = ai * br - ar * bi if conj_second else ai * br + ar * bi
    if packed:
        line = lax.broadcasted_iota(jnp.int32, inner.shape, 0) == 0
        cross = jnp.where(line, inner, cross)
        inner = jnp.where(line, 0.0, inner)
    return (ar * br + inner if conj_second else ar * br - inner), cross


def spec_parts(spec, rows, column):
    lanes = slice(column * LANES, (column + 1) * LANES)
    return spec[:rows, lanes], spec[rows:, lanes]


def side_by_side(products):
    pairs = [split_pair(jnp.concatenate(pair, axis=0)) for pair in products]
    return jnp.concatenate([high for high, _ in pairs] + [low for _, low in pairs], axis=1)


def put_classes(ref, column, columns, rows, b0, values):
    for f, pair in enumerate(forward_classes(values)):
        for part, value in enumerate(pair):
            high, low = split_pair(value)
            at = pl.ds(part * rows + b0, CHUNK)
            ref[f, at, pl.ds(column * LANES, LANES)] = high
            ref[f, at, pl.ds((columns + column) * LANES, LANES)] = low


def take_classes(ref, column, rows, b0):
    lanes = pl.ds(column * LANES, LANES)
    found = []
    for f in range(ref.shape[0]):
        pair = ref[f, pl.ds(b0, CHUNK), lanes], ref[f, pl.ds(rows + b0, CHUNK), lanes]
        found.append(pair)
    return inverse_classes(found)


def short_filter(gain, ref, at):
    return (
        gain[0] * ref[pl.ds(at, CHUNK), :]
        + gain[1] * ref[pl.ds(at - 1, CHUNK), :]
        + gain[2] * ref[pl.ds(at - 2, CHUNK), :]
    )


def widen(me_ref, got, targets, rows):
    def body(step, carry):
        b0 = pl.multiple_of(step * CHUNK, CHUNK)
        for k, ref in zip(SENT, got):
            at = pl.multiple_of((me_ref[0] ^ k) * rows + b0, CHUNK)
            for field, (target, pad) in enumerate(targets):
                target[pl.ds(pad + at, CHUNK), :] = ref[pl.ds(field * rows + b0, CHUNK), :].astype(
                    jnp.float32
                )
        return carry

    lax.fori_loop(0, rows // CHUNK, body, 0, unroll=8)


def gains(taps_ref):
    return [[taps_ref[3 * i + j : 3 * i + j + 1, :] for j in range(3)] for i in range(3)]


def layer_kernel(me_ref, gain_ref, forward_ref, inverse_ref, *refs):
    got, outs = refs[:RADIX], refs[RADIX : 2 * RADIX]
    qp, kp, vp, hs, cot, ks, vs, xs, xs_grad, spec, spec_grad, ys_conv, ys, zs_conv, zs, conv, mgrad, fgrad, peak, sums, head = refs[2 * RADIX :]
    rows = got[0].shape[0] // FIELDS
    total = RADIX * rows
    f32 = jnp.float32
    gain = gains(gain_ref)
    for ref in (qp, kp, vp):
        ref[pl.ds(0, PAD), :] = jnp.zeros((PAD, LANES), f32)
    for ref in (cot, ks, vs, conv, mgrad):
        ref[pl.ds(total, PAD), :] = jnp.zeros((PAD, LANES), f32)
    widen(me_ref, got, ((qp, PAD), (kp, PAD), (vp, PAD), (hs, 0), (cot, 0)), rows)

    chunks = range(0, rows, CHUNK)
    classes = range(xs.shape[0])
    for b0 in chunks:
        mixed = []
        for a in range(RADIX):
            at = a * rows + b0
            key_filt = short_filter(gain[1], kp, PAD + at)
            value_filt = short_filter(gain[2], vp, PAD + at)
            ks[pl.ds(at, CHUNK), :] = key_filt
            vs[pl.ds(at, CHUNK), :] = value_filt
            mixed.append(key_filt * value_filt)
        put_classes(xs, 0, 2, rows, b0, mixed)
        filt = [hs[pl.ds(a * rows + b0, CHUNK), :] for a in range(RADIX)]
        put_classes(xs, 1, 2, rows, b0, filt)
    for f, b0 in zip(classes, chunks):
        spec[f] = table_dot(forward_ref, f, xs[f])
        conv_grad = []
        for a in range(RADIX):
            at = a * rows + b0
            conv_grad.append(short_filter(gain[0], qp, PAD + at) * cot[pl.ds(at, CHUNK), :])
        put_classes(xs_grad, 0, 1, rows, b0, conv_grad)
    for f in classes:
        spec_grad[f] = table_dot(forward_ref, f, xs_grad[f])
        mixed, filt = [spec_parts(spec[f], rows, c) for c in range(2)]
        ys_conv[f] = side_by_side([times_spec(mixed, filt, False, f == 0)])
    for f in classes:
        zs_conv[f] = table_dot(inverse_ref, f, ys_conv[f])
        mixed, filt = [spec_parts(spec[f], rows, c) for c in range(2)]
        grad = spec_parts(spec_grad[f], rows, 0)
        ys[f] = side_by_side([times_spec(grad, one, True, f == 0) for one in (filt, mixed)])
    peak[...] = jnp.zeros_like(peak)
    sums[...] = jnp.zeros_like(sums)

    def take(column, b0, ref, source, place):
        found = take_classes(source, place, rows, b0)
        for a, value in enumerate(found):
            ref[pl.ds(a * rows + b0, CHUNK), :] = value
            size = jnp.abs(value)
            peak[column, a] = jnp.maximum(peak[column, a], jnp.maximum(size[:8], size[8:]))
        return found

    def add(i, b0, source, values, other):
        found = [jnp.zeros((CHUNK, LANES), f32)] * 3
        for a, value in enumerate(values):
            at = a * rows + b0
            now = value * other[pl.ds(at, CHUNK), :]
            for j in range(3):
                found[j] = found[j] + now * source[pl.ds(PAD + at - j, CHUNK), :]
        for j in range(3):
            sums[3 * i + j] += found[j][:8] + found[j][8:]

    for f, b0 in zip(classes, chunks):
        zs[f] = table_dot(inverse_ref, f, ys[f])
        add(0, b0, qp, take(0, b0, conv, zs_conv, 0), cot)
    for b0 in chunks:
        found = take(1, b0, mgrad, zs, 0)
        add(1, b0, kp, found, vs)
        add(2, b0, vp, found, ks)
        take(2, b0, fgrad, zs, 1)
    grad_scale = 1.0 / math.sqrt(total)
    head[...] = jnp.zeros_like(head)
    taps = [jnp.sum(sums[n], axis=0, keepdims=True) * grad_scale for n in range(9)]
    scale = code_scale(reduce(jnp.maximum, [jnp.abs(line) for line in taps]))
    head[pl.ds(9, 1), :] = scale
    for at, line in zip(TAPS_AT, taps):
        head[pl.ds(at, 1), :] = log_code(line, 1.0 / scale).astype(f32)
    for k, out_ref in zip(BACK, outs):
        a = me_ref[0] ^ k
        first = pl.multiple_of(a * rows, rows)
        after = first + rows
        for i, ref in enumerate((qp, kp, vp)):
            head[pl.ds(2 * i, 2), :] = ref[pl.ds(first + PAD - 2, 2), :]
        for column, ref in enumerate((conv, mgrad, fgrad)):
            top = jnp.max(peak[column, a], axis=0, keepdims=True)
            scale = code_scale(top)
            head[pl.ds(6 + column, 1), :] = scale
            out_ref[pl.ds(column * rows, rows), :] = log_code(
                ref[pl.ds(first, rows), :], 1.0 / scale
            )
        for i, (ref, other) in enumerate(((conv, cot), (mgrad, vs), (mgrad, ks))):
            head[pl.ds(16 + 2 * i, 2), :] = ref[pl.ds(after, 2), :] * other[pl.ds(after, 2), :]
        head[pl.ds(22, 6), :] = split_pair(head[pl.ds(16, 6), :])[1].astype(f32)
        out_ref[pl.ds(3 * rows, HEAD), :] = head[...].astype(jnp.bfloat16)


def prepare_kernel(
    me_ref, forward_any, inverse_any, taps_any, _, query_ref, key_ref, value_ref, cot_ref,
    forward_ref, inverse_ref, gain_ref, wide_ref, early_ref, wide, sem,
):
    lane = pl.ds(pl.multiple_of(me_ref[0] * LANES, LANES), LANES)
    copies = [
        pltpu.make_async_copy(forward_any.at[n], forward_ref.at[n], sem.at[n]) for n in range(2)
    ] + [
        pltpu.make_async_copy(inverse_any.at[n], inverse_ref.at[n], sem.at[2 + n]) for n in range(2)
    ]
    for copy in copies:
        copy.start()
    taps = taps_any[...].astype(jnp.float32)
    for i in range(3):
        for j in range(3):
            at = 3 * i + j
            wide_ref[at : at + 1, :] = taps[i, j : j + 1, :]
            gain_ref[at : at + 1, :] = wide_ref[at : at + 1, lane]
    rows = cot_ref.shape[0]
    for i, ref in enumerate((query_ref, key_ref, value_ref)):
        wide[pl.ds(0, PAD), :] = jnp.zeros((PAD, wide.shape[1]), jnp.float32)
        wide[pl.ds(PAD, rows), :] = ref[...].astype(jnp.float32)
        early_ref[i] = (
            wide_ref[3 * i : 3 * i + 1, :] * wide[pl.ds(PAD, rows), :]
            + wide_ref[3 * i + 1 : 3 * i + 2, :] * wide[pl.ds(PAD - 1, rows), :]
            + wide_ref[3 * i + 2 : 3 * i + 3, :] * wide[pl.ds(PAD - 2, rows), :]
        )
    early_ref[3] = cot_ref[...].astype(jnp.float32)
    for copy in copies:
        copy.wait()


def whole_vmem(count):
    return [pl.BlockSpec(memory_space=pltpu.VMEM)] * count


def whole_any(count):
    return [pl.BlockSpec(memory_space=pl.ANY)] * count


IN_SMEM = pl.BlockSpec(memory_space=pltpu.SMEM)


def pack_kernel(places, me_ref, *refs):
    sources, outs, land, sem = refs[:FIELDS], refs[FIELDS:-2], refs[-2], refs[-1]
    rows = sources[0].shape[0]
    copies = [
        pltpu.make_async_copy(source, land.at[field], sem.at[field])
        for field, source in enumerate(sources)
    ]
    for copy in copies:
        copy.start()
    for field, copy in enumerate(copies):
        copy.wait()
        for k, out_ref in zip(places, outs):
            lane = pl.multiple_of((me_ref[0] ^ k) * LANES, LANES)
            out_ref[pl.ds(field * rows, rows), :] = land[field, :, pl.ds(lane, LANES)]


def finish_blocks(me_ref, places, got, wide_ref, early_ref, outs, grads, stage, stage_filter, stage_taps, sem):
    rows = early_ref.shape[1]
    f32, bf16 = jnp.float32, jnp.bfloat16
    copies = []
    for n, (k, got_ref) in enumerate(zip(places, got)):
        lanes = pl.ds(pl.multiple_of((me_ref[0] ^ k) * LANES, LANES), LANES)
        head = got_ref[pl.ds(3 * rows, HEAD), :].astype(f32)
        conv, mixed_grad, filt = [
            log_decode(got_ref[pl.ds(c * rows, rows), :], head[6 + c : 7 + c]) for c in range(3)
        ]
        stage_filter[n] = filt * (1.0 / math.sqrt(RADIX * rows))
        pairs = head[16:22] + head[22:28]
        for c, at in enumerate(TAPS_AT):
            stage_taps[n, c // 3, c % 3 : c % 3 + 1, :] = log_decode(head[at : at + 1], head[9:10])
        line = lax.broadcasted_iota(jnp.int32, (PAD, LANES), 0)
        filtered = []
        gain = []
        for i in range(3):
            gain.append([wide_ref[3 * i + j : 3 * i + j + 1, lanes] for j in range(3)])
            before, last = head[2 * i : 2 * i + 1], head[2 * i + 1 : 2 * i + 2]
            top = early_ref[i, 0:PAD, lanes] + jnp.where(
                line == 0,
                gain[i][1] * last + gain[i][2] * before,
                jnp.where(line == 1, gain[i][2] * last, 0.0),
            )
            filtered.append(jnp.concatenate([top, early_ref[i, PAD:, lanes]], axis=0))
        stage[n, 0] = (filtered[0] * conv).astype(bf16)
        inner = (
            conv * early_ref[3, :, lanes],
            mixed_grad * filtered[2],
            mixed_grad * filtered[1],
        )
        for i in range(3):
            grads[i, pl.ds(0, rows), :] = inner[i]
            grads[i, pl.ds(rows, 2), :] = pairs[2 * i : 2 * i + 2]
            stage[n, 1 + i] = (
                gain[i][0] * inner[i]
                + gain[i][1] * grads[i, pl.ds(1, rows), :]
                + gain[i][2] * grads[i, pl.ds(2, rows), :]
            ).astype(bf16)
        for c, out in enumerate(outs):
            source = stage.at[n, c] if c < 4 else (stage_filter, stage_taps)[c - 4].at[n]
            target = out.at[:, lanes] if c < 5 else out.at[:, :, lanes]
            copies.append(pltpu.make_async_copy(source, target, sem.at[len(copies)]))
            copies[-1].start()
    return copies


def finish_kernel(places, begun, me_ref, *refs):
    count = len(places)
    got, (wide_ref, early_ref), refs = refs[:count], refs[count : count + 2], refs[count + 2 + begun :]
    for copy in finish_blocks(me_ref, places, got, wide_ref, early_ref, refs[:6], *refs[6:]):
        copy.wait()


def swap_blocks(places, blocks):
    devices = range(RADIX)
    return [
        lax.ppermute(block, "ctx", [(i, i ^ k) for i in devices]) if k else block
        for k, block in zip(places, blocks)
    ]


def held(arrays, space):
    return [pltpu.with_memory_space_constraint(jnp.asarray(one), space) for one in arrays]


def local_fast(query_in, key_in, value_in, long_filter, short_taps, out_grad):
    rows, channels = query_in.shape
    total = RADIX * rows
    f32, bf16 = jnp.float32, jnp.bfloat16
    shape = jax.ShapeDtypeStruct
    inputs = held((query_in, key_in, value_in, out_grad), pltpu.HBM)
    small = pltpu.CompilerParams(vmem_limit_bytes=12 * 1024 * 1024)
    me = lax.axis_index("ctx").astype(jnp.int32).reshape(1)
    sources = held((query_in, key_in, value_in, long_filter, out_grad), pltpu.HBM)

    def pack(places):
        return pl.pallas_call(
            partial(pack_kernel, places),
            out_shape=[pltpu.VMEM((FIELDS * rows, LANES), bf16)] * len(places),
            in_specs=[IN_SMEM] + whole_any(FIELDS),
            out_specs=whole_vmem(len(places)),
            scratch_shapes=[
                pltpu.VMEM((FIELDS, rows, channels), bf16),
                pltpu.SemaphoreType.DMA((FIELDS,)),
            ],
            compiler_params=small,
            name="pack",
        )(me, *sources)

    packed = pack(SENT)
    got = swap_blocks(SENT, packed)
    forward, inverse = class_tables(rows)
    count = 1 + len(CLASSES)
    ready = pl.pallas_call(
        prepare_kernel,
        out_shape=[
            pltpu.VMEM(forward.shape, bf16),
            pltpu.VMEM(inverse.shape, bf16),
            pltpu.VMEM((16, LANES), f32),
            pltpu.VMEM((16, channels), f32),
            pltpu.VMEM((4, rows, channels), f32),
        ],
        in_specs=[IN_SMEM] + whole_any(2) + whole_vmem(6),
        out_specs=whole_vmem(5),
        scratch_shapes=[pltpu.VMEM((PAD + rows, channels), f32), pltpu.SemaphoreType.DMA((4,))],
        compiler_params=small,
        name="prepare",
    )(me, *held((forward, inverse), pltpu.HBM), short_taps, *held(got[1:2], pltpu.VMEM), *inputs)
    ready = held(ready, pltpu.VMEM)
    done = pl.pallas_call(
        layer_kernel,
        out_shape=[pltpu.VMEM((3 * rows + HEAD, LANES), bf16)] * RADIX,
        in_specs=[IN_SMEM] + whole_vmem(3 + RADIX),
        out_specs=whole_vmem(RADIX),
        scratch_shapes=[pltpu.VMEM((total + PAD, LANES), f32)] * 7
        + [
            pltpu.VMEM((count, 2 * rows, columns * LANES), kind)
            for columns, kind in (
                (4, bf16), (2, bf16), (2, f32), (1, f32), (2, bf16), (4, bf16), (1, f32), (2, f32)
            )
        ]
        + [pltpu.VMEM((total + PAD, LANES), f32)] * 3
        + [
            pltpu.VMEM((3, RADIX, 8, LANES), f32),
            pltpu.VMEM((9, 8, LANES), f32),
            pltpu.VMEM((HEAD, LANES), f32),
        ],
        compiler_params=pltpu.CompilerParams(vmem_limit_bytes=20 * 1024 * 1024),
        name="layer",
    )(me, ready[2], *ready[:2], *held(got, pltpu.VMEM))
    back = held(swap_blocks(BACK, done), pltpu.VMEM)
    results = [shape((rows, channels), bf16)] * 4 + [
        shape((rows, channels), f32),
        shape((3, 3, channels), f32),
    ]

    begun = []
    for first, last in zip(FINISHED, FINISHED[1:]):
        count = last - first
        begun = pl.pallas_call(
            partial(finish_kernel, BACK[first:last], len(begun)),
            out_shape=results,
            in_specs=[IN_SMEM] + whole_vmem(count + 2) + whole_any(len(begun)),
            out_specs=whole_any(6),
            scratch_shapes=[
                pltpu.VMEM((3, rows + PAD, LANES), f32),
                pltpu.VMEM((count, 4, rows, LANES), bf16),
                pltpu.VMEM((count, rows, LANES), f32),
                pltpu.VMEM((count, 3, 3, LANES), f32),
                pltpu.SemaphoreType.DMA((6 * count,)),
            ],
            input_output_aliases={count + 3 + n: n for n in range(len(begun))},
            compiler_params=small,
            name="finish",
        )(me, *back[first:last], *ready[3:], *begun)
    return tuple(begun)


def local(query_in, key_in, value_in, long_filter, short_taps, out_grad):
    rows, channels = query_in.shape
    blocks = lax.axis_size("ctx")
    taps = short_taps.shape[:2]
    if blocks == RADIX and channels == blocks * LANES and rows == LANES and taps == (3, 3):
        return local_fast(query_in, key_in, value_in, long_filter, short_taps, out_grad)
    return local_general(query_in, key_in, value_in, long_filter, short_taps, out_grad)


def solution(mesh):
    placed = (
        P("ctx", "tp"),
        P("ctx", "tp"),
        P("ctx", "tp"),
        P("ctx", "tp"),
        P(None, None, "tp"),
        P("ctx", "tp"),
    )
    return jax.shard_map(
        local,
        mesh=mesh,
        in_specs=placed,
        out_specs=(
            P("ctx", "tp"),
            P("ctx", "tp"),
            P("ctx", "tp"),
            P("ctx", "tp"),
            P("ctx", "tp"),
            P(None, None, "tp"),
        ),
        check_vma=False,
    )
```

```python
from functools import lru_cache, partial, reduce
import math

import jax
import jax.numpy as jnp
import ml_dtypes
import numpy as np
from jax import lax
from jax.experimental import pallas as pl
from jax.experimental.pallas import tpu as pltpu
from jax.sharding import PartitionSpec as P

HIGHEST_PREC = lax.Precision.HIGHEST
TWO_PI = 2.0 * math.pi


def passed_along(block, axis, distance):
    devices = range(lax.axis_size(axis))
    route = [(i - distance, i) for i in devices if i - distance in devices]
    return lax.ppermute(block, axis, route)


def phase_pair(count_a, count_b, period, direction):
    product = (
        jnp.arange(count_a, dtype=jnp.int32)[:, None]
        * jnp.arange(count_b, dtype=jnp.int32)[None, :]
    )
    phase_angle = direction * TWO_PI / period * (product % period).astype(jnp.float32)
    return (jnp.cos(phase_angle), jnp.sin(phase_angle))


def rotate_pair(real_part, imag_part, cosine, sine_part):
    return (real_part * cosine - imag_part * sine_part, real_part * sine_part + imag_part * cosine)


def times_pair(first_pair, second_pair, conj_second):
    factor = -1.0 if conj_second else 1.0
    real_part = first_pair[0] * second_pair[0] - factor * first_pair[1] * second_pair[1]
    imag_part = first_pair[1] * second_pair[0] + factor * first_pair[0] * second_pair[1]
    return (real_part, imag_part)


def unpack_fields(spectrum, comp_axis, field_axis):
    collected = []
    for partner_rank in range(spectrum.shape[field_axis]):
        single = lax.index_in_dim(spectrum, partner_rank, field_axis, keepdims=True)
        collected.append(
            (
                lax.index_in_dim(single, 0, comp_axis, keepdims=True),
                lax.index_in_dim(single, 1, comp_axis, keepdims=True),
            )
        )
    return collected


def pack_fields(pairs, comp_axis, field_axis):
    return jnp.concatenate(
        [jnp.concatenate([real_part, imag_part], axis=comp_axis) for real_part, imag_part in pairs],
        axis=field_axis,
    )


def spread_forward(regroup, fields):
    row_count, field_count, channels = fields.shape
    part_count = lax.axis_size("ctx")
    block_rows = row_count // part_count
    length = 2 * part_count * row_count
    my_index = lax.axis_index("ctx")
    gathered = regroup(fields.reshape(part_count, 1, block_rows, field_count, channels))
    cosine, sine_part = phase_pair(2 * part_count, part_count, 2 * part_count, -1.0)
    first_table = jnp.stack([cosine, sine_part], axis=1)
    first_pass = jnp.einsum("kda,arfc->kdrfc", first_table, gathered, precision=HIGHEST_PREC)
    row_index = my_index * block_rows + jnp.arange(block_rows, dtype=jnp.int32)
    twist_index = jnp.arange(2 * part_count, dtype=jnp.int32)[:, None] * row_index[None, :] % length
    phase_angle = -TWO_PI / length * twist_index.astype(jnp.float32)
    cos_twist = jnp.cos(phase_angle)[:, :, None, None]
    sin_twist = jnp.sin(phase_angle)[:, :, None, None]
    real_part, imag_part = rotate_pair(first_pass[:, 0], first_pass[:, 1], cos_twist, sin_twist)
    turned = jnp.stack([real_part, imag_part], axis=1)
    arrived = regroup(turned.reshape(part_count, 1, 2, 2, block_rows, field_count, channels))
    cosine, sine_part = phase_pair(row_count, row_count, row_count, -1.0)
    second_table = jnp.stack(
        [jnp.stack([cosine, sine_part], axis=-1), jnp.stack([-sine_part, cosine], axis=-1)], axis=0
    )
    second_table = second_table.reshape(2, part_count, block_rows, row_count, 2)
    return jnp.einsum("pqsrfc,sprkd->qkdfc", arrived, second_table, precision=HIGHEST_PREC)


def spread_inverse(regroup, spectrum):
    pair_count, row_count, _, field_count, channels = spectrum.shape
    part_count = lax.axis_size("ctx")
    block_rows = row_count // part_count
    length = 2 * part_count * row_count
    my_index = lax.axis_index("ctx")
    cosine, sine_part = phase_pair(row_count, row_count, row_count, 1.0)
    second_table = jnp.stack(
        [jnp.stack([cosine, sine_part], axis=-1), jnp.stack([-sine_part, cosine], axis=-1)], axis=0
    )
    second_table = second_table.reshape(2, row_count, part_count, block_rows, 2)
    row_parts = jnp.einsum("qkdfc,dkprs->pqsrfc", spectrum, second_table, precision=HIGHEST_PREC)
    freq_index = my_index * pair_count + jnp.arange(pair_count, dtype=jnp.int32)
    twist_index = freq_index[:, None] * jnp.arange(row_count, dtype=jnp.int32)[None, :] % length
    phase_angle = TWO_PI / length * twist_index.astype(jnp.float32)
    cos_twist = (
        jnp.cos(phase_angle)
        .reshape(pair_count, part_count, block_rows)
        .transpose(1, 0, 2)[:, :, :, None, None]
    )
    sin_twist = (
        jnp.sin(phase_angle)
        .reshape(pair_count, part_count, block_rows)
        .transpose(1, 0, 2)[:, :, :, None, None]
    )
    real_part, imag_part = rotate_pair(row_parts[:, :, 0], row_parts[:, :, 1], cos_twist, sin_twist)
    turned = jnp.stack([real_part, imag_part], axis=2)
    arrived = regroup(
        turned.reshape(part_count, 1, pair_count, 2, block_rows, field_count, channels)
    )
    cosine, sine_part = phase_pair(2 * part_count, part_count, 2 * part_count, 1.0)
    first_table = (jnp.stack([cosine, -sine_part], axis=1) / length).reshape(
        part_count, pair_count, 2, part_count
    )
    values = jnp.einsum("pqsrfc,pqsa->arfc", arrived, first_table, precision=HIGHEST_PREC)
    returned = regroup(values.reshape(part_count, 1, block_rows, field_count, channels))
    return returned.reshape(row_count, field_count, channels)


def local_general(query_in, key_in, value_in, long_filter, short_taps, out_grad):
    row_count = query_in.shape[0]
    tap_count = short_taps.shape[1]
    margin = tap_count - 1
    part_count = lax.axis_size("ctx")

    def regroup(blocks):
        return lax.all_to_all(blocks, "ctx", split_axis=0, concat_axis=1, tiled=True)[0]

    to_freq = partial(spread_forward, regroup)
    from_freq = partial(spread_inverse, regroup)
    comp_axis = 2
    field_axis = 3
    inputs = jnp.stack([query_in, key_in, value_in])
    earlier = passed_along(inputs[:, row_count - margin :], "ctx", 1)
    extended = jnp.concatenate([earlier, inputs], axis=1).astype(jnp.float32)
    tap_gain = short_taps.astype(jnp.float32)
    filtered = tap_gain[:, 0, None, :] * extended[:, margin:]
    for offset in range(1, tap_count):
        filtered = (
            filtered
            + tap_gain[:, offset, None, :]
            * extended[:, margin - offset : margin - offset + row_count]
        )
    query_filt = filtered[0]
    key_filt = filtered[1]
    value_filt = filtered[2]
    mixed_in = key_filt * value_filt
    spectra = to_freq(jnp.stack([mixed_in, long_filter.astype(jnp.float32)], axis=1))
    mixed_spec, filter_spec = unpack_fields(spectra, comp_axis, field_axis)
    convolved = from_freq(
        pack_fields([times_pair(mixed_spec, filter_spec, False)], comp_axis, field_axis)
    )[:, 0]
    output = (query_filt * convolved).astype(jnp.bfloat16)
    grad_in = out_grad.astype(jnp.float32)
    gate_grad = grad_in * convolved
    conv_grad = grad_in * query_filt
    grad_spec = unpack_fields(to_freq(conv_grad[:, None, :]), comp_axis, field_axis)[0]
    returned = from_freq(
        pack_fields(
            [times_pair(grad_spec, filter_spec, True), times_pair(grad_spec, mixed_spec, True)],
            comp_axis,
            field_axis,
        )
    )
    grad_scale = 1.0 / math.sqrt(part_count * row_count)
    mixed_grad = returned[:, 0]
    filter_grad = returned[:, 1] * grad_scale
    grad_stack = jnp.stack([gate_grad, mixed_grad * value_filt, mixed_grad * key_filt])
    later_rows = passed_along(grad_stack[:, :margin], "ctx", -1)
    padded_grad = jnp.concatenate([grad_stack, later_rows], axis=1)
    input_grads = tap_gain[:, 0, None, :] * grad_stack
    for offset in range(1, tap_count):
        input_grads = (
            input_grads + tap_gain[:, offset, None, :] * padded_grad[:, offset : offset + row_count]
        )
    partial_taps = jnp.stack(
        [
            jnp.sum(grad_stack * extended[:, margin - offset : margin - offset + row_count], axis=1)
            for offset in range(tap_count)
        ],
        axis=1,
    )
    taps_grad = lax.psum(partial_taps, "ctx") * grad_scale
    return (
        output,
        input_grads[0].astype(jnp.bfloat16),
        input_grads[1].astype(jnp.bfloat16),
        input_grads[2].astype(jnp.bfloat16),
        filter_grad,
        taps_grad,
    )


RADIX = 8
FIELDS = 5
CLASSES = (4, 2, 6, 1, 5, 9, 13)
LANES = 128
PAD = 8
CHUNK = 16
SENT = (0, 6, 2, 4, 5, 3, 7, 1)
BACK = (0, 6, 5, 2, 4, 3, 7, 1)
FINISHED = (0, 4, 6, 8)
REACH = 124.0
TINY = 1e-30
HEAD = 32
TAPS_AT = (10, 11, 12, 13, 14, 15, 28, 29, 30)


def split_pair(values):
    high = values.astype(jnp.bfloat16)
    low = (values - high.astype(jnp.float32)).astype(jnp.bfloat16)
    return high, low


@lru_cache(maxsize=None)
def class_tables(rows):
    length = 2 * RADIX * rows
    back = np.arange(rows)

    def waves(residue, count):
        angle = 2.0 * np.pi * (np.outer(2 * RADIX * np.arange(count) + residue, back) % length) / length
        return np.cos(angle), np.sin(angle)

    half = rows // 2
    cos0, sin0 = waves(0, half)
    cos8, sin8 = waves(RADIX, half)
    none = np.zeros((half, rows))
    middle = (1.0 - 2.0 * (back % 2))[None, :]
    imag0 = np.concatenate([middle, -sin0[1:]])
    forward = [np.block([[cos0, none], [none, cos8], [imag0, none], [none, -sin8]])]
    weight = np.full((2 * rows, 1), 2.0)
    weight[0] = weight[rows] = 1.0
    inverse = [(weight * forward[0]).T]
    for residue in CLASSES:
        cosine, sine = waves(residue, rows)
        forward.append(np.block([[cosine, sine], [-sine, cosine]]))
        inverse.append(2.0 * forward[-1].T)
    tables = []
    for table in (np.stack(forward), np.stack(inverse) / length):
        high = table.astype(ml_dtypes.bfloat16)
        low = (table - high.astype(np.float64)).astype(ml_dtypes.bfloat16)
        tables.append(np.stack([high, low]))
    return tables


ROOT = math.sqrt(0.5)
COS1 = math.cos(math.pi / 8)
SIN1 = math.sin(math.pi / 8)


def forward_classes(x):
    u = [x[a] + x[a + 4] for a in range(4)]
    d = [x[a] - x[a + 4] for a in range(4)]
    even, odd = u[0] + u[2], u[1] + u[3]
    dif, tot = ROOT * (d[1] - d[3]), ROOT * (d[1] + d[3])
    found = [
        (even + odd, even - odd),
        (u[0] - u[2], u[3] - u[1]),
        (d[0] + dif, -d[2] - tot),
        (d[0] - dif, d[2] - tot),
    ]
    w0 = (x[0], -x[4])
    w1 = (COS1 * x[1] - SIN1 * x[5], -SIN1 * x[1] - COS1 * x[5])
    w2 = (ROOT * (x[2] - x[6]), -ROOT * (x[2] + x[6]))
    w3 = (SIN1 * x[3] - COS1 * x[7], -COS1 * x[3] - SIN1 * x[7])
    s02 = (w0[0] + w2[0], w0[1] + w2[1])
    d02 = (w0[0] - w2[0], w0[1] - w2[1])
    s13 = (w1[0] + w3[0], w1[1] + w3[1])
    d13 = (w1[0] - w3[0], w1[1] - w3[1])
    found.append((s02[0] + s13[0], s02[1] + s13[1]))
    found.append((d02[0] + d13[1], d02[1] - d13[0]))
    found.append((s02[0] - s13[0], s02[1] - s13[1]))
    found.append((d02[0] - d13[1], d02[1] + d13[0]))
    return found


def inverse_classes(z):
    (z0, z8), (r4, i4), (r2, i2), (r6, i6) = z[:4]
    up, down = z0 + z8, z0 - z8
    even = [up + r4, down - i4, up - r4, down + i4]
    gap, tot = ROOT * (r2 - r6), ROOT * (i2 + i6)
    turn = [r2 + r6, gap - tot, i6 - i2, -gap - tot]
    (r1, i1), (r5, i5), (r9, i9), (rd, id_) = z[4:]
    s = (r1 + r9, i1 + i9)
    d = (r1 - r9, i1 - i9)
    t = (r5 + rd, i5 + id_)
    e = (r5 - rd, i5 - id_)
    s0 = (s[0] + t[0], s[1] + t[1])
    s2 = (s[0] - t[0], s[1] - t[1])
    s1 = (d[0] - e[1], d[1] + e[0])
    s3 = (d[0] + e[1], d[1] - e[0])
    q = [
        s0,
        (COS1 * s1[0] - SIN1 * s1[1], SIN1 * s1[0] + COS1 * s1[1]),
        (ROOT * (s2[0] - s2[1]), ROOT * (s2[0] + s2[1])),
        (SIN1 * s3[0] - COS1 * s3[1], COS1 * s3[0] + SIN1 * s3[1]),
    ]
    return [even[a] + turn[a] + q[a][0] for a in range(4)] + [
        even[a] - turn[a] - q[a][1] for a in range(4)
    ]


def log_code(values, inverse_scale):
    code = jnp.exp2(jnp.abs(values) * (inverse_scale * (2.0 * REACH)) - REACH)
    return jnp.where(values < 0.0, -code, code).astype(jnp.bfloat16)


def code_scale(peak):
    return jnp.maximum(peak * (1.0 + 2.0**-7), TINY).astype(jnp.bfloat16).astype(jnp.float32)


def log_decode(code, scale):
    code = code.astype(jnp.float32)
    values = (jnp.log2(jnp.abs(code)) + REACH) * (scale * (0.5 / REACH))
    return jnp.where(code < 0.0, -values, values)


def table_dot(table_ref, f, both):
    half = both.shape[1] // 2
    found = jnp.dot(table_ref[0, f], both, preferred_element_type=jnp.float32)
    rest = jnp.dot(table_ref[1, f], both[:, :half], preferred_element_type=jnp.float32)
    return found[:, :half] + (found[:, half:] + rest)


def times_spec(first, second, conj_second, packed):
    (ar, ai), (br, bi) = first, second
    inner = ai * bi
    cross = ai * br - ar * bi if conj_second else ai * br + ar * bi
    if packed:
        line = lax.broadcasted_iota(jnp.int32, inner.shape, 0) == 0
        cross = jnp.where(line, inner, cross)
        inner = jnp.where(line, 0.0, inner)
    return (ar * br + inner if conj_second else ar * br - inner), cross


def spec_parts(spec, rows, column):
    lanes = slice(column * LANES, (column + 1) * LANES)
    return spec[:rows, lanes], spec[rows:, lanes]


def side_by_side(products):
    pairs = [split_pair(jnp.concatenate(pair, axis=0)) for pair in products]
    return jnp.concatenate([high for high, _ in pairs] + [low for _, low in pairs], axis=1)


def put_classes(ref, column, columns, rows, b0, values):
    for f, pair in enumerate(forward_classes(values)):
        for part, value in enumerate(pair):
            high, low = split_pair(value)
            at = pl.ds(part * rows + b0, CHUNK)
            ref[f, at, pl.ds(column * LANES, LANES)] = high
            ref[f, at, pl.ds((columns + column) * LANES, LANES)] = low


def take_classes(ref, column, rows, b0):
    lanes = pl.ds(column * LANES, LANES)
    found = []
    for f in range(ref.shape[0]):
        pair = ref[f, pl.ds(b0, CHUNK), lanes], ref[f, pl.ds(rows + b0, CHUNK), lanes]
        found.append(pair)
    return inverse_classes(found)


def short_filter(gain, ref, at):
    return (
        gain[0] * ref[pl.ds(at, CHUNK), :]
        + gain[1] * ref[pl.ds(at - 1, CHUNK), :]
        + gain[2] * ref[pl.ds(at - 2, CHUNK), :]
    )


def widen(me_ref, got, targets, rows):
    def body(step, carry):
        b0 = pl.multiple_of(step * CHUNK, CHUNK)
        for k, ref in zip(SENT, got):
            at = pl.multiple_of((me_ref[0] ^ k) * rows + b0, CHUNK)
            for field, (target, pad) in enumerate(targets):
                target[pl.ds(pad + at, CHUNK), :] = ref[pl.ds(field * rows + b0, CHUNK), :].astype(
                    jnp.float32
                )
        return carry

    lax.fori_loop(0, rows // CHUNK, body, 0, unroll=8)


def gains(taps_ref):
    return [[taps_ref[3 * i + j : 3 * i + j + 1, :] for j in range(3)] for i in range(3)]


def layer_kernel(me_ref, gain_ref, forward_ref, inverse_ref, *refs):
    got, outs = refs[:RADIX], refs[RADIX : 2 * RADIX]
    qp, kp, vp, hs, cot, ks, vs, xs, xs_grad, spec, spec_grad, ys_conv, ys, zs_conv, zs, conv, mgrad, fgrad, peak, sums, head = refs[2 * RADIX :]
    rows = got[0].shape[0] // FIELDS
    total = RADIX * rows
    f32 = jnp.float32
    gain = gains(gain_ref)
    for ref in (qp, kp, vp):
        ref[pl.ds(0, PAD), :] = jnp.zeros((PAD, LANES), f32)
    for ref in (cot, ks, vs, conv, mgrad):
        ref[pl.ds(total, PAD), :] = jnp.zeros((PAD, LANES), f32)
    widen(me_ref, got, ((qp, PAD), (kp, PAD), (vp, PAD), (hs, 0), (cot, 0)), rows)

    chunks = range(0, rows, CHUNK)
    classes = range(xs.shape[0])
    for b0 in chunks:
        mixed = []
        for a in range(RADIX):
            at = a * rows + b0
            key_filt = short_filter(gain[1], kp, PAD + at)
            value_filt = short_filter(gain[2], vp, PAD + at)
            ks[pl.ds(at, CHUNK), :] = key_filt
            vs[pl.ds(at, CHUNK), :] = value_filt
            mixed.append(key_filt * value_filt)
        put_classes(xs, 0, 2, rows, b0, mixed)
        filt = [hs[pl.ds(a * rows + b0, CHUNK), :] for a in range(RADIX)]
        put_classes(xs, 1, 2, rows, b0, filt)
    for f, b0 in zip(classes, chunks):
        spec[f] = table_dot(forward_ref, f, xs[f])
        conv_grad = []
        for a in range(RADIX):
            at = a * rows + b0
            conv_grad.append(short_filter(gain[0], qp, PAD + at) * cot[pl.ds(at, CHUNK), :])
        put_classes(xs_grad, 0, 1, rows, b0, conv_grad)
    for f in classes:
        spec_grad[f] = table_dot(forward_ref, f, xs_grad[f])
        mixed, filt = [spec_parts(spec[f], rows, c) for c in range(2)]
        ys_conv[f] = side_by_side([times_spec(mixed, filt, False, f == 0)])
    for f in classes:
        zs_conv[f] = table_dot(inverse_ref, f, ys_conv[f])
        mixed, filt = [spec_parts(spec[f], rows, c) for c in range(2)]
        grad = spec_parts(spec_grad[f], rows, 0)
        ys[f] = side_by_side([times_spec(grad, one, True, f == 0) for one in (filt, mixed)])
    peak[...] = jnp.zeros_like(peak)
    sums[...] = jnp.zeros_like(sums)

    def take(column, b0, ref, source, place):
        found = take_classes(source, place, rows, b0)
        for a, value in enumerate(found):
            ref[pl.ds(a * rows + b0, CHUNK), :] = value
            size = jnp.abs(value)
            peak[column, a] = jnp.maximum(peak[column, a], jnp.maximum(size[:8], size[8:]))
        return found

    def add(i, b0, source, values, other):
        found = [jnp.zeros((CHUNK, LANES), f32)] * 3
        for a, value in enumerate(values):
            at = a * rows + b0
            now = value * other[pl.ds(at, CHUNK), :]
            for j in range(3):
                found[j] = found[j] + now * source[pl.ds(PAD + at - j, CHUNK), :]
        for j in range(3):
            sums[3 * i + j] += found[j][:8] + found[j][8:]

    for f, b0 in zip(classes, chunks):
        zs[f] = table_dot(inverse_ref, f, ys[f])
        add(0, b0, qp, take(0, b0, conv, zs_conv, 0), cot)
    for b0 in chunks:
        found = take(1, b0, mgrad, zs, 0)
        add(1, b0, kp, found, vs)
        add(2, b0, vp, found, ks)
        take(2, b0, fgrad, zs, 1)
    grad_scale = 1.0 / math.sqrt(total)
    head[...] = jnp.zeros_like(head)
    taps = [jnp.sum(sums[n], axis=0, keepdims=True) * grad_scale for n in range(9)]
    scale = code_scale(reduce(jnp.maximum, [jnp.abs(line) for line in taps]))
    head[pl.ds(9, 1), :] = scale
    for at, line in zip(TAPS_AT, taps):
        head[pl.ds(at, 1), :] = log_code(line, 1.0 / scale).astype(f32)
    for k, out_ref in zip(BACK, outs):
        a = me_ref[0] ^ k
        first = pl.multiple_of(a * rows, rows)
        after = first + rows
        for i, ref in enumerate((qp, kp, vp)):
            head[pl.ds(2 * i, 2), :] = ref[pl.ds(first + PAD - 2, 2), :]
        for column, ref in enumerate((conv, mgrad, fgrad)):
            top = jnp.max(peak[column, a], axis=0, keepdims=True)
            scale = code_scale(top)
            head[pl.ds(6 + column, 1), :] = scale
            out_ref[pl.ds(column * rows, rows), :] = log_code(
                ref[pl.ds(first, rows), :], 1.0 / scale
            )
        for i, (ref, other) in enumerate(((conv, cot), (mgrad, vs), (mgrad, ks))):
            head[pl.ds(16 + 2 * i, 2), :] = ref[pl.ds(after, 2), :] * other[pl.ds(after, 2), :]
        head[pl.ds(22, 6), :] = split_pair(head[pl.ds(16, 6), :])[1].astype(f32)
        out_ref[pl.ds(3 * rows, HEAD), :] = head[...].astype(jnp.bfloat16)


def prepare_kernel(
    me_ref, forward_any, inverse_any, taps_any, _, query_ref, key_ref, value_ref, cot_ref,
    forward_ref, inverse_ref, gain_ref, wide_ref, early_ref, wide, sem,
):
    lane = pl.ds(pl.multiple_of(me_ref[0] * LANES, LANES), LANES)
    copies = [
        pltpu.make_async_copy(forward_any.at[n], forward_ref.at[n], sem.at[n]) for n in range(2)
    ] + [
        pltpu.make_async_copy(inverse_any.at[n], inverse_ref.at[n], sem.at[2 + n]) for n in range(2)
    ]
    for copy in copies:
        copy.start()
    taps = taps_any[...].astype(jnp.float32)
    for i in range(3):
        for j in range(3):
            at = 3 * i + j
            wide_ref[at : at + 1, :] = taps[i, j : j + 1, :]
            gain_ref[at : at + 1, :] = wide_ref[at : at + 1, lane]
    rows = cot_ref.shape[0]
    for i, ref in enumerate((query_ref, key_ref, value_ref)):
        wide[pl.ds(0, PAD), :] = jnp.zeros((PAD, wide.shape[1]), jnp.float32)
        wide[pl.ds(PAD, rows), :] = ref[...].astype(jnp.float32)
        early_ref[i] = (
            wide_ref[3 * i : 3 * i + 1, :] * wide[pl.ds(PAD, rows), :]
            + wide_ref[3 * i + 1 : 3 * i + 2, :] * wide[pl.ds(PAD - 1, rows), :]
            + wide_ref[3 * i + 2 : 3 * i + 3, :] * wide[pl.ds(PAD - 2, rows), :]
        )
    early_ref[3] = cot_ref[...].astype(jnp.float32)
    for copy in copies:
        copy.wait()


def whole_vmem(count):
    return [pl.BlockSpec(memory_space=pltpu.VMEM)] * count


def whole_any(count):
    return [pl.BlockSpec(memory_space=pl.ANY)] * count


IN_SMEM = pl.BlockSpec(memory_space=pltpu.SMEM)


def pack_kernel(places, me_ref, *refs):
    sources, outs, land, sem = refs[:FIELDS], refs[FIELDS:-2], refs[-2], refs[-1]
    rows = sources[0].shape[0]
    copies = [
        pltpu.make_async_copy(source, land.at[field], sem.at[field])
        for field, source in enumerate(sources)
    ]
    for copy in copies:
        copy.start()
    for field, copy in enumerate(copies):
        copy.wait()
        for k, out_ref in zip(places, outs):
            lane = pl.multiple_of((me_ref[0] ^ k) * LANES, LANES)
            out_ref[pl.ds(field * rows, rows), :] = land[field, :, pl.ds(lane, LANES)]


def finish_blocks(me_ref, places, got, wide_ref, early_ref, outs, grads, stage, stage_filter, stage_taps, sem):
    rows = early_ref.shape[1]
    f32, bf16 = jnp.float32, jnp.bfloat16
    copies = []
    for n, (k, got_ref) in enumerate(zip(places, got)):
        lanes = pl.ds(pl.multiple_of((me_ref[0] ^ k) * LANES, LANES), LANES)
        head = got_ref[pl.ds(3 * rows, HEAD), :].astype(f32)
        conv, mixed_grad, filt = [
            log_decode(got_ref[pl.ds(c * rows, rows), :], head[6 + c : 7 + c]) for c in range(3)
        ]
        stage_filter[n] = filt * (1.0 / math.sqrt(RADIX * rows))
        pairs = head[16:22] + head[22:28]
        for c, at in enumerate(TAPS_AT):
            stage_taps[n, c // 3, c % 3 : c % 3 + 1, :] = log_decode(head[at : at + 1], head[9:10])
        line = lax.broadcasted_iota(jnp.int32, (PAD, LANES), 0)
        filtered = []
        gain = []
        for i in range(3):
            gain.append([wide_ref[3 * i + j : 3 * i + j + 1, lanes] for j in range(3)])
            before, last = head[2 * i : 2 * i + 1], head[2 * i + 1 : 2 * i + 2]
            top = early_ref[i, 0:PAD, lanes] + jnp.where(
                line == 0,
                gain[i][1] * last + gain[i][2] * before,
                jnp.where(line == 1, gain[i][2] * last, 0.0),
            )
            filtered.append(jnp.concatenate([top, early_ref[i, PAD:, lanes]], axis=0))
        stage[n, 0] = (filtered[0] * conv).astype(bf16)
        inner = (
            conv * early_ref[3, :, lanes],
            mixed_grad * filtered[2],
            mixed_grad * filtered[1],
        )
        for i in range(3):
            grads[i, pl.ds(0, rows), :] = inner[i]
            grads[i, pl.ds(rows, 2), :] = pairs[2 * i : 2 * i + 2]
            stage[n, 1 + i] = (
                gain[i][0] * inner[i]
                + gain[i][1] * grads[i, pl.ds(1, rows), :]
                + gain[i][2] * grads[i, pl.ds(2, rows), :]
            ).astype(bf16)
        for c, out in enumerate(outs):
            source = stage.at[n, c] if c < 4 else (stage_filter, stage_taps)[c - 4].at[n]
            target = out.at[:, lanes] if c < 5 else out.at[:, :, lanes]
            copies.append(pltpu.make_async_copy(source, target, sem.at[len(copies)]))
            copies[-1].start()
    return copies


def finish_kernel(places, begun, me_ref, *refs):
    count = len(places)
    got, (wide_ref, early_ref), refs = refs[:count], refs[count : count + 2], refs[count + 2 + begun :]
    for copy in finish_blocks(me_ref, places, got, wide_ref, early_ref, refs[:6], *refs[6:]):
        copy.wait()


def swap_blocks(places, blocks):
    devices = range(RADIX)
    return [
        lax.ppermute(block, "ctx", [(i, i ^ k) for i in devices]) if k else block
        for k, block in zip(places, blocks)
    ]


def held(arrays, space):
    return [pltpu.with_memory_space_constraint(jnp.asarray(one), space) for one in arrays]


def local_fast(query_in, key_in, value_in, long_filter, short_taps, out_grad):
    rows, channels = query_in.shape
    total = RADIX * rows
    f32, bf16 = jnp.float32, jnp.bfloat16
    shape = jax.ShapeDtypeStruct
    inputs = held((query_in, key_in, value_in, out_grad), pltpu.HBM)
    small = pltpu.CompilerParams(vmem_limit_bytes=12 * 1024 * 1024)
    me = lax.axis_index("ctx").astype(jnp.int32).reshape(1)
    sources = held((query_in, key_in, value_in, long_filter, out_grad), pltpu.HBM)

    def pack(places):
        return pl.pallas_call(
            partial(pack_kernel, places),
            out_shape=[pltpu.VMEM((FIELDS * rows, LANES), bf16)] * len(places),
            in_specs=[IN_SMEM] + whole_any(FIELDS),
            out_specs=whole_vmem(len(places)),
            scratch_shapes=[
                pltpu.VMEM((FIELDS, rows, channels), bf16),
                pltpu.SemaphoreType.DMA((FIELDS,)),
            ],
            compiler_params=small,
            name="pack",
        )(me, *sources)

    packed = pack(SENT)
    got = swap_blocks(SENT, packed)
    forward, inverse = class_tables(rows)
    count = 1 + len(CLASSES)
    ready = pl.pallas_call(
        prepare_kernel,
        out_shape=[
            pltpu.VMEM(forward.shape, bf16),
            pltpu.VMEM(inverse.shape, bf16),
            pltpu.VMEM((16, LANES), f32),
            pltpu.VMEM((16, channels), f32),
            pltpu.VMEM((4, rows, channels), f32),
        ],
        in_specs=[IN_SMEM] + whole_any(2) + whole_vmem(6),
        out_specs=whole_vmem(5),
        scratch_shapes=[pltpu.VMEM((PAD + rows, channels), f32), pltpu.SemaphoreType.DMA((4,))],
        compiler_params=small,
        name="prepare",
    )(me, *held((forward, inverse), pltpu.HBM), short_taps, *held(got[1:2], pltpu.VMEM), *inputs)
    ready = held(ready, pltpu.VMEM)
    done = pl.pallas_call(
        layer_kernel,
        out_shape=[pltpu.VMEM((3 * rows + HEAD, LANES), bf16)] * RADIX,
        in_specs=[IN_SMEM] + whole_vmem(3 + RADIX),
        out_specs=whole_vmem(RADIX),
        scratch_shapes=[pltpu.VMEM((total + PAD, LANES), f32)] * 7
        + [
            pltpu.VMEM((count, 2 * rows, columns * LANES), kind)
            for columns, kind in (
                (4, bf16), (2, bf16), (2, f32), (1, f32), (2, bf16), (4, bf16), (1, f32), (2, f32)
            )
        ]
        + [pltpu.VMEM((total + PAD, LANES), f32)] * 3
        + [
            pltpu.VMEM((3, RADIX, 8, LANES), f32),
            pltpu.VMEM((9, 8, LANES), f32),
            pltpu.VMEM((HEAD, LANES), f32),
        ],
        compiler_params=pltpu.CompilerParams(vmem_limit_bytes=20 * 1024 * 1024),
        name="layer",
    )(me, ready[2], *ready[:2], *held(got, pltpu.VMEM))
    back = held(swap_blocks(BACK, done), pltpu.VMEM)
    results = [shape((rows, channels), bf16)] * 4 + [
        shape((rows, channels), f32),
        shape((3, 3, channels), f32),
    ]

    begun = []
    for first, last in zip(FINISHED, FINISHED[1:]):
        count = last - first
        begun = pl.pallas_call(
            partial(finish_kernel, BACK[first:last], len(begun)),
            out_shape=results,
            in_specs=[IN_SMEM] + whole_vmem(count + 2) + whole_any(len(begun)),
            out_specs=whole_any(6),
            scratch_shapes=[
                pltpu.VMEM((3, rows + PAD, LANES), f32),
                pltpu.VMEM((count, 4, rows, LANES), bf16),
                pltpu.VMEM((count, rows, LANES), f32),
                pltpu.VMEM((count, 3, 3, LANES), f32),
                pltpu.SemaphoreType.DMA((6 * count,)),
            ],
            input_output_aliases={count + 3 + n: n for n in range(len(begun))},
            compiler_params=small,
            name="finish",
        )(me, *back[first:last], *ready[3:], *begun)
    return tuple(begun)


def local(query_in, key_in, value_in, long_filter, short_taps, out_grad):
    rows, channels = query_in.shape
    blocks = lax.axis_size("ctx")
    taps = short_taps.shape[:2]
    if blocks == RADIX and channels == blocks * LANES and rows == LANES and taps == (3, 3):
        return local_fast(query_in, key_in, value_in, long_filter, short_taps, out_grad)
    return local_general(query_in, key_in, value_in, long_filter, short_taps, out_grad)


def solution(mesh):
    placed = (
        P("ctx", "tp"),
        P("ctx", "tp"),
        P("ctx", "tp"),
        P("ctx", "tp"),
        P(None, None, "tp"),
        P("ctx", "tp"),
    )
    return jax.shard_map(
        local,
        mesh=mesh,
        in_specs=placed,
        out_specs=(
            P("ctx", "tp"),
            P("ctx", "tp"),
            P("ctx", "tp"),
            P("ctx", "tp"),
            P("ctx", "tp"),
            P(None, None, "tp"),
        ),
        check_vma=False,
    )
```

```python
from functools import lru_cache, partial, reduce
import math

import jax
import jax.numpy as jnp
import ml_dtypes
import numpy as np
from jax import lax
from jax.experimental import pallas as pl
from jax.experimental.pallas import tpu as pltpu
from jax.sharding import PartitionSpec as P

HIGHEST_PREC = lax.Precision.HIGHEST
TWO_PI = 2.0 * math.pi


def passed_along(block, axis, distance):
    devices = range(lax.axis_size(axis))
    route = [(i - distance, i) for i in devices if i - distance in devices]
    return lax.ppermute(block, axis, route)


def phase_pair(count_a, count_b, period, direction):
    product = (
        jnp.arange(count_a, dtype=jnp.int32)[:, None]
        * jnp.arange(count_b, dtype=jnp.int32)[None, :]
    )
    phase_angle = direction * TWO_PI / period * (product % period).astype(jnp.float32)
    return (jnp.cos(phase_angle), jnp.sin(phase_angle))


def rotate_pair(real_part, imag_part, cosine, sine_part):
    return (real_part * cosine - imag_part * sine_part, real_part * sine_part + imag_part * cosine)


def times_pair(first_pair, second_pair, conj_second):
    factor = -1.0 if conj_second else 1.0
    real_part = first_pair[0] * second_pair[0] - factor * first_pair[1] * second_pair[1]
    imag_part = first_pair[1] * second_pair[0] + factor * first_pair[0] * second_pair[1]
    return (real_part, imag_part)


def unpack_fields(spectrum, comp_axis, field_axis):
    collected = []
    for partner_rank in range(spectrum.shape[field_axis]):
        single = lax.index_in_dim(spectrum, partner_rank, field_axis, keepdims=True)
        collected.append(
            (
                lax.index_in_dim(single, 0, comp_axis, keepdims=True),
                lax.index_in_dim(single, 1, comp_axis, keepdims=True),
            )
        )
    return collected


def pack_fields(pairs, comp_axis, field_axis):
    return jnp.concatenate(
        [jnp.concatenate([real_part, imag_part], axis=comp_axis) for real_part, imag_part in pairs],
        axis=field_axis,
    )


def spread_forward(regroup, fields):
    row_count, field_count, channels = fields.shape
    part_count = lax.axis_size("ctx")
    block_rows = row_count // part_count
    length = 2 * part_count * row_count
    my_index = lax.axis_index("ctx")
    gathered = regroup(fields.reshape(part_count, 1, block_rows, field_count, channels))
    cosine, sine_part = phase_pair(2 * part_count, part_count, 2 * part_count, -1.0)
    first_table = jnp.stack([cosine, sine_part], axis=1)
    first_pass = jnp.einsum("kda,arfc->kdrfc", first_table, gathered, precision=HIGHEST_PREC)
    row_index = my_index * block_rows + jnp.arange(block_rows, dtype=jnp.int32)
    twist_index = jnp.arange(2 * part_count, dtype=jnp.int32)[:, None] * row_index[None, :] % length
    phase_angle = -TWO_PI / length * twist_index.astype(jnp.float32)
    cos_twist = jnp.cos(phase_angle)[:, :, None, None]
    sin_twist = jnp.sin(phase_angle)[:, :, None, None]
    real_part, imag_part = rotate_pair(first_pass[:, 0], first_pass[:, 1], cos_twist, sin_twist)
    turned = jnp.stack([real_part, imag_part], axis=1)
    arrived = regroup(turned.reshape(part_count, 1, 2, 2, block_rows, field_count, channels))
    cosine, sine_part = phase_pair(row_count, row_count, row_count, -1.0)
    second_table = jnp.stack(
        [jnp.stack([cosine, sine_part], axis=-1), jnp.stack([-sine_part, cosine], axis=-1)], axis=0
    )
    second_table = second_table.reshape(2, part_count, block_rows, row_count, 2)
    return jnp.einsum("pqsrfc,sprkd->qkdfc", arrived, second_table, precision=HIGHEST_PREC)


def spread_inverse(regroup, spectrum):
    pair_count, row_count, _, field_count, channels = spectrum.shape
    part_count = lax.axis_size("ctx")
    block_rows = row_count // part_count
    length = 2 * part_count * row_count
    my_index = lax.axis_index("ctx")
    cosine, sine_part = phase_pair(row_count, row_count, row_count, 1.0)
    second_table = jnp.stack(
        [jnp.stack([cosine, sine_part], axis=-1), jnp.stack([-sine_part, cosine], axis=-1)], axis=0
    )
    second_table = second_table.reshape(2, row_count, part_count, block_rows, 2)
    row_parts = jnp.einsum("qkdfc,dkprs->pqsrfc", spectrum, second_table, precision=HIGHEST_PREC)
    freq_index = my_index * pair_count + jnp.arange(pair_count, dtype=jnp.int32)
    twist_index = freq_index[:, None] * jnp.arange(row_count, dtype=jnp.int32)[None, :] % length
    phase_angle = TWO_PI / length * twist_index.astype(jnp.float32)
    cos_twist = (
        jnp.cos(phase_angle)
        .reshape(pair_count, part_count, block_rows)
        .transpose(1, 0, 2)[:, :, :, None, None]
    )
    sin_twist = (
        jnp.sin(phase_angle)
        .reshape(pair_count, part_count, block_rows)
        .transpose(1, 0, 2)[:, :, :, None, None]
    )
    real_part, imag_part = rotate_pair(row_parts[:, :, 0], row_parts[:, :, 1], cos_twist, sin_twist)
    turned = jnp.stack([real_part, imag_part], axis=2)
    arrived = regroup(
        turned.reshape(part_count, 1, pair_count, 2, block_rows, field_count, channels)
    )
    cosine, sine_part = phase_pair(2 * part_count, part_count, 2 * part_count, 1.0)
    first_table = (jnp.stack([cosine, -sine_part], axis=1) / length).reshape(
        part_count, pair_count, 2, part_count
    )
    values = jnp.einsum("pqsrfc,pqsa->arfc", arrived, first_table, precision=HIGHEST_PREC)
    returned = regroup(values.reshape(part_count, 1, block_rows, field_count, channels))
    return returned.reshape(row_count, field_count, channels)


def local_general(query_in, key_in, value_in, long_filter, short_taps, out_grad):
    row_count = query_in.shape[0]
    tap_count = short_taps.shape[1]
    margin = tap_count - 1
    part_count = lax.axis_size("ctx")

    def regroup(blocks):
        return lax.all_to_all(blocks, "ctx", split_axis=0, concat_axis=1, tiled=True)[0]

    to_freq = partial(spread_forward, regroup)
    from_freq = partial(spread_inverse, regroup)
    comp_axis = 2
    field_axis = 3
    inputs = jnp.stack([query_in, key_in, value_in])
    earlier = passed_along(inputs[:, row_count - margin :], "ctx", 1)
    extended = jnp.concatenate([earlier, inputs], axis=1).astype(jnp.float32)
    tap_gain = short_taps.astype(jnp.float32)
    filtered = tap_gain[:, 0, None, :] * extended[:, margin:]
    for offset in range(1, tap_count):
        filtered = (
            filtered
            + tap_gain[:, offset, None, :]
            * extended[:, margin - offset : margin - offset + row_count]
        )
    query_filt = filtered[0]
    key_filt = filtered[1]
    value_filt = filtered[2]
    mixed_in = key_filt * value_filt
    spectra = to_freq(jnp.stack([mixed_in, long_filter.astype(jnp.float32)], axis=1))
    mixed_spec, filter_spec = unpack_fields(spectra, comp_axis, field_axis)
    convolved = from_freq(
        pack_fields([times_pair(mixed_spec, filter_spec, False)], comp_axis, field_axis)
    )[:, 0]
    output = (query_filt * convolved).astype(jnp.bfloat16)
    grad_in = out_grad.astype(jnp.float32)
    gate_grad = grad_in * convolved
    conv_grad = grad_in * query_filt
    grad_spec = unpack_fields(to_freq(conv_grad[:, None, :]), comp_axis, field_axis)[0]
    returned = from_freq(
        pack_fields(
            [times_pair(grad_spec, filter_spec, True), times_pair(grad_spec, mixed_spec, True)],
            comp_axis,
            field_axis,
        )
    )
    grad_scale = 1.0 / math.sqrt(part_count * row_count)
    mixed_grad = returned[:, 0]
    filter_grad = returned[:, 1] * grad_scale
    grad_stack = jnp.stack([gate_grad, mixed_grad * value_filt, mixed_grad * key_filt])
    later_rows = passed_along(grad_stack[:, :margin], "ctx", -1)
    padded_grad = jnp.concatenate([grad_stack, later_rows], axis=1)
    input_grads = tap_gain[:, 0, None, :] * grad_stack
    for offset in range(1, tap_count):
        input_grads = (
            input_grads + tap_gain[:, offset, None, :] * padded_grad[:, offset : offset + row_count]
        )
    partial_taps = jnp.stack(
        [
            jnp.sum(grad_stack * extended[:, margin - offset : margin - offset + row_count], axis=1)
            for offset in range(tap_count)
        ],
        axis=1,
    )
    taps_grad = lax.psum(partial_taps, "ctx") * grad_scale
    return (
        output,
        input_grads[0].astype(jnp.bfloat16),
        input_grads[1].astype(jnp.bfloat16),
        input_grads[2].astype(jnp.bfloat16),
        filter_grad,
        taps_grad,
    )


RADIX = 8
FIELDS = 5
CLASSES = (4, 2, 6, 1, 5, 9, 13)
LANES = 128
PAD = 8
CHUNK = 16
SENT = (0, 6, 2, 4, 5, 3, 7, 1)
BACK = (0, 6, 5, 2, 4, 3, 7, 1)
FINISHED = (0, 4, 6, 8)
REACH = 124.0
TINY = 1e-30
HEAD = 32
TAPS_AT = (10, 11, 12, 13, 14, 15, 28, 29, 30)


def split_pair(values):
    high = values.astype(jnp.bfloat16)
    low = (values - high.astype(jnp.float32)).astype(jnp.bfloat16)
    return high, low


@lru_cache(maxsize=None)
def class_tables(rows):
    length = 2 * RADIX * rows
    back = np.arange(rows)

    def waves(residue, count):
        angle = 2.0 * np.pi * (np.outer(2 * RADIX * np.arange(count) + residue, back) % length) / length
        return np.cos(angle), np.sin(angle)

    half = rows // 2
    cos0, sin0 = waves(0, half)
    cos8, sin8 = waves(RADIX, half)
    none = np.zeros((half, rows))
    middle = (1.0 - 2.0 * (back % 2))[None, :]
    imag0 = np.concatenate([middle, -sin0[1:]])
    forward = [np.block([[cos0, none], [none, cos8], [imag0, none], [none, -sin8]])]
    weight = np.full((2 * rows, 1), 2.0)
    weight[0] = weight[rows] = 1.0
    inverse = [(weight * forward[0]).T]
    for residue in CLASSES:
        cosine, sine = waves(residue, rows)
        forward.append(np.block([[cosine, sine], [-sine, cosine]]))
        inverse.append(2.0 * forward[-1].T)
    tables = []
    for table in (np.stack(forward), np.stack(inverse) / length):
        high = table.astype(ml_dtypes.bfloat16)
        low = (table - high.astype(np.float64)).astype(ml_dtypes.bfloat16)
        tables.append(np.stack([high, low]))
    return tables


ROOT = math.sqrt(0.5)
COS1 = math.cos(math.pi / 8)
SIN1 = math.sin(math.pi / 8)


def forward_classes(x):
    u = [x[a] + x[a + 4] for a in range(4)]
    d = [x[a] - x[a + 4] for a in range(4)]
    even, odd = u[0] + u[2], u[1] + u[3]
    dif, tot = ROOT * (d[1] - d[3]), ROOT * (d[1] + d[3])
    found = [
        (even + odd, even - odd),
        (u[0] - u[2], u[3] - u[1]),
        (d[0] + dif, -d[2] - tot),
        (d[0] - dif, d[2] - tot),
    ]
    w0 = (x[0], -x[4])
    w1 = (COS1 * x[1] - SIN1 * x[5], -SIN1 * x[1] - COS1 * x[5])
    w2 = (ROOT * (x[2] - x[6]), -ROOT * (x[2] + x[6]))
    w3 = (SIN1 * x[3] - COS1 * x[7], -COS1 * x[3] - SIN1 * x[7])
    s02 = (w0[0] + w2[0], w0[1] + w2[1])
    d02 = (w0[0] - w2[0], w0[1] - w2[1])
    s13 = (w1[0] + w3[0], w1[1] + w3[1])
    d13 = (w1[0] - w3[0], w1[1] - w3[1])
    found.append((s02[0] + s13[0], s02[1] + s13[1]))
    found.append((d02[0] + d13[1], d02[1] - d13[0]))
    found.append((s02[0] - s13[0], s02[1] - s13[1]))
    found.append((d02[0] - d13[1], d02[1] + d13[0]))
    return found


def inverse_classes(z):
    (z0, z8), (r4, i4), (r2, i2), (r6, i6) = z[:4]
    up, down = z0 + z8, z0 - z8
    even = [up + r4, down - i4, up - r4, down + i4]
    gap, tot = ROOT * (r2 - r6), ROOT * (i2 + i6)
    turn = [r2 + r6, gap - tot, i6 - i2, -gap - tot]
    (r1, i1), (r5, i5), (r9, i9), (rd, id_) = z[4:]
    s = (r1 + r9, i1 + i9)
    d = (r1 - r9, i1 - i9)
    t = (r5 + rd, i5 + id_)
    e = (r5 - rd, i5 - id_)
    s0 = (s[0] + t[0], s[1] + t[1])
    s2 = (s[0] - t[0], s[1] - t[1])
    s1 = (d[0] - e[1], d[1] + e[0])
    s3 = (d[0] + e[1], d[1] - e[0])
    q = [
        s0,
        (COS1 * s1[0] - SIN1 * s1[1], SIN1 * s1[0] + COS1 * s1[1]),
        (ROOT * (s2[0] - s2[1]), ROOT * (s2[0] + s2[1])),
        (SIN1 * s3[0] - COS1 * s3[1], COS1 * s3[0] + SIN1 * s3[1]),
    ]
    return [even[a] + turn[a] + q[a][0] for a in range(4)] + [
        even[a] - turn[a] - q[a][1] for a in range(4)
    ]


def log_code(values, inverse_scale):
    code = jnp.exp2(jnp.abs(values) * (inverse_scale * (2.0 * REACH)) - REACH)
    return jnp.where(values < 0.0, -code, code).astype(jnp.bfloat16)


def code_scale(peak):
    return jnp.maximum(peak * (1.0 + 2.0**-7), TINY).astype(jnp.bfloat16).astype(jnp.float32)


def log_decode(code, scale):
    code = code.astype(jnp.float32)
    values = (jnp.log2(jnp.abs(code)) + REACH) * (scale * (0.5 / REACH))
    return jnp.where(code < 0.0, -values, values)


def table_dot(table_ref, f, both):
    half = both.shape[1] // 2
    found = jnp.dot(table_ref[0, f], both, preferred_element_type=jnp.float32)
    rest = jnp.dot(table_ref[1, f], both[:, :half], preferred_element_type=jnp.float32)
    return found[:, :half] + (found[:, half:] + rest)


def times_spec(first, second, conj_second, packed):
    (ar, ai), (br, bi) = first, second
    inner = ai * bi
    cross = ai * br - ar * bi if conj_second else ai * br + ar * bi
    if packed:
        line = lax.broadcasted_iota(jnp.int32, inner.shape, 0) == 0
        cross = jnp.where(line, inner, cross)
        inner = jnp.where(line, 0.0, inner)
    return (ar * br + inner if conj_second else ar * br - inner), cross


def spec_parts(spec, rows, column):
    lanes = slice(column * LANES, (column + 1) * LANES)
    return spec[:rows, lanes], spec[rows:, lanes]


def side_by_side(products):
    pairs = [split_pair(jnp.concatenate(pair, axis=0)) for pair in products]
    return jnp.concatenate([high for high, _ in pairs] + [low for _, low in pairs], axis=1)


def put_classes(ref, column, columns, rows, b0, values):
    for f, pair in enumerate(forward_classes(values)):
        for part, value in enumerate(pair):
            high, low = split_pair(value)
            at = pl.ds(part * rows + b0, CHUNK)
            ref[f, at, pl.ds(column * LANES, LANES)] = high
            ref[f, at, pl.ds((columns + column) * LANES, LANES)] = low


def take_classes(ref, column, rows, b0):
    lanes = pl.ds(column * LANES, LANES)
    found = []
    for f in range(ref.shape[0]):
        pair = ref[f, pl.ds(b0, CHUNK), lanes], ref[f, pl.ds(rows + b0, CHUNK), lanes]
        found.append(pair)
    return inverse_classes(found)


def short_filter(gain, ref, at):
    return (
        gain[0] * ref[pl.ds(at, CHUNK), :]
        + gain[1] * ref[pl.ds(at - 1, CHUNK), :]
        + gain[2] * ref[pl.ds(at - 2, CHUNK), :]
    )


def widen(me_ref, got, targets, rows):
    def body(step, carry):
        b0 = pl.multiple_of(step * CHUNK, CHUNK)
        for k, ref in zip(SENT, got):
            at = pl.multiple_of((me_ref[0] ^ k) * rows + b0, CHUNK)
            for field, (target, pad) in enumerate(targets):
                target[pl.ds(pad + at, CHUNK), :] = ref[pl.ds(field * rows + b0, CHUNK), :].astype(
                    jnp.float32
                )
        return carry

    lax.fori_loop(0, rows // CHUNK, body, 0, unroll=8)


def gains(taps_ref):
    return [[taps_ref[3 * i + j : 3 * i + j + 1, :] for j in range(3)] for i in range(3)]


def layer_kernel(me_ref, gain_ref, forward_ref, inverse_ref, *refs):
    got, outs = refs[:RADIX], refs[RADIX : 2 * RADIX]
    qp, kp, vp, hs, cot, ks, vs, xs, xs_grad, spec, spec_grad, ys_conv, ys, zs_conv, zs, conv, mgrad, fgrad, peak, sums, head = refs[2 * RADIX :]
    rows = got[0].shape[0] // FIELDS
    total = RADIX * rows
    f32 = jnp.float32
    gain = gains(gain_ref)
    for ref in (qp, kp, vp):
        ref[pl.ds(0, PAD), :] = jnp.zeros((PAD, LANES), f32)
    for ref in (cot, ks, vs, conv, mgrad):
        ref[pl.ds(total, PAD), :] = jnp.zeros((PAD, LANES), f32)
    widen(me_ref, got, ((qp, PAD), (kp, PAD), (vp, PAD), (hs, 0), (cot, 0)), rows)

    chunks = range(0, rows, CHUNK)
    classes = range(xs.shape[0])
    for b0 in chunks:
        mixed = []
        for a in range(RADIX):
            at = a * rows + b0
            key_filt = short_filter(gain[1], kp, PAD + at)
            value_filt = short_filter(gain[2], vp, PAD + at)
            ks[pl.ds(at, CHUNK), :] = key_filt
            vs[pl.ds(at, CHUNK), :] = value_filt
            mixed.append(key_filt * value_filt)
        put_classes(xs, 0, 2, rows, b0, mixed)
        filt = [hs[pl.ds(a * rows + b0, CHUNK), :] for a in range(RADIX)]
        put_classes(xs, 1, 2, rows, b0, filt)
    for f, b0 in zip(classes, chunks):
        spec[f] = table_dot(forward_ref, f, xs[f])
        conv_grad = []
        for a in range(RADIX):
            at = a * rows + b0
            conv_grad.append(short_filter(gain[0], qp, PAD + at) * cot[pl.ds(at, CHUNK), :])
        put_classes(xs_grad, 0, 1, rows, b0, conv_grad)
    for f in classes:
        spec_grad[f] = table_dot(forward_ref, f, xs_grad[f])
        mixed, filt = [spec_parts(spec[f], rows, c) for c in range(2)]
        ys_conv[f] = side_by_side([times_spec(mixed, filt, False, f == 0)])
    for f in classes:
        zs_conv[f] = table_dot(inverse_ref, f, ys_conv[f])
        mixed, filt = [spec_parts(spec[f], rows, c) for c in range(2)]
        grad = spec_parts(spec_grad[f], rows, 0)
        ys[f] = side_by_side([times_spec(grad, one, True, f == 0) for one in (filt, mixed)])
    peak[...] = jnp.zeros_like(peak)
    sums[...] = jnp.zeros_like(sums)

    def take(column, b0, ref, source, place):
        found = take_classes(source, place, rows, b0)
        for a, value in enumerate(found):
            ref[pl.ds(a * rows + b0, CHUNK), :] = value
            size = jnp.abs(value)
            peak[column, a] = jnp.maximum(peak[column, a], jnp.maximum(size[:8], size[8:]))
        return found

    def add(i, b0, source, values, other):
        found = [jnp.zeros((CHUNK, LANES), f32)] * 3
        for a, value in enumerate(values):
            at = a * rows + b0
            now = value * other[pl.ds(at, CHUNK), :]
            for j in range(3):
                found[j] = found[j] + now * source[pl.ds(PAD + at - j, CHUNK), :]
        for j in range(3):
            sums[3 * i + j] += found[j][:8] + found[j][8:]

    for f, b0 in zip(classes, chunks):
        zs[f] = table_dot(inverse_ref, f, ys[f])
        add(0, b0, qp, take(0, b0, conv, zs_conv, 0), cot)
    for b0 in chunks:
        found = take(1, b0, mgrad, zs, 0)
        add(1, b0, kp, found, vs)
        add(2, b0, vp, found, ks)
        take(2, b0, fgrad, zs, 1)
    grad_scale = 1.0 / math.sqrt(total)
    head[...] = jnp.zeros_like(head)
    taps = [jnp.sum(sums[n], axis=0, keepdims=True) * grad_scale for n in range(9)]
    scale = code_scale(reduce(jnp.maximum, [jnp.abs(line) for line in taps]))
    head[pl.ds(9, 1), :] = scale
    for at, line in zip(TAPS_AT, taps):
        head[pl.ds(at, 1), :] = log_code(line, 1.0 / scale).astype(f32)
    for k, out_ref in zip(BACK, outs):
        a = me_ref[0] ^ k
        first = pl.multiple_of(a * rows, rows)
        after = first + rows
        for i, ref in enumerate((qp, kp, vp)):
            head[pl.ds(2 * i, 2), :] = ref[pl.ds(first + PAD - 2, 2), :]
        for column, ref in enumerate((conv, mgrad, fgrad)):
            top = jnp.max(peak[column, a], axis=0, keepdims=True)
            scale = code_scale(top)
            head[pl.ds(6 + column, 1), :] = scale
            out_ref[pl.ds(column * rows, rows), :] = log_code(
                ref[pl.ds(first, rows), :], 1.0 / scale
            )
        for i, (ref, other) in enumerate(((conv, cot), (mgrad, vs), (mgrad, ks))):
            head[pl.ds(16 + 2 * i, 2), :] = ref[pl.ds(after, 2), :] * other[pl.ds(after, 2), :]
        head[pl.ds(22, 6), :] = split_pair(head[pl.ds(16, 6), :])[1].astype(f32)
        out_ref[pl.ds(3 * rows, HEAD), :] = head[...].astype(jnp.bfloat16)


def prepare_kernel(
    me_ref, forward_any, inverse_any, taps_any, _, query_ref, key_ref, value_ref, cot_ref,
    forward_ref, inverse_ref, gain_ref, wide_ref, early_ref, wide, sem,
):
    lane = pl.ds(pl.multiple_of(me_ref[0] * LANES, LANES), LANES)
    copies = [
        pltpu.make_async_copy(forward_any.at[n], forward_ref.at[n], sem.at[n]) for n in range(2)
    ] + [
        pltpu.make_async_copy(inverse_any.at[n], inverse_ref.at[n], sem.at[2 + n]) for n in range(2)
    ]
    for copy in copies:
        copy.start()
    taps = taps_any[...].astype(jnp.float32)
    for i in range(3):
        for j in range(3):
            at = 3 * i + j
            wide_ref[at : at + 1, :] = taps[i, j : j + 1, :]
            gain_ref[at : at + 1, :] = wide_ref[at : at + 1, lane]
    rows = cot_ref.shape[0]
    for i, ref in enumerate((query_ref, key_ref, value_ref)):
        wide[pl.ds(0, PAD), :] = jnp.zeros((PAD, wide.shape[1]), jnp.float32)
        wide[pl.ds(PAD, rows), :] = ref[...].astype(jnp.float32)
        early_ref[i] = (
            wide_ref[3 * i : 3 * i + 1, :] * wide[pl.ds(PAD, rows), :]
            + wide_ref[3 * i + 1 : 3 * i + 2, :] * wide[pl.ds(PAD - 1, rows), :]
            + wide_ref[3 * i + 2 : 3 * i + 3, :] * wide[pl.ds(PAD - 2, rows), :]
        )
    early_ref[3] = cot_ref[...].astype(jnp.float32)
    for copy in copies:
        copy.wait()


def whole_vmem(count):
    return [pl.BlockSpec(memory_space=pltpu.VMEM)] * count


def whole_any(count):
    return [pl.BlockSpec(memory_space=pl.ANY)] * count


IN_SMEM = pl.BlockSpec(memory_space=pltpu.SMEM)


def pack_kernel(places, me_ref, *refs):
    sources, outs, land, sem = refs[:FIELDS], refs[FIELDS:-2], refs[-2], refs[-1]
    rows = sources[0].shape[0]
    copies = [
        pltpu.make_async_copy(source, land.at[field], sem.at[field])
        for field, source in enumerate(sources)
    ]
    for copy in copies:
        copy.start()
    for field, copy in enumerate(copies):
        copy.wait()
        for k, out_ref in zip(places, outs):
            lane = pl.multiple_of((me_ref[0] ^ k) * LANES, LANES)
            out_ref[pl.ds(field * rows, rows), :] = land[field, :, pl.ds(lane, LANES)]


def finish_blocks(me_ref, places, got, wide_ref, early_ref, outs, grads, stage, stage_filter, stage_taps, sem):
    rows = early_ref.shape[1]
    f32, bf16 = jnp.float32, jnp.bfloat16
    copies = []
    for n, (k, got_ref) in enumerate(zip(places, got)):
        lanes = pl.ds(pl.multiple_of((me_ref[0] ^ k) * LANES, LANES), LANES)
        head = got_ref[pl.ds(3 * rows, HEAD), :].astype(f32)
        conv, mixed_grad, filt = [
            log_decode(got_ref[pl.ds(c * rows, rows), :], head[6 + c : 7 + c]) for c in range(3)
        ]

        def store(c):
            source = stage.at[n, c] if c < 4 else (stage_filter, stage_taps)[c - 4].at[n]
            target = outs[c].at[:, lanes] if c < 5 else outs[c].at[:, :, lanes]
            copies.append(pltpu.make_async_copy(source, target, sem.at[len(copies)]))
            copies[-1].start()

        stage_filter[n] = filt * (1.0 / math.sqrt(RADIX * rows))
        store(4)
        pairs = head[16:22] + head[22:28]
        for c, at in enumerate(TAPS_AT):
            stage_taps[n, c // 3, c % 3 : c % 3 + 1, :] = log_decode(head[at : at + 1], head[9:10])
        store(5)
        line = lax.broadcasted_iota(jnp.int32, (PAD, LANES), 0)
        filtered = []
        gain = []
        for i in range(3):
            gain.append([wide_ref[3 * i + j : 3 * i + j + 1, lanes] for j in range(3)])
            before, last = head[2 * i : 2 * i + 1], head[2 * i + 1 : 2 * i + 2]
            top = early_ref[i, 0:PAD, lanes] + jnp.where(
                line == 0,
                gain[i][1] * last + gain[i][2] * before,
                jnp.where(line == 1, gain[i][2] * last, 0.0),
            )
            filtered.append(jnp.concatenate([top, early_ref[i, PAD:, lanes]], axis=0))
        stage[n, 0] = (filtered[0] * conv).astype(bf16)
        store(0)
        inner = (
            conv * early_ref[3, :, lanes],
            mixed_grad * filtered[2],
            mixed_grad * filtered[1],
        )
        for i in range(3):
            grads[i, pl.ds(0, rows), :] = inner[i]
            grads[i, pl.ds(rows, 2), :] = pairs[2 * i : 2 * i + 2]
            stage[n, 1 + i] = (
                gain[i][0] * inner[i]
                + gain[i][1] * grads[i, pl.ds(1, rows), :]
                + gain[i][2] * grads[i, pl.ds(2, rows), :]
            ).astype(bf16)
            store(1 + i)
    return copies


def finish_kernel(places, begun, me_ref, *refs):
    count = len(places)
    got, (wide_ref, early_ref), refs = refs[:count], refs[count : count + 2], refs[count + 2 + begun :]
    for copy in finish_blocks(me_ref, places, got, wide_ref, early_ref, refs[:6], *refs[6:]):
        copy.wait()


def swap_blocks(places, blocks):
    devices = range(RADIX)
    return [
        lax.ppermute(block, "ctx", [(i, i ^ k) for i in devices]) if k else block
        for k, block in zip(places, blocks)
    ]


def held(arrays, space):
    return [pltpu.with_memory_space_constraint(jnp.asarray(one), space) for one in arrays]


def local_fast(query_in, key_in, value_in, long_filter, short_taps, out_grad):
    rows, channels = query_in.shape
    total = RADIX * rows
    f32, bf16 = jnp.float32, jnp.bfloat16
    shape = jax.ShapeDtypeStruct
    inputs = held((query_in, key_in, value_in, out_grad), pltpu.HBM)
    small = pltpu.CompilerParams(vmem_limit_bytes=12 * 1024 * 1024)
    me = lax.axis_index("ctx").astype(jnp.int32).reshape(1)
    sources = held((query_in, key_in, value_in, long_filter, out_grad), pltpu.HBM)

    def pack(places):
        return pl.pallas_call(
            partial(pack_kernel, places),
            out_shape=[pltpu.VMEM((FIELDS * rows, LANES), bf16)] * len(places),
            in_specs=[IN_SMEM] + whole_any(FIELDS),
            out_specs=whole_vmem(len(places)),
            scratch_shapes=[
                pltpu.VMEM((FIELDS, rows, channels), bf16),
                pltpu.SemaphoreType.DMA((FIELDS,)),
            ],
            compiler_params=small,
            name="pack",
        )(me, *sources)

    packed = pack(SENT)
    got = swap_blocks(SENT, packed)
    forward, inverse = class_tables(rows)
    count = 1 + len(CLASSES)
    ready = pl.pallas_call(
        prepare_kernel,
        out_shape=[
            pltpu.VMEM(forward.shape, bf16),
            pltpu.VMEM(inverse.shape, bf16),
            pltpu.VMEM((16, LANES), f32),
            pltpu.VMEM((16, channels), f32),
            pltpu.VMEM((4, rows, channels), f32),
        ],
        in_specs=[IN_SMEM] + whole_any(2) + whole_vmem(6),
        out_specs=whole_vmem(5),
        scratch_shapes=[pltpu.VMEM((PAD + rows, channels), f32), pltpu.SemaphoreType.DMA((4,))],
        compiler_params=small,
        name="prepare",
    )(me, *held((forward, inverse), pltpu.HBM), short_taps, *held(got[1:2], pltpu.VMEM), *inputs)
    ready = held(ready, pltpu.VMEM)
    done = pl.pallas_call(
        layer_kernel,
        out_shape=[pltpu.VMEM((3 * rows + HEAD, LANES), bf16)] * RADIX,
        in_specs=[IN_SMEM] + whole_vmem(3 + RADIX),
        out_specs=whole_vmem(RADIX),
        scratch_shapes=[pltpu.VMEM((total + PAD, LANES), f32)] * 7
        + [
            pltpu.VMEM((count, 2 * rows, columns * LANES), kind)
            for columns, kind in (
                (4, bf16), (2, bf16), (2, f32), (1, f32), (2, bf16), (4, bf16), (1, f32), (2, f32)
            )
        ]
        + [pltpu.VMEM((total + PAD, LANES), f32)] * 3
        + [
            pltpu.VMEM((3, RADIX, 8, LANES), f32),
            pltpu.VMEM((9, 8, LANES), f32),
            pltpu.VMEM((HEAD, LANES), f32),
        ],
        compiler_params=pltpu.CompilerParams(vmem_limit_bytes=20 * 1024 * 1024),
        name="layer",
    )(me, ready[2], *ready[:2], *held(got, pltpu.VMEM))
    back = held(swap_blocks(BACK, done), pltpu.VMEM)
    results = [shape((rows, channels), bf16)] * 4 + [
        shape((rows, channels), f32),
        shape((3, 3, channels), f32),
    ]

    begun = []
    for first, last in zip(FINISHED, FINISHED[1:]):
        count = last - first
        begun = pl.pallas_call(
            partial(finish_kernel, BACK[first:last], len(begun)),
            out_shape=results,
            in_specs=[IN_SMEM] + whole_vmem(count + 2) + whole_any(len(begun)),
            out_specs=whole_any(6),
            scratch_shapes=[
                pltpu.VMEM((3, rows + PAD, LANES), f32),
                pltpu.VMEM((count, 4, rows, LANES), bf16),
                pltpu.VMEM((count, rows, LANES), f32),
                pltpu.VMEM((count, 3, 3, LANES), f32),
                pltpu.SemaphoreType.DMA((6 * count,)),
            ],
            input_output_aliases={count + 3 + n: n for n in range(len(begun))},
            compiler_params=small,
            name="finish",
        )(me, *back[first:last], *ready[3:], *begun)
    return tuple(begun)


def local(query_in, key_in, value_in, long_filter, short_taps, out_grad):
    rows, channels = query_in.shape
    blocks = lax.axis_size("ctx")
    taps = short_taps.shape[:2]
    if blocks == RADIX and channels == blocks * LANES and rows == LANES and taps == (3, 3):
        return local_fast(query_in, key_in, value_in, long_filter, short_taps, out_grad)
    return local_general(query_in, key_in, value_in, long_filter, short_taps, out_grad)


def solution(mesh):
    placed = (
        P("ctx", "tp"),
        P("ctx", "tp"),
        P("ctx", "tp"),
        P("ctx", "tp"),
        P(None, None, "tp"),
        P("ctx", "tp"),
    )
    return jax.shard_map(
        local,
        mesh=mesh,
        in_specs=placed,
        out_specs=(
            P("ctx", "tp"),
            P("ctx", "tp"),
            P("ctx", "tp"),
            P("ctx", "tp"),
            P("ctx", "tp"),
            P(None, None, "tp"),
        ),
        check_vma=False,
    )
```

```python
from functools import lru_cache, partial, reduce
import math

import jax
import jax.numpy as jnp
import ml_dtypes
import numpy as np
from jax import lax
from jax.experimental import pallas as pl
from jax.experimental.pallas import tpu as pltpu
from jax.sharding import PartitionSpec as P

HIGHEST_PREC = lax.Precision.HIGHEST
TWO_PI = 2.0 * math.pi


def passed_along(block, axis, distance):
    devices = range(lax.axis_size(axis))
    route = [(i - distance, i) for i in devices if i - distance in devices]
    return lax.ppermute(block, axis, route)


def phase_pair(count_a, count_b, period, direction):
    product = (
        jnp.arange(count_a, dtype=jnp.int32)[:, None]
        * jnp.arange(count_b, dtype=jnp.int32)[None, :]
    )
    phase_angle = direction * TWO_PI / period * (product % period).astype(jnp.float32)
    return (jnp.cos(phase_angle), jnp.sin(phase_angle))


def rotate_pair(real_part, imag_part, cosine, sine_part):
    return (real_part * cosine - imag_part * sine_part, real_part * sine_part + imag_part * cosine)


def times_pair(first_pair, second_pair, conj_second):
    factor = -1.0 if conj_second else 1.0
    real_part = first_pair[0] * second_pair[0] - factor * first_pair[1] * second_pair[1]
    imag_part = first_pair[1] * second_pair[0] + factor * first_pair[0] * second_pair[1]
    return (real_part, imag_part)


def unpack_fields(spectrum, comp_axis, field_axis):
    collected = []
    for partner_rank in range(spectrum.shape[field_axis]):
        single = lax.index_in_dim(spectrum, partner_rank, field_axis, keepdims=True)
        collected.append(
            (
                lax.index_in_dim(single, 0, comp_axis, keepdims=True),
                lax.index_in_dim(single, 1, comp_axis, keepdims=True),
            )
        )
    return collected


def pack_fields(pairs, comp_axis, field_axis):
    return jnp.concatenate(
        [jnp.concatenate([real_part, imag_part], axis=comp_axis) for real_part, imag_part in pairs],
        axis=field_axis,
    )


def spread_forward(regroup, fields):
    row_count, field_count, channels = fields.shape
    part_count = lax.axis_size("ctx")
    block_rows = row_count // part_count
    length = 2 * part_count * row_count
    my_index = lax.axis_index("ctx")
    gathered = regroup(fields.reshape(part_count, 1, block_rows, field_count, channels))
    cosine, sine_part = phase_pair(2 * part_count, part_count, 2 * part_count, -1.0)
    first_table = jnp.stack([cosine, sine_part], axis=1)
    first_pass = jnp.einsum("kda,arfc->kdrfc", first_table, gathered, precision=HIGHEST_PREC)
    row_index = my_index * block_rows + jnp.arange(block_rows, dtype=jnp.int32)
    twist_index = jnp.arange(2 * part_count, dtype=jnp.int32)[:, None] * row_index[None, :] % length
    phase_angle = -TWO_PI / length * twist_index.astype(jnp.float32)
    cos_twist = jnp.cos(phase_angle)[:, :, None, None]
    sin_twist = jnp.sin(phase_angle)[:, :, None, None]
    real_part, imag_part = rotate_pair(first_pass[:, 0], first_pass[:, 1], cos_twist, sin_twist)
    turned = jnp.stack([real_part, imag_part], axis=1)
    arrived = regroup(turned.reshape(part_count, 1, 2, 2, block_rows, field_count, channels))
    cosine, sine_part = phase_pair(row_count, row_count, row_count, -1.0)
    second_table = jnp.stack(
        [jnp.stack([cosine, sine_part], axis=-1), jnp.stack([-sine_part, cosine], axis=-1)], axis=0
    )
    second_table = second_table.reshape(2, part_count, block_rows, row_count, 2)
    return jnp.einsum("pqsrfc,sprkd->qkdfc", arrived, second_table, precision=HIGHEST_PREC)


def spread_inverse(regroup, spectrum):
    pair_count, row_count, _, field_count, channels = spectrum.shape
    part_count = lax.axis_size("ctx")
    block_rows = row_count // part_count
    length = 2 * part_count * row_count
    my_index = lax.axis_index("ctx")
    cosine, sine_part = phase_pair(row_count, row_count, row_count, 1.0)
    second_table = jnp.stack(
        [jnp.stack([cosine, sine_part], axis=-1), jnp.stack([-sine_part, cosine], axis=-1)], axis=0
    )
    second_table = second_table.reshape(2, row_count, part_count, block_rows, 2)
    row_parts = jnp.einsum("qkdfc,dkprs->pqsrfc", spectrum, second_table, precision=HIGHEST_PREC)
    freq_index = my_index * pair_count + jnp.arange(pair_count, dtype=jnp.int32)
    twist_index = freq_index[:, None] * jnp.arange(row_count, dtype=jnp.int32)[None, :] % length
    phase_angle = TWO_PI / length * twist_index.astype(jnp.float32)
    cos_twist = (
        jnp.cos(phase_angle)
        .reshape(pair_count, part_count, block_rows)
        .transpose(1, 0, 2)[:, :, :, None, None]
    )
    sin_twist = (
        jnp.sin(phase_angle)
        .reshape(pair_count, part_count, block_rows)
        .transpose(1, 0, 2)[:, :, :, None, None]
    )
    real_part, imag_part = rotate_pair(row_parts[:, :, 0], row_parts[:, :, 1], cos_twist, sin_twist)
    turned = jnp.stack([real_part, imag_part], axis=2)
    arrived = regroup(
        turned.reshape(part_count, 1, pair_count, 2, block_rows, field_count, channels)
    )
    cosine, sine_part = phase_pair(2 * part_count, part_count, 2 * part_count, 1.0)
    first_table = (jnp.stack([cosine, -sine_part], axis=1) / length).reshape(
        part_count, pair_count, 2, part_count
    )
    values = jnp.einsum("pqsrfc,pqsa->arfc", arrived, first_table, precision=HIGHEST_PREC)
    returned = regroup(values.reshape(part_count, 1, block_rows, field_count, channels))
    return returned.reshape(row_count, field_count, channels)


def local_general(query_in, key_in, value_in, long_filter, short_taps, out_grad):
    row_count = query_in.shape[0]
    tap_count = short_taps.shape[1]
    margin = tap_count - 1
    part_count = lax.axis_size("ctx")

    def regroup(blocks):
        return lax.all_to_all(blocks, "ctx", split_axis=0, concat_axis=1, tiled=True)[0]

    to_freq = partial(spread_forward, regroup)
    from_freq = partial(spread_inverse, regroup)
    comp_axis = 2
    field_axis = 3
    inputs = jnp.stack([query_in, key_in, value_in])
    earlier = passed_along(inputs[:, row_count - margin :], "ctx", 1)
    extended = jnp.concatenate([earlier, inputs], axis=1).astype(jnp.float32)
    tap_gain = short_taps.astype(jnp.float32)
    filtered = tap_gain[:, 0, None, :] * extended[:, margin:]
    for offset in range(1, tap_count):
        filtered = (
            filtered
            + tap_gain[:, offset, None, :]
            * extended[:, margin - offset : margin - offset + row_count]
        )
    query_filt = filtered[0]
    key_filt = filtered[1]
    value_filt = filtered[2]
    mixed_in = key_filt * value_filt
    spectra = to_freq(jnp.stack([mixed_in, long_filter.astype(jnp.float32)], axis=1))
    mixed_spec, filter_spec = unpack_fields(spectra, comp_axis, field_axis)
    convolved = from_freq(
        pack_fields([times_pair(mixed_spec, filter_spec, False)], comp_axis, field_axis)
    )[:, 0]
    output = (query_filt * convolved).astype(jnp.bfloat16)
    grad_in = out_grad.astype(jnp.float32)
    gate_grad = grad_in * convolved
    conv_grad = grad_in * query_filt
    grad_spec = unpack_fields(to_freq(conv_grad[:, None, :]), comp_axis, field_axis)[0]
    returned = from_freq(
        pack_fields(
            [times_pair(grad_spec, filter_spec, True), times_pair(grad_spec, mixed_spec, True)],
            comp_axis,
            field_axis,
        )
    )
    grad_scale = 1.0 / math.sqrt(part_count * row_count)
    mixed_grad = returned[:, 0]
    filter_grad = returned[:, 1] * grad_scale
    grad_stack = jnp.stack([gate_grad, mixed_grad * value_filt, mixed_grad * key_filt])
    later_rows = passed_along(grad_stack[:, :margin], "ctx", -1)
    padded_grad = jnp.concatenate([grad_stack, later_rows], axis=1)
    input_grads = tap_gain[:, 0, None, :] * grad_stack
    for offset in range(1, tap_count):
        input_grads = (
            input_grads + tap_gain[:, offset, None, :] * padded_grad[:, offset : offset + row_count]
        )
    partial_taps = jnp.stack(
        [
            jnp.sum(grad_stack * extended[:, margin - offset : margin - offset + row_count], axis=1)
            for offset in range(tap_count)
        ],
        axis=1,
    )
    taps_grad = lax.psum(partial_taps, "ctx") * grad_scale
    return (
        output,
        input_grads[0].astype(jnp.bfloat16),
        input_grads[1].astype(jnp.bfloat16),
        input_grads[2].astype(jnp.bfloat16),
        filter_grad,
        taps_grad,
    )


RADIX = 8
FIELDS = 5
CLASSES = (4, 2, 6, 1, 5, 9, 13)
LANES = 128
PAD = 8
CHUNK = 16
SENT = (0, 6, 2, 4, 5, 3, 7, 1)
BACK = (0, 6, 5, 2, 4, 3, 7, 1)
FINISHED = (0, 4, 6, 8)
REACH = 124.0
TINY = 1e-30
HEAD = 32
TAPS_AT = (10, 11, 12, 13, 14, 15, 28, 29, 30)


def split_pair(values):
    high = values.astype(jnp.bfloat16)
    low = (values - high.astype(jnp.float32)).astype(jnp.bfloat16)
    return high, low


@lru_cache(maxsize=None)
def class_tables(rows):
    length = 2 * RADIX * rows
    back = np.arange(rows)

    def waves(residue, count):
        angle = 2.0 * np.pi * (np.outer(2 * RADIX * np.arange(count) + residue, back) % length) / length
        return np.cos(angle), np.sin(angle)

    half = rows // 2
    cos0, sin0 = waves(0, half)
    cos8, sin8 = waves(RADIX, half)
    none = np.zeros((half, rows))
    middle = (1.0 - 2.0 * (back % 2))[None, :]
    imag0 = np.concatenate([middle, -sin0[1:]])
    forward = [np.block([[cos0, none], [none, cos8], [imag0, none], [none, -sin8]])]
    weight = np.full((2 * rows, 1), 2.0)
    weight[0] = weight[rows] = 1.0
    inverse = [(weight * forward[0]).T]
    for residue in CLASSES:
        cosine, sine = waves(residue, rows)
        forward.append(np.block([[cosine, sine], [-sine, cosine]]))
        inverse.append(2.0 * forward[-1].T)
    tables = []
    for table in (np.stack(forward), np.stack(inverse) / length):
        high = table.astype(ml_dtypes.bfloat16)
        low = (table - high.astype(np.float64)).astype(ml_dtypes.bfloat16)
        tables.append(np.stack([high, low]))
    return tables


ROOT = math.sqrt(0.5)
COS1 = math.cos(math.pi / 8)
SIN1 = math.sin(math.pi / 8)


def forward_classes(x):
    u = [x[a] + x[a + 4] for a in range(4)]
    d = [x[a] - x[a + 4] for a in range(4)]
    even, odd = u[0] + u[2], u[1] + u[3]
    dif, tot = ROOT * (d[1] - d[3]), ROOT * (d[1] + d[3])
    found = [
        (even + odd, even - odd),
        (u[0] - u[2], u[3] - u[1]),
        (d[0] + dif, -d[2] - tot),
        (d[0] - dif, d[2] - tot),
    ]
    w0 = (x[0], -x[4])
    w1 = (COS1 * x[1] - SIN1 * x[5], -SIN1 * x[1] - COS1 * x[5])
    w2 = (ROOT * (x[2] - x[6]), -ROOT * (x[2] + x[6]))
    w3 = (SIN1 * x[3] - COS1 * x[7], -COS1 * x[3] - SIN1 * x[7])
    s02 = (w0[0] + w2[0], w0[1] + w2[1])
    d02 = (w0[0] - w2[0], w0[1] - w2[1])
    s13 = (w1[0] + w3[0], w1[1] + w3[1])
    d13 = (w1[0] - w3[0], w1[1] - w3[1])
    found.append((s02[0] + s13[0], s02[1] + s13[1]))
    found.append((d02[0] + d13[1], d02[1] - d13[0]))
    found.append((s02[0] - s13[0], s02[1] - s13[1]))
    found.append((d02[0] - d13[1], d02[1] + d13[0]))
    return found


def inverse_classes(z):
    (z0, z8), (r4, i4), (r2, i2), (r6, i6) = z[:4]
    up, down = z0 + z8, z0 - z8
    even = [up + r4, down - i4, up - r4, down + i4]
    gap, tot = ROOT * (r2 - r6), ROOT * (i2 + i6)
    turn = [r2 + r6, gap - tot, i6 - i2, -gap - tot]
    (r1, i1), (r5, i5), (r9, i9), (rd, id_) = z[4:]
    s = (r1 + r9, i1 + i9)
    d = (r1 - r9, i1 - i9)
    t = (r5 + rd, i5 + id_)
    e = (r5 - rd, i5 - id_)
    s0 = (s[0] + t[0], s[1] + t[1])
    s2 = (s[0] - t[0], s[1] - t[1])
    s1 = (d[0] - e[1], d[1] + e[0])
    s3 = (d[0] + e[1], d[1] - e[0])
    q = [
        s0,
        (COS1 * s1[0] - SIN1 * s1[1], SIN1 * s1[0] + COS1 * s1[1]),
        (ROOT * (s2[0] - s2[1]), ROOT * (s2[0] + s2[1])),
        (SIN1 * s3[0] - COS1 * s3[1], COS1 * s3[0] + SIN1 * s3[1]),
    ]
    return [even[a] + turn[a] + q[a][0] for a in range(4)] + [
        even[a] - turn[a] - q[a][1] for a in range(4)
    ]


def log_code(values, inverse_scale):
    code = jnp.exp2(jnp.abs(values) * (inverse_scale * (2.0 * REACH)) - REACH)
    return jnp.where(values < 0.0, -code, code).astype(jnp.bfloat16)


def code_scale(peak):
    return jnp.maximum(peak * (1.0 + 2.0**-7), TINY).astype(jnp.bfloat16).astype(jnp.float32)


def log_decode(code, scale):
    code = code.astype(jnp.float32)
    values = (jnp.log2(jnp.abs(code)) + REACH) * (scale * (0.5 / REACH))
    return jnp.where(code < 0.0, -values, values)


def table_dot(table_ref, f, both):
    half = both.shape[1] // 2
    found = jnp.dot(table_ref[0, f], both, preferred_element_type=jnp.float32)
    rest = jnp.dot(table_ref[1, f], both[:, :half], preferred_element_type=jnp.float32)
    return found[:, :half] + (found[:, half:] + rest)


def times_spec(first, second, conj_second, packed):
    (ar, ai), (br, bi) = first, second
    inner = ai * bi
    cross = ai * br - ar * bi if conj_second else ai * br + ar * bi
    if packed:
        line = lax.broadcasted_iota(jnp.int32, inner.shape, 0) == 0
        cross = jnp.where(line, inner, cross)
        inner = jnp.where(line, 0.0, inner)
    return (ar * br + inner if conj_second else ar * br - inner), cross


def spec_parts(spec, rows, column):
    lanes = slice(column * LANES, (column + 1) * LANES)
    return spec[:rows, lanes], spec[rows:, lanes]


def side_by_side(products):
    pairs = [split_pair(jnp.concatenate(pair, axis=0)) for pair in products]
    return jnp.concatenate([high for high, _ in pairs] + [low for _, low in pairs], axis=1)


def put_classes(ref, column, columns, rows, b0, values):
    for f, pair in enumerate(forward_classes(values)):
        for part, value in enumerate(pair):
            high, low = split_pair(value)
            at = pl.ds(part * rows + b0, CHUNK)
            ref[f, at, pl.ds(column * LANES, LANES)] = high
            ref[f, at, pl.ds((columns + column) * LANES, LANES)] = low


def take_classes(ref, column, rows, b0):
    lanes = pl.ds(column * LANES, LANES)
    found = []
    for f in range(ref.shape[0]):
        pair = ref[f, pl.ds(b0, CHUNK), lanes], ref[f, pl.ds(rows + b0, CHUNK), lanes]
        found.append(pair)
    return inverse_classes(found)


def short_filter(gain, ref, at):
    return (
        gain[0] * ref[pl.ds(at, CHUNK), :]
        + gain[1] * ref[pl.ds(at - 1, CHUNK), :]
        + gain[2] * ref[pl.ds(at - 2, CHUNK), :]
    )


def widen(me_ref, got, targets, rows):
    def body(step, carry):
        b0 = pl.multiple_of(step * CHUNK, CHUNK)
        for k, ref in zip(SENT, got):
            at = pl.multiple_of((me_ref[0] ^ k) * rows + b0, CHUNK)
            for field, (target, pad) in enumerate(targets):
                target[pl.ds(pad + at, CHUNK), :] = ref[pl.ds(field * rows + b0, CHUNK), :].astype(
                    jnp.float32
                )
        return carry

    lax.fori_loop(0, rows // CHUNK, body, 0, unroll=8)


def gains(taps_ref):
    return [[taps_ref[3 * i + j : 3 * i + j + 1, :] for j in range(3)] for i in range(3)]


def layer_kernel(me_ref, gain_ref, forward_ref, inverse_ref, *refs):
    got, outs = refs[:RADIX], refs[RADIX : 2 * RADIX]
    qp, kp, vp, hs, cot, ks, vs, xs, xs_grad, spec, spec_grad, ys_conv, ys, zs_conv, zs, conv, mgrad, fgrad, peak, sums, head = refs[2 * RADIX :]
    rows = got[0].shape[0] // FIELDS
    total = RADIX * rows
    f32 = jnp.float32
    gain = gains(gain_ref)
    for ref in (qp, kp, vp):
        ref[pl.ds(0, PAD), :] = jnp.zeros((PAD, LANES), f32)
    for ref in (cot, ks, vs, conv, mgrad):
        ref[pl.ds(total, PAD), :] = jnp.zeros((PAD, LANES), f32)
    widen(me_ref, got, ((qp, PAD), (kp, PAD), (vp, PAD), (hs, 0), (cot, 0)), rows)

    chunks = range(0, rows, CHUNK)
    classes = range(xs.shape[0])
    for b0 in chunks:
        mixed = []
        for a in range(RADIX):
            at = a * rows + b0
            key_filt = short_filter(gain[1], kp, PAD + at)
            value_filt = short_filter(gain[2], vp, PAD + at)
            ks[pl.ds(at, CHUNK), :] = key_filt
            vs[pl.ds(at, CHUNK), :] = value_filt
            mixed.append(key_filt * value_filt)
        put_classes(xs, 0, 2, rows, b0, mixed)
        filt = [hs[pl.ds(a * rows + b0, CHUNK), :] for a in range(RADIX)]
        put_classes(xs, 1, 2, rows, b0, filt)
    for f, b0 in zip(classes, chunks):
        spec[f] = table_dot(forward_ref, f, xs[f])
        conv_grad = []
        for a in range(RADIX):
            at = a * rows + b0
            conv_grad.append(short_filter(gain[0], qp, PAD + at) * cot[pl.ds(at, CHUNK), :])
        put_classes(xs_grad, 0, 1, rows, b0, conv_grad)
    for f in classes:
        spec_grad[f] = table_dot(forward_ref, f, xs_grad[f])
        mixed, filt = [spec_parts(spec[f], rows, c) for c in range(2)]
        ys_conv[f] = side_by_side([times_spec(mixed, filt, False, f == 0)])
    for f in classes:
        zs_conv[f] = table_dot(inverse_ref, f, ys_conv[f])
        mixed, filt = [spec_parts(spec[f], rows, c) for c in range(2)]
        grad = spec_parts(spec_grad[f], rows, 0)
        ys[f] = side_by_side([times_spec(grad, one, True, f == 0) for one in (filt, mixed)])

    def take(column, b0, ref, source, place):
        found = take_classes(source, place, rows, b0)
        for a, value in enumerate(found):
            ref[pl.ds(a * rows + b0, CHUNK), :] = value
            size = jnp.abs(value)
            top = jnp.maximum(size[:8], size[8:])
            peak[column, a] = jnp.maximum(peak[column, a], top) if b0 else top
        return found

    def add(i, b0, source, values, other):
        found = [None] * 3
        for a, value in enumerate(values):
            at = a * rows + b0
            now = value * other[pl.ds(at, CHUNK), :]
            for j in range(3):
                term = now * source[pl.ds(PAD + at - j, CHUNK), :]
                found[j] = found[j] + term if a else term
        for j in range(3):
            line = found[j][:8] + found[j][8:]
            sums[3 * i + j] = sums[3 * i + j] + line if b0 else line

    for f, b0 in zip(classes, chunks):
        zs[f] = table_dot(inverse_ref, f, ys[f])
        add(0, b0, qp, take(0, b0, conv, zs_conv, 0), cot)
    for b0 in chunks:
        found = take(1, b0, mgrad, zs, 0)
        add(1, b0, kp, found, vs)
        add(2, b0, vp, found, ks)
        take(2, b0, fgrad, zs, 1)
    grad_scale = 1.0 / math.sqrt(total)
    head[...] = jnp.zeros_like(head)
    taps = [jnp.sum(sums[n], axis=0, keepdims=True) * grad_scale for n in range(9)]
    scale = code_scale(reduce(jnp.maximum, [jnp.abs(line) for line in taps]))
    head[pl.ds(9, 1), :] = scale
    for at, line in zip(TAPS_AT, taps):
        head[pl.ds(at, 1), :] = log_code(line, 1.0 / scale).astype(f32)
    for k, out_ref in zip(BACK, outs):
        a = me_ref[0] ^ k
        first = pl.multiple_of(a * rows, rows)
        after = first + rows
        for i, ref in enumerate((qp, kp, vp)):
            head[pl.ds(2 * i, 2), :] = ref[pl.ds(first + PAD - 2, 2), :]
        for column, ref in enumerate((conv, mgrad, fgrad)):
            top = jnp.max(peak[column, a], axis=0, keepdims=True)
            scale = code_scale(top)
            head[pl.ds(6 + column, 1), :] = scale
            out_ref[pl.ds(column * rows, rows), :] = log_code(
                ref[pl.ds(first, rows), :], 1.0 / scale
            )
        for i, (ref, other) in enumerate(((conv, cot), (mgrad, vs), (mgrad, ks))):
            head[pl.ds(16 + 2 * i, 2), :] = ref[pl.ds(after, 2), :] * other[pl.ds(after, 2), :]
        head[pl.ds(22, 6), :] = split_pair(head[pl.ds(16, 6), :])[1].astype(f32)
        out_ref[pl.ds(3 * rows, HEAD), :] = head[...].astype(jnp.bfloat16)


def prepare_kernel(
    me_ref, forward_any, inverse_any, taps_any, _, query_ref, key_ref, value_ref, cot_ref,
    forward_ref, inverse_ref, gain_ref, wide_ref, early_ref, wide, sem,
):
    lane = pl.ds(pl.multiple_of(me_ref[0] * LANES, LANES), LANES)
    copies = [
        pltpu.make_async_copy(forward_any.at[n], forward_ref.at[n], sem.at[n]) for n in range(2)
    ] + [
        pltpu.make_async_copy(inverse_any.at[n], inverse_ref.at[n], sem.at[2 + n]) for n in range(2)
    ]
    for copy in copies:
        copy.start()
    taps = taps_any[...].astype(jnp.float32)
    for i in range(3):
        for j in range(3):
            at = 3 * i + j
            wide_ref[at : at + 1, :] = taps[i, j : j + 1, :]
            gain_ref[at : at + 1, :] = wide_ref[at : at + 1, lane]
    rows = cot_ref.shape[0]
    for i, ref in enumerate((query_ref, key_ref, value_ref)):
        wide[pl.ds(0, PAD), :] = jnp.zeros((PAD, wide.shape[1]), jnp.float32)
        wide[pl.ds(PAD, rows), :] = ref[...].astype(jnp.float32)
        early_ref[i] = (
            wide_ref[3 * i : 3 * i + 1, :] * wide[pl.ds(PAD, rows), :]
            + wide_ref[3 * i + 1 : 3 * i + 2, :] * wide[pl.ds(PAD - 1, rows), :]
            + wide_ref[3 * i + 2 : 3 * i + 3, :] * wide[pl.ds(PAD - 2, rows), :]
        )
    early_ref[3] = cot_ref[...].astype(jnp.float32)
    for copy in copies:
        copy.wait()


def whole_vmem(count):
    return [pl.BlockSpec(memory_space=pltpu.VMEM)] * count


def whole_any(count):
    return [pl.BlockSpec(memory_space=pl.ANY)] * count


IN_SMEM = pl.BlockSpec(memory_space=pltpu.SMEM)


def pack_kernel(places, me_ref, *refs):
    sources, outs, land, sem = refs[:FIELDS], refs[FIELDS:-2], refs[-2], refs[-1]
    rows = sources[0].shape[0]
    copies = [
        pltpu.make_async_copy(source, land.at[field], sem.at[field])
        for field, source in enumerate(sources)
    ]
    for copy in copies:
        copy.start()
    for field, copy in enumerate(copies):
        copy.wait()
        for k, out_ref in zip(places, outs):
            lane = pl.multiple_of((me_ref[0] ^ k) * LANES, LANES)
            out_ref[pl.ds(field * rows, rows), :] = land[field, :, pl.ds(lane, LANES)]


def finish_blocks(me_ref, places, got, wide_ref, early_ref, outs, grads, stage, stage_filter, stage_taps, sem):
    rows = early_ref.shape[1]
    f32, bf16 = jnp.float32, jnp.bfloat16
    copies = []
    for n, (k, got_ref) in enumerate(zip(places, got)):
        lanes = pl.ds(pl.multiple_of((me_ref[0] ^ k) * LANES, LANES), LANES)
        head = got_ref[pl.ds(3 * rows, HEAD), :].astype(f32)
        conv, mixed_grad, filt = [
            log_decode(got_ref[pl.ds(c * rows, rows), :], head[6 + c : 7 + c]) for c in range(3)
        ]

        def store(c):
            source = stage.at[n, c] if c < 4 else (stage_filter, stage_taps)[c - 4].at[n]
            target = outs[c].at[:, lanes] if c < 5 else outs[c].at[:, :, lanes]
            copies.append(pltpu.make_async_copy(source, target, sem.at[len(copies)]))
            copies[-1].start()

        stage_filter[n] = filt * (1.0 / math.sqrt(RADIX * rows))
        store(4)
        pairs = head[16:22] + head[22:28]
        for c, at in enumerate(TAPS_AT):
            stage_taps[n, c // 3, c % 3 : c % 3 + 1, :] = log_decode(head[at : at + 1], head[9:10])
        store(5)
        line = lax.broadcasted_iota(jnp.int32, (PAD, LANES), 0)
        filtered = []
        gain = []
        for i in range(3):
            gain.append([wide_ref[3 * i + j : 3 * i + j + 1, lanes] for j in range(3)])
            before, last = head[2 * i : 2 * i + 1], head[2 * i + 1 : 2 * i + 2]
            top = early_ref[i, 0:PAD, lanes] + jnp.where(
                line == 0,
                gain[i][1] * last + gain[i][2] * before,
                jnp.where(line == 1, gain[i][2] * last, 0.0),
            )
            filtered.append(jnp.concatenate([top, early_ref[i, PAD:, lanes]], axis=0))
        stage[n, 0] = (filtered[0] * conv).astype(bf16)
        store(0)
        inner = (
            conv * early_ref[3, :, lanes],
            mixed_grad * filtered[2],
            mixed_grad * filtered[1],
        )
        for i in range(3):
            grads[i, pl.ds(0, rows), :] = inner[i]
            grads[i, pl.ds(rows, 2), :] = pairs[2 * i : 2 * i + 2]
            stage[n, 1 + i] = (
                gain[i][0] * inner[i]
                + gain[i][1] * grads[i, pl.ds(1, rows), :]
                + gain[i][2] * grads[i, pl.ds(2, rows), :]
            ).astype(bf16)
            store(1 + i)
    return copies


def finish_kernel(places, begun, me_ref, *refs):
    count = len(places)
    got, (wide_ref, early_ref), refs = refs[:count], refs[count : count + 2], refs[count + 2 + begun :]
    for copy in finish_blocks(me_ref, places, got, wide_ref, early_ref, refs[:6], *refs[6:]):
        copy.wait()


def swap_blocks(places, blocks):
    devices = range(RADIX)
    return [
        lax.ppermute(block, "ctx", [(i, i ^ k) for i in devices]) if k else block
        for k, block in zip(places, blocks)
    ]


def held(arrays, space):
    return [pltpu.with_memory_space_constraint(jnp.asarray(one), space) for one in arrays]


def local_fast(query_in, key_in, value_in, long_filter, short_taps, out_grad):
    rows, channels = query_in.shape
    total = RADIX * rows
    f32, bf16 = jnp.float32, jnp.bfloat16
    shape = jax.ShapeDtypeStruct
    inputs = held((query_in, key_in, value_in, out_grad), pltpu.HBM)
    small = pltpu.CompilerParams(vmem_limit_bytes=12 * 1024 * 1024)
    me = lax.axis_index("ctx").astype(jnp.int32).reshape(1)
    sources = held((query_in, key_in, value_in, long_filter, out_grad), pltpu.HBM)

    def pack(places):
        return pl.pallas_call(
            partial(pack_kernel, places),
            out_shape=[pltpu.VMEM((FIELDS * rows, LANES), bf16)] * len(places),
            in_specs=[IN_SMEM] + whole_any(FIELDS),
            out_specs=whole_vmem(len(places)),
            scratch_shapes=[
                pltpu.VMEM((FIELDS, rows, channels), bf16),
                pltpu.SemaphoreType.DMA((FIELDS,)),
            ],
            compiler_params=small,
            name="pack",
        )(me, *sources)

    packed = pack(SENT)
    got = swap_blocks(SENT, packed)
    forward, inverse = class_tables(rows)
    count = 1 + len(CLASSES)
    ready = pl.pallas_call(
        prepare_kernel,
        out_shape=[
            pltpu.VMEM(forward.shape, bf16),
            pltpu.VMEM(inverse.shape, bf16),
            pltpu.VMEM((16, LANES), f32),
            pltpu.VMEM((16, channels), f32),
            pltpu.VMEM((4, rows, channels), f32),
        ],
        in_specs=[IN_SMEM] + whole_any(2) + whole_vmem(6),
        out_specs=whole_vmem(5),
        scratch_shapes=[pltpu.VMEM((PAD + rows, channels), f32), pltpu.SemaphoreType.DMA((4,))],
        compiler_params=small,
        name="prepare",
    )(me, *held((forward, inverse), pltpu.HBM), short_taps, *held(got[1:2], pltpu.VMEM), *inputs)
    ready = held(ready, pltpu.VMEM)
    done = pl.pallas_call(
        layer_kernel,
        out_shape=[pltpu.VMEM((3 * rows + HEAD, LANES), bf16)] * RADIX,
        in_specs=[IN_SMEM] + whole_vmem(3 + RADIX),
        out_specs=whole_vmem(RADIX),
        scratch_shapes=[pltpu.VMEM((total + PAD, LANES), f32)] * 7
        + [
            pltpu.VMEM((count, 2 * rows, columns * LANES), kind)
            for columns, kind in (
                (4, bf16), (2, bf16), (2, f32), (1, f32), (2, bf16), (4, bf16), (1, f32), (2, f32)
            )
        ]
        + [pltpu.VMEM((total + PAD, LANES), f32)] * 3
        + [
            pltpu.VMEM((3, RADIX, 8, LANES), f32),
            pltpu.VMEM((9, 8, LANES), f32),
            pltpu.VMEM((HEAD, LANES), f32),
        ],
        compiler_params=pltpu.CompilerParams(vmem_limit_bytes=20 * 1024 * 1024),
        name="layer",
    )(me, ready[2], *ready[:2], *held(got, pltpu.VMEM))
    back = held(swap_blocks(BACK, done), pltpu.VMEM)
    results = [shape((rows, channels), bf16)] * 4 + [
        shape((rows, channels), f32),
        shape((3, 3, channels), f32),
    ]

    begun = []
    for first, last in zip(FINISHED, FINISHED[1:]):
        count = last - first
        begun = pl.pallas_call(
            partial(finish_kernel, BACK[first:last], len(begun)),
            out_shape=results,
            in_specs=[IN_SMEM] + whole_vmem(count + 2) + whole_any(len(begun)),
            out_specs=whole_any(6),
            scratch_shapes=[
                pltpu.VMEM((3, rows + PAD, LANES), f32),
                pltpu.VMEM((count, 4, rows, LANES), bf16),
                pltpu.VMEM((count, rows, LANES), f32),
                pltpu.VMEM((count, 3, 3, LANES), f32),
                pltpu.SemaphoreType.DMA((6 * count,)),
            ],
            input_output_aliases={count + 3 + n: n for n in range(len(begun))},
            compiler_params=small,
            name="finish",
        )(me, *back[first:last], *ready[3:], *begun)
    return tuple(begun)


def local(query_in, key_in, value_in, long_filter, short_taps, out_grad):
    rows, channels = query_in.shape
    blocks = lax.axis_size("ctx")
    taps = short_taps.shape[:2]
    if blocks == RADIX and channels == blocks * LANES and rows == LANES and taps == (3, 3):
        return local_fast(query_in, key_in, value_in, long_filter, short_taps, out_grad)
    return local_general(query_in, key_in, value_in, long_filter, short_taps, out_grad)


def solution(mesh):
    placed = (
        P("ctx", "tp"),
        P("ctx", "tp"),
        P("ctx", "tp"),
        P("ctx", "tp"),
        P(None, None, "tp"),
        P("ctx", "tp"),
    )
    return jax.shard_map(
        local,
        mesh=mesh,
        in_specs=placed,
        out_specs=(
            P("ctx", "tp"),
            P("ctx", "tp"),
            P("ctx", "tp"),
            P("ctx", "tp"),
            P("ctx", "tp"),
            P(None, None, "tp"),
        ),
        check_vma=False,
    )
```
